256 devices in a mesh: dp: 32 (over x, y, core), ctx: 8 (over z).
Axes of the slice: x: 4, y: 4, z: 8, core: 2. Of those that a mesh axis runs over, the one named last changes fastest.
Arguments:
- embedded: bfloat16 [8, 6144, 1024], P('ctx', 'dp'), may hold values from -30 to 30
- upstream: bfloat16 [8, 6144, 1024], P('ctx', 'dp'), may hold values from -6 to 6
- w_uvqk: bfloat16 [1024, 2048], replicated, may hold values from -0.1875 to 0.1875
- w_out: bfloat16 [512, 1024], replicated, may hold values from -0.25 to 0.25
- lengths: int32 [64], replicated, may hold values from 1 to 31, as said below
Outputs:
- layer_out: bfloat16 [8, 6144, 1024], P('ctx', 'dp')
- embedded_gradient: bfloat16 [8, 6144, 1024], P('ctx', 'dp')
- grad_w_uvqk: float32 [1024, 2048], P('ctx', 'dp')
- grad_w_out: float32 [512, 1024], P('ctx', 'dp')
The draws below stay inside these ranges and needn't reach their ends.
Inputs may be any that keep to these rules, and one draw needn't show every extreme that they name: The 2 sequences of one owner hold at most 32 blocks together; in every draw some owner holds exactly 32; the lengths sum to 512.
All inputs are finite; a program needn't handle non-finite values.
Results may differ from the reference program's by a relative error of at most 0.025.
Values may be sent and summed in bfloat16 or wider, within the bound.
A program may use at most 128 MiB of HBM per device.

```python
import math
import jax
import jax.numpy as jnp
from jax import lax

D = 1024
HEADS = 8
HEAD_DIM = 64
BR = 12
BLK_DEV = 16
MAXB = 32
SEQ_DP = 2
HD = 512
NSEQ = 64
NBLK = 512
ROWS = 192
TOKENS = 49152
N_DP = 32
N_CTX = 8


def draw_lengths(key, part):
    key = jax.random.fold_in(key, 3)
    key_forced, key_pool = jax.random.split(key, 2)
    forced_owner = jax.random.randint(key_forced, (), 0, N_DP).astype(jnp.int32)
    spare = MAXB - SEQ_DP
    chosen = NBLK - MAXB - (N_DP - 1) * SEQ_DP
    ranked = jax.random.permutation(key_pool, (N_DP - 1) * spare).astype(jnp.int32).reshape(N_DP - 1, spare)
    picked = (ranked < chosen).astype(jnp.int32)
    number = jnp.arange(NSEQ, dtype=jnp.int32)
    owner_ids = number // SEQ_DP
    within = number % SEQ_DP
    owner_rank = jnp.clip(owner_ids - (owner_ids > forced_owner).astype(jnp.int32), 0, N_DP - 2)
    slot = jnp.arange(spare, dtype=jnp.int32)
    mine = (jnp.mod(slot[None, :], SEQ_DP) == within[:, None]).astype(jnp.int32)
    extra = jnp.sum(picked[owner_rank] * mine, 1)
    forced_length = jnp.where(within == 0, MAXB - SEQ_DP + 1, 1)
    return jnp.where(owner_ids == forced_owner, forced_length, 1 + extra).astype(jnp.int32)


def draw_embedded(key, part):
    key = jax.random.fold_in(key, 7)
    key_base, key_column, key_row = jax.random.split(key, 3)
    shape = (N_CTX, N_DP * ROWS, D)
    column = jnp.exp(jax.random.uniform(key_column, (D,), minval=math.log(0.3), maxval=math.log(3.0)))
    base = jnp.clip(jax.random.normal(key_base, shape), -5.0, 5.0)
    row_scale = jnp.exp(jax.random.uniform(key_row, (N_CTX, N_DP * ROWS, 1), minval=math.log(0.5), maxval=math.log(2.0)))
    return (base * column * row_scale).astype(jnp.bfloat16)


def block_levels(stream_key, dims, cuts, smallest, high):
    def one(dim, parts):
        steps = jax.random.uniform(jax.random.fold_in(jax.random.fold_in(stream_key, 6), dim), (parts,), jnp.float32, smallest / len(cuts), high / len(cuts))
        return jnp.repeat(jnp.exp(steps), dims[dim] // parts).reshape((-1,) + (1,) * (len(dims) - dim - 1))

    level = one(*cuts[0])
    for cut in cuts[1:]:
        level = level * one(*cut)
    return level


def gaussian(stream_key, extent, deviation, reach, cuts=(), kind=jnp.bfloat16):
    level = block_levels(stream_key, extent, cuts, -0.22, 0.18) if cuts else 1.0
    entries = jax.random.normal(stream_key, extent, jnp.float32) * deviation * level
    return jnp.minimum(jnp.maximum(entries, -reach), reach).astype(kind)


def setup_inputs(seed: int = 0) -> dict:
    keys = jax.random.split(jax.random.key(seed), 6)
    return {
        "embedded": draw_embedded(jax.random.fold_in(keys[5], 71), 0),
        "upstream": gaussian(keys[1], (N_CTX, N_DP * ROWS, D), 1.0, 6.0, ((0, 8), (1, 32))),
        "w_uvqk": gaussian(keys[2], (D, 4 * HD), D ** -0.5, 0.1875),
        "w_out": gaussian(keys[3], (HD, D), HD ** -0.5, 0.25),
        "lengths": draw_lengths(jax.random.fold_in(keys[5], 71), 0),
    }


EPS = 1e-06

def layer_normalize(tensor):
    centre = lax.optimization_barrier(jnp.mean(tensor, -1, keepdims=True))
    centred = tensor - centre
    inverse_deviation = lax.rsqrt(lax.optimization_barrier(jnp.mean(centred * centred, -1, keepdims=True)) + EPS)
    return (centred * inverse_deviation, inverse_deviation)

def layer_norm_backward(incoming, normal, inverse_deviation):
    first_mean = lax.optimization_barrier(jnp.mean(incoming, -1, keepdims=True))
    second_mean = lax.optimization_barrier(jnp.mean(incoming * normal, -1, keepdims=True))
    return (incoming - first_mean - normal * second_mean) * inverse_deviation

def silu_grad(argument):
    sigmoid = jax.nn.sigmoid(argument)
    return sigmoid * (1.0 + argument * (1.0 - sigmoid))

def to_stream(tensor):
    feature = tensor.shape[-1]
    moved = tensor.reshape(N_CTX, N_DP, BLK_DEV, BR, feature).transpose(0, 2, 1, 3, 4)
    return moved.reshape(N_CTX * NBLK * BR, feature)

def from_stream(tensor):
    feature = tensor.shape[-1]
    moved = tensor.reshape(N_CTX, BLK_DEV, N_DP, BR, feature).transpose(0, 2, 1, 3, 4)
    return moved.reshape(N_CTX, N_DP * ROWS, feature)

def sequence_rows(start, length):
    offsets = jnp.arange(MAXB * BR, dtype=jnp.int32)[None, :]
    context = jnp.arange(N_CTX, dtype=jnp.int32)[:, None]
    limit = length * BR
    inside = jnp.broadcast_to(offsets < limit, (N_CTX, MAXB * BR))
    row_index = context * (NBLK * BR) + start * BR + jnp.minimum(offsets, limit - 1)
    position = context * limit + offsets
    return (row_index.reshape(-1), inside.reshape(-1), position.reshape(-1))

def split_heads(tensor):
    return tensor.reshape(tensor.shape[0], HEADS, HEAD_DIM).astype(jnp.float32)

def causal_scores(queries, key_rows, inside, position):
    allowed = inside[:, None] & inside[None, :] & (position[None, :] <= position[:, None])
    scores = jnp.einsum('ihd,jhd->hij', split_heads(queries), split_heads(key_rows)) * HEAD_DIM ** (-0.5)
    return (scores, allowed)

def reference(embedded, upstream, w_uvqk, w_out, lengths):
    hidden_width = HEADS * HEAD_DIM
    score_scale = HEAD_DIM ** (-0.5)
    input_rows = to_stream(embedded).astype(jnp.float32)
    upstream_rows = to_stream(upstream)
    centered_scaled, inverse_deviation = layer_normalize(input_rows)
    normalized_rows = centered_scaled.astype(jnp.bfloat16)
    pre = jnp.dot(normalized_rows, w_uvqk, preferred_element_type=jnp.float32)
    proj = lax.optimization_barrier(jax.nn.silu(pre).astype(jnp.bfloat16))
    gate_u = proj[:, :hidden_width]
    value_all = proj[:, hidden_width:2 * hidden_width]
    query_all = proj[:, 2 * hidden_width:3 * hidden_width]
    key_all = proj[:, 3 * hidden_width:]
    seq_start = (jnp.cumsum(lengths) - lengths).astype(jnp.int32)
    row_index, inside, position = jax.vmap(sequence_rows)(seq_start, lengths.astype(jnp.int32))
    total_rows = N_CTX * NBLK * BR
    flat_index = row_index.reshape(-1)
    flat_inside = inside.reshape(-1)

    def forward_one(number):
        here = row_index[number]
        scores, allowed = causal_scores(query_all[here], key_all[here], inside[number], position[number])
        weights = lax.optimization_barrier(jnp.where(allowed[None], jax.nn.silu(scores), 0.0).astype(jnp.bfloat16))
        result = jnp.einsum('hij,jhd->ihd', weights.astype(jnp.float32), split_heads(value_all[here]))
        return result.reshape(-1, hidden_width)
    att_seq = lax.map(forward_one, jnp.arange(NSEQ, dtype=jnp.int32))
    att = jnp.zeros((total_rows, hidden_width), jnp.float32).at[flat_index].add(jnp.where(flat_inside[:, None], att_seq.reshape(-1, hidden_width), 0.0))
    att_norm, att_inverse = layer_normalize(att)
    gated = lax.optimization_barrier((att_norm * gate_u.astype(jnp.float32)).astype(jnp.bfloat16))
    out_rows = (input_rows + jnp.dot(gated, w_out, preferred_element_type=jnp.float32)).astype(jnp.bfloat16)
    back_gated = jnp.dot(upstream_rows, w_out.T, preferred_element_type=jnp.float32)
    grad_u = back_gated * att_norm
    grad_att = lax.optimization_barrier(layer_norm_backward(back_gated * gate_u.astype(jnp.float32), att_norm, att_inverse).astype(jnp.bfloat16))

    def backward_one(number):
        here = row_index[number]
        scores, allowed = causal_scores(query_all[here], key_all[here], inside[number], position[number])
        weights = lax.optimization_barrier(jnp.where(allowed[None], jax.nn.silu(scores), 0.0).astype(jnp.bfloat16))
        grad_heads = split_heads(grad_att[here])
        grad_a = jnp.einsum('ihd,jhd->hij', grad_heads, split_heads(value_all[here]))
        grad_s = lax.optimization_barrier(jnp.where(allowed[None], grad_a * silu_grad(scores), 0.0).astype(jnp.bfloat16)).astype(jnp.float32)
        grad_q = jnp.einsum('hij,jhd->ihd', grad_s, split_heads(key_all[here])) * score_scale
        grad_k = jnp.einsum('hij,ihd->jhd', grad_s, split_heads(query_all[here])) * score_scale
        grad_v = jnp.einsum('hij,ihd->jhd', weights.astype(jnp.float32), grad_heads)
        return jnp.concatenate([grad_v.reshape(-1, hidden_width), grad_q.reshape(-1, hidden_width), grad_k.reshape(-1, hidden_width)], 1)
    back_seq = lax.map(backward_one, jnp.arange(NSEQ, dtype=jnp.int32))
    grad_vqk = jnp.zeros((total_rows, 3 * hidden_width), jnp.float32).at[flat_index].add(jnp.where(flat_inside[:, None], back_seq.reshape(-1, 3 * hidden_width), 0.0))
    grad_pre = (jnp.concatenate([grad_u, grad_vqk], 1) * silu_grad(pre)).astype(jnp.bfloat16)
    token_scale = TOKENS ** (-0.5)
    grad_w_uvqk = jnp.dot(normalized_rows.T, grad_pre, preferred_element_type=jnp.float32) * token_scale
    grad_w_out = jnp.dot(gated.T, upstream_rows, preferred_element_type=jnp.float32) * token_scale
    normalized_backward = jnp.dot(grad_pre, w_uvqk.T, preferred_element_type=jnp.float32)
    embedded_gradient = (upstream_rows.astype(jnp.float32) + layer_norm_backward(normalized_backward, centered_scaled, inverse_deviation)).astype(jnp.bfloat16)
    return (from_stream(out_rows), from_stream(embedded_gradient), grad_w_uvqk, grad_w_out)
```

```python
import functools

import jax
import jax.numpy as jnp
import numpy as np
from jax import lax
from jax.experimental import pallas as pl
from jax.experimental.pallas import tpu as pltpu
from jax.sharding import PartitionSpec as P

HEAD_DIM = 64
BR = 12
SEQ_DP = 2
GROUP = 4
LANES = 128
EPS = 1e-06
BIG = 1e30
MESH = pl.DeviceIdType.MESH
BF = jnp.bfloat16
F32 = jnp.float32
VMEM = pl.BlockSpec(memory_space=pltpu.VMEM)
SMEM = pl.BlockSpec(memory_space=pltpu.SMEM)
LIMIT = 48 * 1024 * 1024


class Cfg:
    def __init__(self, n_dp, n_ctx, rows, width):
        self.n_dp = n_dp
        self.n_ctx = n_ctx
        self.rows = rows
        self.width = width
        self.blocks = rows // BR
        self.heads = n_ctx
        self.hd = self.heads * HEAD_DIM
        self.half = n_ctx // 2
        self.chunk_vk = n_ctx * BR
        self.chunk_q = n_ctx * BR // 2
        self.span = n_dp * BR
        self.total = n_ctx * self.span
        self.tile = min(512, self.total // 3)
        self.tab_owner = n_dp
        self.tab_own = n_dp + self.blocks + 1


def permutation(contexts):
    size = contexts * GROUP * BR
    matrix = np.zeros((size, size), np.float32)
    for block in range(GROUP):
        for context in range(contexts):
            for row in range(BR):
                matrix[
                    (block * contexts + context) * BR + row, (context * GROUP + block) * BR + row
                ] = 1.0
    return matrix


def lane(shape):
    return lax.broadcasted_iota(jnp.int32, shape, len(shape) - 1)


def swap(tensor):
    return pltpu.roll(tensor, HEAD_DIM, 1)


def join(left, right):
    return jnp.where(lane(left.shape) < HEAD_DIM, left, right)


def mm(left, right):
    return jnp.dot(left, right, preferred_element_type=F32)


def mm_nt(left, right):
    return lax.dot_general(left, right, (((1,), (1,)), ((), ())), preferred_element_type=F32)


def layer_normalize(tensor):
    centre = jnp.mean(tensor, -1, keepdims=True)
    centred = tensor - centre
    inverse = lax.rsqrt(jnp.mean(centred * centred, -1, keepdims=True) + EPS)
    return centred * inverse, inverse


def layer_norm_backward(incoming, normal, inverse):
    first = jnp.mean(incoming, -1, keepdims=True)
    second = jnp.mean(incoming * normal, -1, keepdims=True)
    return (incoming - first - normal * second) * inverse


def silu(argument):
    return argument * jax.nn.sigmoid(argument)


def silu_grad(argument):
    sigmoid = jax.nn.sigmoid(argument)
    return sigmoid * (1.0 + argument * (1.0 - sigmoid))


def pre_kernel(cfg, dp_ref, lengths, x, w, tab, pre, zmsg):
    me = dp_ref[0]
    n = cfg.n_dp
    wrap = n * cfg.blocks * n

    def owner(o, start):
        first = lengths[SEQ_DP * o]
        total = first + lengths[SEQ_DP * o + 1]
        block = start + lax.rem(me - start + wrap, n)
        index = (block - me) // n
        tab[o] = jnp.clip(index, 0, cfg.blocks - 1)
        held = block < start + total
        tab[cfg.tab_owner + jnp.where(held, index, cfg.blocks)] = o

        @pl.when(o == me)
        def _():
            tab[cfg.tab_own] = lax.rem(start, n)
            tab[cfg.tab_own + 1] = first * BR
            tab[cfg.tab_own + 2] = total * BR

        return start + total

    lax.fori_loop(0, n, owner, jnp.int32(0))
    normal, _ = layer_normalize(x[0].astype(F32))
    normed = normal.astype(BF)
    hd = cfg.hd
    mid = cfg.rows // 2
    step = min(256, hd)
    for base in range(0, hd, step):
        parts = []
        for section in range(4):
            at = section * hd + base
            value = mm(normed, w[:, at : at + step])
            pre[:, at : at + step] = value
            parts.append(silu(value))
        for tile in range(step // LANES):
            cut = slice(tile * LANES, (tile + 1) * LANES)
            v, q, k = parts[1][:, cut], parts[2][:, cut], parts[3][:, cut]
            head = (base + tile * LANES) // HEAD_DIM
            zmsg[head, : cfg.rows] = join(v, swap(k)).astype(BF)
            zmsg[head + 1, : cfg.rows] = join(swap(v), k).astype(BF)
            zmsg[head, cfg.rows :] = join(q[:mid], swap(q[mid:])).astype(BF)
            zmsg[head + 1, cfg.rows :] = join(swap(q[:mid]), q[mid:]).astype(BF)


def pre_work(cfg, dp_index, lengths, x, w):
    return pl.pallas_call(
        functools.partial(pre_kernel, cfg),
        name="pre",
        out_shape=(
            jax.ShapeDtypeStruct((cfg.tab_own + 3,), jnp.int32),
            jax.ShapeDtypeStruct((cfg.rows, 4 * cfg.hd), F32),
            jax.ShapeDtypeStruct((cfg.heads, cfg.rows * 3 // 2, LANES), BF),
        ),
        in_specs=[SMEM, SMEM, VMEM, VMEM],
        out_specs=(SMEM, VMEM, VMEM),
        compiler_params=pltpu.CompilerParams(vmem_limit_bytes=LIMIT),
    )(dp_index, lengths, x, w)


def mid_kernel(cfg, zatt, pre, x, up, w_out, out, zmsg, gpu, t_out):
    hd = cfg.hd
    mid = cfg.rows // 2
    tops, bottoms = [], []
    for head in range(0, cfg.heads, 2):
        a, b = zatt[head].astype(F32), zatt[head + 1].astype(F32)
        tops.append(join(a, swap(b)))
        bottoms.append(join(swap(a), b))
    att = jnp.concatenate(
        [jnp.concatenate(tops, axis=1), jnp.concatenate(bottoms, axis=1)], axis=0
    )
    att_norm, att_inverse = layer_normalize(att)
    pre_u = pre[...]
    gate = silu(pre_u).astype(BF).astype(F32)
    gated = (att_norm * gate).astype(BF)
    out[0] = (x[0].astype(F32) + mm(gated, w_out[...])).astype(BF)
    upstream = up[0]
    back = mm_nt(upstream, w_out[...])
    gpu[...] = (back * att_norm * silu_grad(pre_u)).astype(BF)
    grad_att = layer_norm_backward(back * gate, att_norm, att_inverse)
    for tile in range(hd // LANES):
        g = grad_att[:, tile * LANES : (tile + 1) * LANES]
        zmsg[2 * tile] = join(g[:mid], swap(g[mid:])).astype(BF)
        zmsg[2 * tile + 1] = join(swap(g[:mid]), g[mid:]).astype(BF)
    t_out[...] = lax.dot_general(
        gated, upstream, (((0,), (0,)), ((), ())), preferred_element_type=F32
    ).astype(BF)


def mid_work(cfg, zatt, pre, x, up, w_out):
    return pl.pallas_call(
        functools.partial(mid_kernel, cfg),
        name="mid",
        grid=(1,),
        out_shape=(
            jax.ShapeDtypeStruct(x.shape, BF),
            jax.ShapeDtypeStruct((cfg.heads, cfg.rows // 2, LANES), BF),
            jax.ShapeDtypeStruct((cfg.rows, cfg.hd), BF),
            jax.ShapeDtypeStruct((cfg.hd, cfg.width), BF),
        ),
        in_specs=[
            VMEM,
            pl.BlockSpec((cfg.rows, cfg.hd), lambda i: (0, 0)),
            VMEM,
            VMEM,
            VMEM,
        ],
        out_specs=(VMEM, VMEM, VMEM, VMEM),
        compiler_params=pltpu.CompilerParams(vmem_limit_bytes=LIMIT),
    )(zatt, pre, x, up, w_out)


def post_kernel(cfg, zgrad, gpu, pre, x, up, w, gradient, term, gp, normal_t):
    hd = cfg.hd
    rows = cfg.rows
    mid = rows // 2
    gp[:, :hd] = gpu[...]
    for head in range(0, cfg.heads, 2):
        a, b = zgrad[head].astype(F32), zgrad[head + 1].astype(F32)
        av, bv = a[:rows], b[:rows]
        aq, bq = a[rows:], b[rows:]
        grad_v = join(av, swap(bv))
        grad_k = join(swap(av), bv)
        grad_q = jnp.concatenate([join(aq, swap(bq)), join(swap(aq), bq)], axis=0)
        for section, value in ((1, grad_v), (2, grad_q), (3, grad_k)):
            at = section * hd + head * HEAD_DIM
            cut = slice(at, at + LANES)
            gp[:, cut] = (value * silu_grad(pre[:, cut])).astype(BF)
    normal, inverse = layer_normalize(x[0].astype(F32))
    back = mm_nt(gp[...], w[...])
    gradient[0] = (up[0].astype(F32) + layer_norm_backward(back, normal, inverse)).astype(BF)
    normal_t[...] = normal.T.astype(BF)
    step = min(256, hd)
    for base in range(0, 4 * hd, step):
        term[:, base : base + step] = mm(normal_t[...], gp[:, base : base + step]).astype(BF)


def post_work(cfg, zgrad, gpu, pre, x, up, w):
    return pl.pallas_call(
        functools.partial(post_kernel, cfg),
        name="post",
        out_shape=(
            jax.ShapeDtypeStruct(x.shape, BF),
            jax.ShapeDtypeStruct((cfg.width, 4 * cfg.hd), BF),
        ),
        in_specs=[VMEM] * 6,
        out_specs=(VMEM, VMEM),
        scratch_shapes=[
            pltpu.VMEM((cfg.rows, 4 * cfg.hd), BF),
            pltpu.VMEM((cfg.width, cfg.rows), BF),
        ],
        compiler_params=pltpu.CompilerParams(vmem_limit_bytes=LIMIT),
    )(zgrad, gpu, pre, x, up, w)


def greet(cfg, me, ctx):
    barrier = pltpu.get_barrier_semaphore()

    def along_dp(k, carry):
        pl.semaphore_signal(
            barrier, inc=1, device_id={"dp": lax.rem(me + k, cfg.n_dp)}, device_id_type=MESH
        )
        return carry

    def along_ctx(k, carry):
        pl.semaphore_signal(
            barrier, inc=1, device_id={"ctx": lax.rem(ctx + k, cfg.n_ctx)}, device_id_type=MESH
        )
        return carry

    lax.fori_loop(1, cfg.n_dp, along_dp, 0)
    lax.fori_loop(1, cfg.n_ctx, along_ctx, 0)
    pl.semaphore_wait(barrier, cfg.n_dp + cfg.n_ctx - 2)


def exchange(axis, count, mine, part, rows, source, target, send_sem, recv_sem, land=None):
    land = rows[0] if land is None else land

    def copy(other):
        return pltpu.make_async_remote_copy(
            src_ref=source.at[other, pl.ds(rows[0], rows[1])],
            dst_ref=target.at[mine, pl.ds(land, rows[1])],
            send_sem=send_sem.at[part, other],
            recv_sem=recv_sem.at[part, mine],
            device_id={axis: other},
            device_id_type=MESH,
        )

    def arrival(other):
        return pltpu.make_async_remote_copy(
            src_ref=source.at[other, pl.ds(rows[0], rows[1])],
            dst_ref=target.at[other, pl.ds(land, rows[1])],
            send_sem=send_sem.at[part, other],
            recv_sem=recv_sem.at[part, other],
            device_id={axis: other},
            device_id_type=MESH,
        )

    def start(k, carry):
        copy(lax.rem(mine + k, count)).start()
        return carry

    def wait_recv(k, carry):
        arrival(lax.rem(mine + k, count)).wait_recv()
        return carry

    def wait_send(k, carry):
        copy(lax.rem(mine + k, count)).wait_send()
        return carry

    return (
        lambda: lax.fori_loop(1, count, start, 0),
        lambda: lax.fori_loop(1, count, wait_recv, 0),
        lambda: lax.fori_loop(1, count, wait_send, 0),
        copy,
    )


def scatter_kernel(cfg, has_vk, tab, zmsg, perm_vk, perm_q, recv, zrecv, chunks, sendbuf, *sems):
    zs, zr, xs, xr = sems
    me, ctx = lax.axis_index("dp"), lax.axis_index("ctx")
    greet(cfg, me, ctx)
    rows, n, c = cfg.rows, cfg.n_dp, cfg.n_ctx
    zq = rows if has_vk else 0
    cq = cfg.chunk_vk if has_vk else 0
    parts = ([(0, rows)] if has_vk else []) + [(zq, rows // 2)]
    cparts = ([(0, cfg.chunk_vk)] if has_vk else []) + [(cq, cfg.chunk_q)]
    zmoves = [exchange("ctx", c, ctx, i, p, zmsg, zrecv, zs, zr) for i, p in enumerate(parts)]
    xmoves = [exchange("dp", n, me, i, p, sendbuf, recv, xs, xr) for i, p in enumerate(cparts)]
    for move in zmoves:
        move[0]()
    zrecv[ctx] = zmsg[ctx]
    width = GROUP * BR

    def forward(i):
        at, size = cparts[i]
        recv[me, at : at + size] = chunks[tab[me], at : at + size]

        def one(k, carry):
            other = lax.rem(me + k, n)
            sendbuf[other, at : at + size] = chunks[tab[other], at : at + size]
            xmoves[i][3](other).start()
            return carry

        lax.fori_loop(1, n, one, 0)

    if has_vk:
        zmoves[0][1]()
        for g in range(cfg.blocks // GROUP):
            x = jnp.concatenate([zrecv[i, width * g : width * (g + 1)] for i in range(c)], axis=0)
            y = mm(perm_vk[...], x).astype(BF)
            for b in range(GROUP):
                chunks[GROUP * g + b, : cfg.chunk_vk] = y[
                    b * cfg.chunk_vk : (b + 1) * cfg.chunk_vk
                ]
        forward(0)
    zmoves[-1][1]()
    half_blocks = cfg.blocks // 2
    for g in range(half_blocks // GROUP):
        at = zq + width * g
        xl = jnp.concatenate([zrecv[i, at : at + width] for i in range(cfg.half)], axis=0)
        xr_ = jnp.concatenate([zrecv[i, at : at + width] for i in range(cfg.half, c)], axis=0)
        yl, yr = mm(perm_q[...], xl), mm(perm_q[...], xr_)
        left = join(yl, swap(yr)).astype(BF)
        right = join(swap(yl), yr).astype(BF)
        for b in range(GROUP):
            cut = slice(b * cfg.chunk_q, (b + 1) * cfg.chunk_q)
            chunks[GROUP * g + b, cq:] = left[cut]
            chunks[half_blocks + GROUP * g + b, cq:] = right[cut]
    forward(len(parts) - 1)
    for move in zmoves:
        move[2]()
    for move in xmoves:
        move[1]()
    for move in xmoves:
        move[2]()


def scatter(cfg, has_vk, collective, tab, zmsg, perm_vk, perm_q):
    size = (cfg.chunk_vk if has_vk else 0) + cfg.chunk_q
    parts = 2 if has_vk else 1
    return pl.pallas_call(
        functools.partial(scatter_kernel, cfg, has_vk),
        name="scatter",
        out_shape=jax.ShapeDtypeStruct((cfg.n_dp, size, LANES), BF),
        in_specs=[SMEM, VMEM, VMEM, VMEM],
        out_specs=VMEM,
        scratch_shapes=[
            pltpu.VMEM(zmsg.shape, BF),
            pltpu.VMEM((cfg.blocks, size, LANES), BF),
            pltpu.VMEM((cfg.n_dp, size, LANES), BF),
            pltpu.SemaphoreType.DMA((parts, cfg.n_ctx)),
            pltpu.SemaphoreType.DMA((parts, cfg.n_ctx)),
            pltpu.SemaphoreType.DMA((parts, cfg.n_dp)),
            pltpu.SemaphoreType.DMA((parts, cfg.n_dp)),
        ],
        compiler_params=pltpu.CompilerParams(
            collective_id=collective, has_side_effects=True, vmem_limit_bytes=LIMIT
        ),
    )(tab, zmsg, perm_vk, perm_q)


def gather_kernel(cfg, has_vk, tab, chunks, perm_vk, perm_q, zrecv, zsend, *rest):
    recvs, (zs, zr, xs, xr) = rest[:-4], rest[-4:]
    me, ctx = lax.axis_index("dp"), lax.axis_index("ctx")
    greet(cfg, me, ctx)
    rows, n, c = cfg.rows, cfg.n_dp, cfg.n_ctx
    zq = rows if has_vk else 0
    parts = ([(0, rows)] if has_vk else []) + [(zq, rows // 2)]
    cparts = ([(0, cfg.chunk_vk)] if has_vk else []) + [
        (cfg.chunk_vk if has_vk else 0, cfg.chunk_q)
    ]
    zmoves = [exchange("ctx", c, ctx, i, p, zsend, zrecv, zs, zr) for i, p in enumerate(parts)]
    xmoves = [
        exchange("dp", n, me, i, p, chunks, recvs[i], xs, xr, 0) for i, p in enumerate(cparts)
    ]
    for move in xmoves:
        move[0]()
    for i, (at, size) in enumerate(cparts):
        recvs[i][me] = chunks[me, at : at + size]
    width = GROUP * BR

    def picked(block, part):
        return recvs[part][tab[cfg.tab_owner + block]]

    if has_vk:
        xmoves[0][1]()
        for g in range(cfg.blocks // GROUP):
            x = jnp.concatenate(
                [picked(GROUP * g + b, 0) for b in range(GROUP)], axis=0
            )
            y = mm(perm_vk[...], x).astype(BF)
            for i in range(c):
                zsend[i, width * g : width * (g + 1)] = y[width * i : width * (i + 1)]
        zmoves[0][0]()
    xmoves[-1][1]()
    half_blocks = cfg.blocks // 2
    for g in range(half_blocks // GROUP):
        at = zq + width * g
        xl = jnp.concatenate(
            [picked(GROUP * g + b, -1) for b in range(GROUP)], axis=0
        )
        xr_ = jnp.concatenate(
            [picked(half_blocks + GROUP * g + b, -1) for b in range(GROUP)], axis=0
        )
        yl, yr = mm(perm_q[...], xl), mm(perm_q[...], xr_)
        left = join(yl, swap(yr)).astype(BF)
        right = join(swap(yl), yr).astype(BF)
        for i in range(cfg.half):
            cut = slice(width * i, width * (i + 1))
            zsend[i, at : at + width] = left[cut]
            zsend[cfg.half + i, at : at + width] = right[cut]
    zmoves[-1][0]()
    zrecv[ctx] = zsend[ctx]
    for move in xmoves:
        move[2]()
    for move in zmoves:
        move[1]()
    for move in zmoves:
        move[2]()


def gather(cfg, has_vk, collective, tab, chunks, perm_vk, perm_q):
    zrows = (cfg.rows if has_vk else 0) + cfg.rows // 2
    parts = 2 if has_vk else 1
    return pl.pallas_call(
        functools.partial(gather_kernel, cfg, has_vk),
        name="gather",
        out_shape=jax.ShapeDtypeStruct((cfg.n_ctx, zrows, LANES), BF),
        in_specs=[SMEM, VMEM, VMEM, VMEM],
        out_specs=VMEM,
        scratch_shapes=[
            pltpu.VMEM((cfg.n_ctx, zrows, LANES), BF),
            *([pltpu.VMEM((cfg.n_dp, cfg.chunk_vk, LANES), BF)] if has_vk else []),
            pltpu.VMEM((cfg.n_dp, cfg.chunk_q, LANES), BF),
            pltpu.SemaphoreType.DMA((parts, cfg.n_ctx)),
            pltpu.SemaphoreType.DMA((parts, cfg.n_ctx)),
            pltpu.SemaphoreType.DMA((parts, cfg.n_dp)),
            pltpu.SemaphoreType.DMA((parts, cfg.n_dp)),
        ],
        compiler_params=pltpu.CompilerParams(
            collective_id=collective, has_side_effects=True, vmem_limit_bytes=LIMIT
        ),
    )(tab, chunks, perm_vk, perm_q)


def unpack_q(cfg, tab, recv, at, perm_qt, store):
    width = GROUP * BR
    own = tab[cfg.tab_own]
    for g in range(cfg.n_dp // GROUP):
        x = jnp.concatenate(
            [
                recv[lax.rem(own + GROUP * g + b, cfg.n_dp), at : at + cfg.chunk_q]
                for b in range(GROUP)
            ],
            axis=0,
        )
        y = mm(perm_qt[...], x)
        turned = swap(y)
        for i in range(cfg.half):
            cut = slice(width * i, width * (i + 1))
            store(i, g, y[cut], turned[cut])
            store(cfg.half + i, g, turned[cut], y[cut])


def segments(cfg, tab, rows):
    inside = lax.broadcasted_iota(jnp.int32, (rows, LANES), 0)
    first, total = tab[cfg.tab_own + 1], tab[cfg.tab_own + 2]
    return jnp.where(inside < first, 0, jnp.where(inside < total, 1, 2))


def pair_loop(count, body):
    pass


def forward_kernel(cfg, tab, recv, perm_vkt, perm_qt, perm_q, vk, qs, chunks, keys, att):
    width = GROUP * BR
    own = tab[cfg.tab_own]
    segment = segments(cfg, tab, cfg.span)
    which = lane((cfg.span, LANES))
    seg_q = jnp.where(which == segment, -BIG, 0.0)
    seg_k = jnp.where((which < 3) & (which != segment), 1.0, 0.0)
    for g in range(cfg.n_dp // GROUP):
        x = jnp.concatenate(
            [
                recv[lax.rem(own + GROUP * g + b, cfg.n_dp), : cfg.chunk_vk]
                for b in range(GROUP)
            ],
            axis=0,
        )
        y = mm(perm_vkt[...], x)
        inside = slice(width * g, width * (g + 1))
        for i in range(cfg.n_ctx):
            piece = y[width * i : width * (i + 1)]
            cut = slice(cfg.span * i + width * g, cfg.span * i + width * (g + 1))
            vk[cut] = piece.astype(BF)
            keys[cut] = join(seg_k[inside], piece).astype(BF)

    def store(i, g, left, right):
        cut = slice(cfg.span * i + width * g, cfg.span * i + width * (g + 1))
        qs[cut] = join(seg_q[width * g : width * (g + 1)], right * (0.5 * HEAD_DIM**-0.5)).astype(
            BF
        )

    unpack_q(cfg, tab, recv, cfg.chunk_vk, perm_qt, store)
    tile = cfg.tile
    above = lax.broadcasted_iota(jnp.int32, (tile, tile), 1) > lax.broadcasted_iota(
        jnp.int32, (tile, tile), 0
    )

    def one(i, j, diagonal):
        qt = qs[pl.ds(pl.multiple_of(i * tile, tile), tile)]
        at = pl.ds(pl.multiple_of(j * tile, tile), tile)
        h = mm_nt(qt, keys[at])
        if diagonal:
            h = jnp.where(above, -BIG, h)
        weights = (h + h * jnp.tanh(h)).astype(BF)
        return mm(weights, vk[at])

    def outer(i, carry):
        at = pl.ds(pl.multiple_of(i * tile, tile), tile)
        att[at] = one(i, i, True)

        def inner(j, carry):
            att[at] += one(i, j, False)
            return carry

        lax.fori_loop(0, i, inner, 0)
        return carry

    lax.fori_loop(0, cfg.total // tile, outer, 0)
    emit_q(cfg, own, att, perm_q, chunks, 0, False)


def emit_q(cfg, own, source, perm_q, chunks, base, in_right):
    width = GROUP * BR
    for g in range(cfg.n_dp // GROUP):
        xl, xr = (
            jnp.concatenate(
                [
                    source[cfg.span * i + width * g : cfg.span * i + width * (g + 1)]
                    for i in range(lo, lo + cfg.half)
                ],
                axis=0,
            )
            for lo in (0, cfg.half)
        )
        both = join(swap(xl), xr) if in_right else join(xl, swap(xr))
        y = mm(perm_q[...], both.astype(BF)).astype(BF)
        for b in range(GROUP):
            chunks[lax.rem(own + GROUP * g + b, cfg.n_dp), base : base + cfg.chunk_q] = y[
                b * cfg.chunk_q : (b + 1) * cfg.chunk_q
            ]


def forward_attention(cfg, tab, recv, perms):
    return pl.pallas_call(
        functools.partial(forward_kernel, cfg),
        name="attend",
        out_shape=(
            jax.ShapeDtypeStruct((cfg.total, LANES), BF),
            jax.ShapeDtypeStruct((cfg.total, LANES), BF),
            jax.ShapeDtypeStruct((cfg.n_dp, cfg.chunk_q, LANES), BF),
        ),
        in_specs=[SMEM] + [VMEM] * 4,
        out_specs=(VMEM,) * 3,
        scratch_shapes=[
            pltpu.VMEM((cfg.total, LANES), BF),
            pltpu.VMEM((cfg.total, LANES), F32),
        ],
        compiler_params=pltpu.CompilerParams(vmem_limit_bytes=LIMIT),
    )(tab, recv, perms["vk_t"], perms["q_t"], perms["q"])


def backward_kernel(
    cfg, tab, recv, vk, qs, perm_vk, perm_qt, perm_q, chunks, keys, go, qz, dvk, dqt, dq
):
    width = GROUP * BR
    own = tab[cfg.tab_own]
    segment = segments(cfg, tab, cfg.span)
    which = lane((cfg.span, LANES))
    seg_k = jnp.where((which < 3) & (which != segment), 1.0, 0.0).astype(BF)
    zero = jnp.zeros((cfg.span, LANES), BF)
    for i in range(cfg.n_ctx):
        cut = slice(cfg.span * i, cfg.span * (i + 1))
        keys[cut] = join(seg_k, vk[cut])
        qz[cut] = join(zero, qs[cut])

    def store(i, g, left, right):
        cut = slice(cfg.span * i + width * g, cfg.span * i + width * (g + 1))
        go[cut] = join(left, jnp.zeros_like(left)).astype(BF)

    unpack_q(cfg, tab, recv, 0, perm_qt, store)
    tile = cfg.tile
    count = cfg.total // tile
    below = lax.broadcasted_iota(jnp.int32, (tile, tile), 0) > lax.broadcasted_iota(
        jnp.int32, (tile, tile), 1
    )
    dqt[...] = jnp.zeros_like(dqt)

    def outer(j, carry):
        jt = pl.ds(pl.multiple_of(j * tile, tile), tile)
        key, both = keys[jt], vk[jt]
        both_t = both.T

        def one(i, diagonal):
            it = pl.ds(pl.multiple_of(i * tile, tile), tile)
            h = mm_nt(key, qs[it])
            if diagonal:
                h = jnp.where(below, -BIG, h)
            p = 1.0 + jnp.tanh(h)
            a = h * p
            weights = a.astype(BF)
            ga = mm_nt(both, go[it])
            grad_s = (ga * p * ((2.0 * h + 1.0) - a)).astype(BF)
            dqt[:, it] += mm(both_t, grad_s)
            return mm(weights, go[it]) + mm(grad_s, qz[it])

        dvk[jt] = one(j, True)

        def inner(i, carry):
            dvk[jt] += one(i, False)
            return carry

        lax.fori_loop(j + 1, count, inner, 0)
        return carry

    lax.fori_loop(0, count, outer, 0)

    for i in range(count):
        cut = slice(tile * i, tile * (i + 1))
        dq[cut] = dqt[:, cut].T * (0.5 * HEAD_DIM**-0.5)
    for g in range(cfg.n_dp // GROUP):
        x = jnp.concatenate(
            [
                dvk[cfg.span * i + width * g : cfg.span * i + width * (g + 1)]
                for i in range(cfg.n_ctx)
            ],
            axis=0,
        )
        y = mm(perm_vk[...], x.astype(BF)).astype(BF)
        for b in range(GROUP):
            chunks[lax.rem(own + GROUP * g + b, cfg.n_dp), : cfg.chunk_vk] = y[
                b * cfg.chunk_vk : (b + 1) * cfg.chunk_vk
            ]
    emit_q(cfg, own, dq, perm_q, chunks, cfg.chunk_vk, True)


def backward_attention(cfg, tab, recv, vk, qs, perms):
    return pl.pallas_call(
        functools.partial(backward_kernel, cfg),
        name="attend_back",
        out_shape=jax.ShapeDtypeStruct((cfg.n_dp, cfg.chunk_vk + cfg.chunk_q, LANES), BF),
        in_specs=[SMEM] + [VMEM] * 6,
        out_specs=VMEM,
        scratch_shapes=[
            pltpu.VMEM((cfg.total, LANES), BF),
            pltpu.VMEM((cfg.total, LANES), BF),
            pltpu.VMEM((cfg.total, LANES), BF),
            pltpu.VMEM((cfg.total, LANES), F32),
            pltpu.VMEM((LANES, cfg.total), F32),
            pltpu.VMEM((cfg.total, LANES), F32),
        ],
        compiler_params=pltpu.CompilerParams(vmem_limit_bytes=LIMIT),
    )(tab, recv, vk, qs, perms["vk"], perms["q_t"], perms["q"])


def shards(n_dp, n_ctx, embedded, upstream, w_uvqk, w_out, lengths):
    cfg = Cfg(n_dp, n_ctx, embedded.shape[1], embedded.shape[2])
    perm_vk, perm_q = permutation(n_ctx), permutation(n_ctx // 2)
    perms = {
        "vk": jnp.asarray(perm_vk, BF),
        "vk_t": jnp.asarray(perm_vk.T, BF),
        "q": jnp.asarray(perm_q, BF),
        "q_t": jnp.asarray(perm_q.T, BF),
    }
    dp_index = lax.axis_index("dp").astype(jnp.int32).reshape(1)
    tab, pre, zmsg = pre_work(cfg, dp_index, lengths, embedded, w_uvqk)
    recv = scatter(cfg, True, 0, tab, zmsg, perms["vk"], perms["q"])
    vk, qs, chunks = forward_attention(cfg, tab, recv, perms)
    zatt = gather(cfg, False, 1, tab, chunks, perms["vk_t"], perms["q_t"])
    layer_out, zmsg2, gpu, term_out = mid_work(cfg, zatt, pre, embedded, upstream, w_out)
    recv2 = scatter(cfg, False, 2, tab, zmsg2, perms["vk"], perms["q"])
    chunks2 = backward_attention(cfg, tab, recv2, vk, qs, perms)
    zgrad = gather(cfg, True, 3, tab, chunks2, perms["vk_t"], perms["q_t"])
    gradient, term = post_work(cfg, zgrad, gpu, pre, embedded, upstream, w_uvqk)
    token_scale = (cfg.rows * n_dp * n_ctx) ** (-0.5)

    def reduced(value):
        value = lax.psum_scatter(value, "dp", scatter_dimension=1, tiled=True)
        value = lax.psum_scatter(value, "ctx", scatter_dimension=0, tiled=True)
        return value.astype(F32) * token_scale

    return layer_out, gradient, reduced(term), reduced(term_out)


def solution(mesh):
    return jax.shard_map(
        functools.partial(shards, mesh.shape["dp"], mesh.shape["ctx"]),
        mesh=mesh,
        in_specs=(P("ctx", "dp", None), P("ctx", "dp", None), P(), P(), P()),
        out_specs=(P("ctx", "dp", None), P("ctx", "dp", None), P("ctx", "dp"), P("ctx", "dp")),
        check_vma=False,
    )
```

```python
import functools
import math

import jax
import jax.numpy as jnp
import numpy as np
from jax import lax
from jax.experimental import pallas as pl
from jax.experimental.pallas import tpu as pltpu
from jax.sharding import PartitionSpec as P

HEAD_DIM = 64
BR = 12
SEQ_DP = 2
GROUP = 4
LANES = 128
EPS = 1e-06
BIG = 1e30
MESH = pl.DeviceIdType.MESH
BF = jnp.bfloat16
F32 = jnp.float32
VMEM = pl.BlockSpec(memory_space=pltpu.VMEM)
SMEM = pl.BlockSpec(memory_space=pltpu.SMEM)
LIMIT = 48 * 1024 * 1024


class Cfg:
    def __init__(self, n_dp, n_ctx, rows, width):
        self.n_dp = n_dp
        self.n_ctx = n_ctx
        self.rows = rows
        self.width = width
        self.blocks = rows // BR
        self.heads = n_ctx
        self.hd = self.heads * HEAD_DIM
        self.half = n_ctx // 2
        self.chunk_vk = n_ctx * BR
        self.chunk_q = n_ctx * BR // 2
        self.span = n_dp * BR
        self.side = math.isqrt(n_dp // 2)
        self.total = n_ctx * self.span
        self.tile = min(512, self.total // 3)
        self.tab_owner = n_dp
        self.tab_own = n_dp + self.blocks + 1


def permutation(contexts):
    size = contexts * GROUP * BR
    matrix = np.zeros((size, size), np.float32)
    for block in range(GROUP):
        for context in range(contexts):
            for row in range(BR):
                matrix[
                    (block * contexts + context) * BR + row, (context * GROUP + block) * BR + row
                ] = 1.0
    return matrix


def lane(shape):
    return lax.broadcasted_iota(jnp.int32, shape, len(shape) - 1)


def swap(tensor):
    return pltpu.roll(tensor, HEAD_DIM, 1)


def join(left, right):
    return jnp.where(lane(left.shape) < HEAD_DIM, left, right)


def mm(left, right):
    return jnp.dot(left, right, preferred_element_type=F32)


def mm_nt(left, right):
    return lax.dot_general(left, right, (((1,), (1,)), ((), ())), preferred_element_type=F32)


def layer_normalize(tensor):
    centre = jnp.mean(tensor, -1, keepdims=True)
    centred = tensor - centre
    inverse = lax.rsqrt(jnp.mean(centred * centred, -1, keepdims=True) + EPS)
    return centred * inverse, inverse


def layer_norm_backward(incoming, normal, inverse):
    first = jnp.mean(incoming, -1, keepdims=True)
    second = jnp.mean(incoming * normal, -1, keepdims=True)
    return (incoming - first - normal * second) * inverse


def silu(argument):
    return argument * jax.nn.sigmoid(argument)


def silu_grad(argument):
    sigmoid = jax.nn.sigmoid(argument)
    return sigmoid * (1.0 + argument * (1.0 - sigmoid))


def pre_kernel(cfg, dp_ref, lengths, x, w, tab, pre, zmsg):
    me = dp_ref[0]
    n = cfg.n_dp
    wrap = n * cfg.blocks * n

    def owner(o, start):
        first = lengths[SEQ_DP * o]
        total = first + lengths[SEQ_DP * o + 1]
        block = start + lax.rem(me - start + wrap, n)
        index = (block - me) // n
        tab[o] = jnp.clip(index, 0, cfg.blocks - 1)
        held = block < start + total
        tab[cfg.tab_owner + jnp.where(held, index, cfg.blocks)] = o

        @pl.when(o == me)
        def _():
            tab[cfg.tab_own] = lax.rem(start, n)
            tab[cfg.tab_own + 1] = first * BR
            tab[cfg.tab_own + 2] = total * BR

        return start + total

    lax.fori_loop(0, n, owner, jnp.int32(0))
    normal, _ = layer_normalize(x[0].astype(F32))
    normed = normal.astype(BF)
    hd = cfg.hd
    mid = cfg.rows // 2
    step = min(256, hd)
    for base in range(0, hd, step):
        parts = []
        for section in range(4):
            at = section * hd + base
            value = mm(normed, w[:, at : at + step])
            pre[:, at : at + step] = value
            parts.append(silu(value))
        for tile in range(step // LANES):
            cut = slice(tile * LANES, (tile + 1) * LANES)
            v, q, k = parts[1][:, cut], parts[2][:, cut], parts[3][:, cut]
            head = (base + tile * LANES) // HEAD_DIM
            zmsg[head, : cfg.rows] = join(v, swap(k)).astype(BF)
            zmsg[head + 1, : cfg.rows] = join(swap(v), k).astype(BF)
            zmsg[head, cfg.rows :] = join(q[:mid], swap(q[mid:])).astype(BF)
            zmsg[head + 1, cfg.rows :] = join(swap(q[:mid]), q[mid:]).astype(BF)


def pre_work(cfg, dp_index, lengths, x, w):
    return pl.pallas_call(
        functools.partial(pre_kernel, cfg),
        name="pre",
        out_shape=(
            jax.ShapeDtypeStruct((cfg.tab_own + 3,), jnp.int32),
            jax.ShapeDtypeStruct((cfg.rows, 4 * cfg.hd), F32),
            jax.ShapeDtypeStruct((cfg.heads, cfg.rows * 3 // 2, LANES), BF),
        ),
        in_specs=[SMEM, SMEM, VMEM, VMEM],
        out_specs=(SMEM, VMEM, VMEM),
        compiler_params=pltpu.CompilerParams(vmem_limit_bytes=LIMIT),
    )(dp_index, lengths, x, w)


def mid_kernel(cfg, zatt, pre, x, up, w_out, out, zmsg, gpu, t_out):
    hd = cfg.hd
    mid = cfg.rows // 2
    tops, bottoms = [], []
    for head in range(0, cfg.heads, 2):
        a, b = zatt[head].astype(F32), zatt[head + 1].astype(F32)
        tops.append(join(a, swap(b)))
        bottoms.append(join(swap(a), b))
    att = jnp.concatenate(
        [jnp.concatenate(tops, axis=1), jnp.concatenate(bottoms, axis=1)], axis=0
    )
    att_norm, att_inverse = layer_normalize(att)
    pre_u = pre[...]
    gate = silu(pre_u).astype(BF).astype(F32)
    gated = (att_norm * gate).astype(BF)
    out[0] = (x[0].astype(F32) + mm(gated, w_out[...])).astype(BF)
    upstream = up[0]
    back = mm_nt(upstream, w_out[...])
    gpu[...] = (back * att_norm * silu_grad(pre_u)).astype(BF)
    grad_att = layer_norm_backward(back * gate, att_norm, att_inverse)
    for tile in range(hd // LANES):
        g = grad_att[:, tile * LANES : (tile + 1) * LANES]
        zmsg[2 * tile] = join(g[:mid], swap(g[mid:])).astype(BF)
        zmsg[2 * tile + 1] = join(swap(g[:mid]), g[mid:]).astype(BF)
    pack_out_term(
        cfg,
        lax.dot_general(
            gated, upstream, (((0,), (0,)), ((), ())), preferred_element_type=F32
        ),
        t_out,
    )


def pack_out_term(cfg, term, t_out):
    side = cfg.side
    for tile in range(cfg.width // LANES):
        straight = term[:, tile * LANES : (tile + 1) * LANES]
        turned = swap(straight)
        for c in range(cfg.n_ctx):
            at = c * HEAD_DIM
            mid, end = at + HEAD_DIM // 2, at + HEAD_DIM
            pieces = (
                join(straight[at:mid], turned[mid:end]),
                join(turned[at:mid], straight[mid:end]),
            )
            for odd, piece in enumerate(pieces):
                x, y = divmod(2 * tile + odd, side)
                place = (0, x, y) if c < cfg.half else (1, y, x)
                t_out[(*place, c % cfg.half)] = piece.astype(BF)


def mid_work(cfg, zatt, pre, x, up, w_out):
    return pl.pallas_call(
        functools.partial(mid_kernel, cfg),
        name="mid",
        grid=(1,),
        out_shape=(
            jax.ShapeDtypeStruct(x.shape, BF),
            jax.ShapeDtypeStruct((cfg.heads, cfg.rows // 2, LANES), BF),
            jax.ShapeDtypeStruct((cfg.rows, cfg.hd), BF),
            jax.ShapeDtypeStruct((2, cfg.side, cfg.side, cfg.half, 32, LANES), BF),
        ),
        in_specs=[
            VMEM,
            pl.BlockSpec((cfg.rows, cfg.hd), lambda i: (0, 0)),
            VMEM,
            VMEM,
            VMEM,
        ],
        out_specs=(VMEM, VMEM, VMEM, VMEM),
        compiler_params=pltpu.CompilerParams(vmem_limit_bytes=LIMIT),
    )(zatt, pre, x, up, w_out)


def post_kernel(
    cfg,
    zgrad,
    gpu,
    pre,
    x,
    up,
    w,
    t_out,
    gradient,
    gw,
    go,
    gp,
    gpt,
    normal_t,
    send0,
    recv0,
    send1,
    recv1,
    send2,
    recv2,
    zsend,
    zrecv,
    acc1,
    ss0,
    rs0,
    ss1,
    rs1,
    ss2,
    rs2,
    ssz,
    rsz,
):
    hd, rows, side, half, n_ctx = cfg.hd, cfg.rows, cfg.side, cfg.half, cfg.n_ctx
    me, ctx = lax.axis_index("dp"), lax.axis_index("ctx")
    core = lax.rem(me, 2)
    chip_x, chip_y = me // (2 * side), lax.rem(me // 2, side)
    a_own = chip_x * (1 - core) + chip_y * core
    b_own = chip_y * (1 - core) + chip_x * core
    along_a = 2 * side - core * (2 * side - 2)
    along_b = 2 + core * (2 * side - 2)
    partner = me + 1 - 2 * core
    home = ctx // half

    def device(a, b):
        return a * along_a + b * along_b + core

    barrier = pltpu.get_barrier_semaphore()

    def greet_dp(other):
        pl.semaphore_signal(barrier, inc=1, device_id={"dp": other}, device_id_type=MESH)

    greet_dp(partner)
    for i in range(side - 1):
        greet_dp(device(lax.rem(a_own + 1 + i, side), b_own))
        greet_dp(device(a_own, lax.rem(b_own + 1 + i, side)))
    for z in range(n_ctx):

        @pl.when(jnp.logical_or(z != ctx, home != core))
        def _():
            pl.semaphore_signal(
                barrier,
                inc=1,
                device_id={"dp": me - core + home, "ctx": z},
                device_id_type=MESH,
            )

    gp[:, :hd] = gpu[...]
    mid = rows // 2
    for head in range(0, cfg.heads, 2):
        a, b = zgrad[head].astype(F32), zgrad[head + 1].astype(F32)
        av, bv = a[:rows], b[:rows]
        aq, bq = a[rows:], b[rows:]
        grad_v = join(av, swap(bv))
        grad_k = join(swap(av), bv)
        grad_q = jnp.concatenate([join(aq, swap(bq)), join(swap(aq), bq)], axis=0)
        for section, value in ((1, grad_v), (2, grad_q), (3, grad_k)):
            at = section * hd + head * HEAD_DIM
            cut = slice(at, at + LANES)
            gp[:, cut] = (value * silu_grad(pre[:, cut])).astype(BF)
    for tile in range(4 * hd // LANES):
        gpt[tile] = gp[:, tile * LANES : (tile + 1) * LANES]
    normal, inverse = layer_normalize(x[0].astype(F32))
    normal_t[...] = normal.T.astype(BF)
    block = cfg.width // n_ctx

    def term(k, a, b):
        tiles = [
            gpt[a * (side - k * (side - 1)) + (b + i) * (1 + k * (side - 1))] for i in range(2)
        ]
        left = normal_t[pl.ds(pl.multiple_of(k * half * block, half * block), half * block)]
        return mm(left, jnp.concatenate(tiles, axis=1)).reshape(half, block, 2 * LANES)

    def swap_copy(a):
        return pltpu.make_async_remote_copy(
            src_ref=send0.at[a],
            dst_ref=recv0.at[a],
            send_sem=ss0.at[a],
            recv_sem=rs0.at[a],
            device_id={"dp": partner},
            device_id_type=MESH,
        )

    other_half = 1 - core
    pl.semaphore_wait(
        barrier, 2 * side - 1 + n_ctx - jnp.where(home == core, 1, 0).astype(jnp.int32)
    )

    def give(i, carry):
        a = lax.rem(b_own + 1 + i, side)
        for b in range(0, side, 2):
            value = term(other_half, a, b).astype(BF)
            for j in range(2):
                send0[a, b + j, :, :block] = value[:, :, j * LANES : (j + 1) * LANES]
                send0[a, b + j, :, block:] = t_out[other_half, a, b + j]
        swap_copy(a).start()
        return carry

    lax.fori_loop(0, side, give, 0)

    def copy1(i):
        a = lax.rem(a_own + 1 + i, side)
        return pltpu.make_async_remote_copy(
            src_ref=send1.at[a],
            dst_ref=recv1.at[i],
            send_sem=ss1.at[i],
            recv_sem=rs1.at[i],
            device_id={"dp": device(a, b_own)},
            device_id_type=MESH,
        )

    def keep(a, b):
        value = term(core, a, b)
        for j in range(2):
            front = value[:, :, j * LANES : (j + 1) * LANES] + recv0[a, b + j, :, :block].astype(
                F32
            )
            back = t_out[core, a, b + j].astype(F32) + recv0[a, b + j, :, block:].astype(F32)
            yield b + j, front, back

    def take(i, carry):
        a = lax.rem(a_own + 1 + i, side)
        swap_copy(a).wait_recv()
        for b in range(0, side, 2):
            for at, front, back in keep(a, b):
                send1[a, at, :, :block] = front.astype(BF)
                send1[a, at, :, block:] = back.astype(BF)
        copy1(i).start()
        return carry

    lax.fori_loop(0, side - 1, take, 0)
    swap_copy(a_own).wait_recv()
    for b in range(0, side, 2):
        for at, front, back in keep(a_own, b):
            acc1[at, :, :block] = front
            acc1[at, :, block:] = back

    back = mm_nt(gp[...], w[...])
    gradient[0] = (up[0].astype(F32) + layer_norm_backward(back, normal, inverse)).astype(BF)

    def copy2(i):
        b = lax.rem(b_own + 1 + i, side)
        return pltpu.make_async_remote_copy(
            src_ref=send2.at[b],
            dst_ref=recv2.at[i],
            send_sem=ss2.at[i],
            recv_sem=rs2.at[i],
            device_id={"dp": device(a_own, b)},
            device_id_type=MESH,
        )

    for i in range(side - 1):
        copy1(i).wait_recv()

    def sum1(b):
        total = acc1[b]
        for i in range(side - 1):
            total = total + recv1[i, b].astype(F32)
        return total

    for i in range(side - 1):
        b = lax.rem(b_own + 1 + i, side)
        send2[b] = sum1(b).astype(BF)
        copy2(i).start()
    total = sum1(b_own)
    for i in range(side - 1):
        copy2(i).wait_recv()
        total = total + recv2[i].astype(F32)

    quarter = lax.rem(lane((16, LANES)), HEAD_DIM) < 32
    for h in range(half):
        top, low = total[h, : block // 2], total[h, block // 2 : block]
        u, v = total[h, block : block + 16], total[h, block + 16 :]
        zsend[h, 0, : block // 2] = join(top, swap(low)).astype(BF)
        zsend[h, 1, : block // 2] = join(swap(top), low).astype(BF)
        zsend[h, 0, block // 2 :] = jnp.where(quarter, u, pltpu.roll(v, 32, 1)).astype(BF)
        zsend[h, 1, block // 2 :] = jnp.where(quarter, pltpu.roll(u, 96, 1), v).astype(BF)

    def copyz(h, kind):
        return pltpu.make_async_remote_copy(
            src_ref=zsend.at[h, kind],
            dst_ref=zrecv.at[ctx],
            send_sem=ssz.at[h, kind],
            recv_sem=rsz.at[ctx],
            device_id={"dp": me - core + kind, "ctx": half * core + h},
            device_id_type=MESH,
        )

    def arrival(z):
        return pltpu.make_async_remote_copy(
            src_ref=zsend.at[0, 0],
            dst_ref=zrecv.at[z],
            send_sem=ssz.at[0, 0],
            recv_sem=rsz.at[z],
            device_id={"dp": me - core + home, "ctx": z},
            device_id_type=MESH,
        )

    for h in range(half):
        for kind in range(2):
            stays = jnp.logical_and(half * core + h == ctx, kind == core)

            @pl.when(stays)
            def _():
                zrecv[ctx] = zsend[h, kind]

            @pl.when(jnp.logical_not(stays))
            def _():
                copyz(h, kind).start()

    for z in range(n_ctx):

        @pl.when(jnp.logical_or(z != ctx, home != core))
        def _():
            arrival(z).wait_recv()

    total = zrecv[0].astype(F32)
    for z in range(1, n_ctx):
        total = total + zrecv[z].astype(F32)
    total = total * (rows * cfg.n_dp * n_ctx) ** -0.5
    front, back = total[: block // 2], total[block // 2 :]
    gw[: block // 2] = front[:, :HEAD_DIM]
    gw[block // 2 :] = swap(front)[:, :HEAD_DIM]
    for i in range(4):
        piece = back if i == 0 else pltpu.roll(back, LANES - 32 * i, 1)
        go[16 * i : 16 * (i + 1)] = piece[:, :32]

    for a in range(side):
        swap_copy(a).wait_send()
    for i in range(side - 1):
        copy1(i).wait_send()
        copy2(i).wait_send()
    for h in range(half):
        for kind in range(2):

            @pl.when(jnp.logical_not(jnp.logical_and(half * core + h == ctx, kind == core)))
            def _():
                copyz(h, kind).wait_send()


def post_work(cfg, collective, zgrad, gpu, pre, x, up, w, t_out):
    side, half, block = cfg.side, cfg.half, cfg.width // cfg.n_ctx
    deep = block + 32
    dma = pltpu.SemaphoreType.DMA
    return pl.pallas_call(
        functools.partial(post_kernel, cfg),
        name="post",
        out_shape=(
            jax.ShapeDtypeStruct(x.shape, BF),
            jax.ShapeDtypeStruct((block, 4 * cfg.hd // cfg.n_dp), F32),
            jax.ShapeDtypeStruct((HEAD_DIM, cfg.width // cfg.n_dp), F32),
        ),
        in_specs=[VMEM] * 7,
        out_specs=(VMEM,) * 3,
        scratch_shapes=[
            pltpu.VMEM((cfg.rows, 4 * cfg.hd), BF),
            pltpu.VMEM((4 * cfg.hd // LANES, cfg.rows, LANES), BF),
            pltpu.VMEM((cfg.width, cfg.rows), BF),
            pltpu.VMEM((side, side, half, deep, LANES), BF),
            pltpu.VMEM((side, side, half, deep, LANES), BF),
            pltpu.VMEM((side, side, half, deep, LANES), BF),
            pltpu.VMEM((side - 1, side, half, deep, LANES), BF),
            pltpu.VMEM((side, half, deep, LANES), BF),
            pltpu.VMEM((side - 1, half, deep, LANES), BF),
            pltpu.VMEM((half, 2, deep // 2, LANES), BF),
            pltpu.VMEM((cfg.n_ctx, deep // 2, LANES), BF),
            pltpu.VMEM((side, half, deep, LANES), F32),
            dma((side,)),
            dma((side,)),
            dma((side - 1,)),
            dma((side - 1,)),
            dma((side - 1,)),
            dma((side - 1,)),
            dma((half, 2)),
            dma((cfg.n_ctx,)),
        ],
        compiler_params=pltpu.CompilerParams(
            collective_id=collective, has_side_effects=True, vmem_limit_bytes=LIMIT
        ),
    )(zgrad, gpu, pre, x, up, w, t_out)


def greet(cfg, me, ctx):
    barrier = pltpu.get_barrier_semaphore()

    def along_dp(k, carry):
        pl.semaphore_signal(
            barrier, inc=1, device_id={"dp": lax.rem(me + k, cfg.n_dp)}, device_id_type=MESH
        )
        return carry

    def along_ctx(k, carry):
        pl.semaphore_signal(
            barrier, inc=1, device_id={"ctx": lax.rem(ctx + k, cfg.n_ctx)}, device_id_type=MESH
        )
        return carry

    lax.fori_loop(1, cfg.n_dp, along_dp, 0)
    lax.fori_loop(1, cfg.n_ctx, along_ctx, 0)
    pl.semaphore_wait(barrier, cfg.n_dp + cfg.n_ctx - 2)


def exchange(axis, count, mine, part, rows, source, target, send_sem, recv_sem, land=None):
    land = rows[0] if land is None else land

    def copy(other):
        return pltpu.make_async_remote_copy(
            src_ref=source.at[other, pl.ds(rows[0], rows[1])],
            dst_ref=target.at[mine, pl.ds(land, rows[1])],
            send_sem=send_sem.at[part, other],
            recv_sem=recv_sem.at[part, mine],
            device_id={axis: other},
            device_id_type=MESH,
        )

    def arrival(other):
        return pltpu.make_async_remote_copy(
            src_ref=source.at[other, pl.ds(rows[0], rows[1])],
            dst_ref=target.at[other, pl.ds(land, rows[1])],
            send_sem=send_sem.at[part, other],
            recv_sem=recv_sem.at[part, other],
            device_id={axis: other},
            device_id_type=MESH,
        )

    def start(k, carry):
        copy(lax.rem(mine + k, count)).start()
        return carry

    def wait_recv(k, carry):
        arrival(lax.rem(mine + k, count)).wait_recv()
        return carry

    def wait_send(k, carry):
        copy(lax.rem(mine + k, count)).wait_send()
        return carry

    return (
        lambda: lax.fori_loop(1, count, start, 0),
        lambda: lax.fori_loop(1, count, wait_recv, 0),
        lambda: lax.fori_loop(1, count, wait_send, 0),
        copy,
    )


def scatter_kernel(cfg, has_vk, tab, zmsg, perm_vk, perm_q, recv, zrecv, chunks, sendbuf, *sems):
    zs, zr, xs, xr = sems
    me, ctx = lax.axis_index("dp"), lax.axis_index("ctx")
    greet(cfg, me, ctx)
    rows, n, c = cfg.rows, cfg.n_dp, cfg.n_ctx
    zq = rows if has_vk else 0
    cq = cfg.chunk_vk if has_vk else 0
    parts = ([(0, rows)] if has_vk else []) + [(zq, rows // 2)]
    cparts = ([(0, cfg.chunk_vk)] if has_vk else []) + [(cq, cfg.chunk_q)]
    zmoves = [exchange("ctx", c, ctx, i, p, zmsg, zrecv, zs, zr) for i, p in enumerate(parts)]
    xmoves = [exchange("dp", n, me, i, p, sendbuf, recv, xs, xr) for i, p in enumerate(cparts)]
    for move in zmoves:
        move[0]()
    zrecv[ctx] = zmsg[ctx]
    width = GROUP * BR

    def forward(i):
        at, size = cparts[i]
        recv[me, at : at + size] = chunks[tab[me], at : at + size]

        def one(k, carry):
            other = lax.rem(me + k, n)
            sendbuf[other, at : at + size] = chunks[tab[other], at : at + size]
            xmoves[i][3](other).start()
            return carry

        lax.fori_loop(1, n, one, 0)

    if has_vk:
        zmoves[0][1]()
        for g in range(cfg.blocks // GROUP):
            x = jnp.concatenate([zrecv[i, width * g : width * (g + 1)] for i in range(c)], axis=0)
            y = mm(perm_vk[...], x).astype(BF)
            for b in range(GROUP):
                chunks[GROUP * g + b, : cfg.chunk_vk] = y[
                    b * cfg.chunk_vk : (b + 1) * cfg.chunk_vk
                ]
        forward(0)
    zmoves[-1][1]()
    half_blocks = cfg.blocks // 2
    for g in range(half_blocks // GROUP):
        at = zq + width * g
        xl = jnp.concatenate([zrecv[i, at : at + width] for i in range(cfg.half)], axis=0)
        xr_ = jnp.concatenate([zrecv[i, at : at + width] for i in range(cfg.half, c)], axis=0)
        yl, yr = mm(perm_q[...], xl), mm(perm_q[...], xr_)
        left = join(yl, swap(yr)).astype(BF)
        right = join(swap(yl), yr).astype(BF)
        for b in range(GROUP):
            cut = slice(b * cfg.chunk_q, (b + 1) * cfg.chunk_q)
            chunks[GROUP * g + b, cq:] = left[cut]
            chunks[half_blocks + GROUP * g + b, cq:] = right[cut]
    forward(len(parts) - 1)
    for move in zmoves:
        move[2]()
    for move in xmoves:
        move[1]()
    for move in xmoves:
        move[2]()


def scatter(cfg, has_vk, collective, tab, zmsg, perm_vk, perm_q):
    size = (cfg.chunk_vk if has_vk else 0) + cfg.chunk_q
    parts = 2 if has_vk else 1
    return pl.pallas_call(
        functools.partial(scatter_kernel, cfg, has_vk),
        name="scatter",
        out_shape=jax.ShapeDtypeStruct((cfg.n_dp, size, LANES), BF),
        in_specs=[SMEM, VMEM, VMEM, VMEM],
        out_specs=VMEM,
        scratch_shapes=[
            pltpu.VMEM(zmsg.shape, BF),
            pltpu.VMEM((cfg.blocks, size, LANES), BF),
            pltpu.VMEM((cfg.n_dp, size, LANES), BF),
            pltpu.SemaphoreType.DMA((parts, cfg.n_ctx)),
            pltpu.SemaphoreType.DMA((parts, cfg.n_ctx)),
            pltpu.SemaphoreType.DMA((parts, cfg.n_dp)),
            pltpu.SemaphoreType.DMA((parts, cfg.n_dp)),
        ],
        compiler_params=pltpu.CompilerParams(
            collective_id=collective, has_side_effects=True, vmem_limit_bytes=LIMIT
        ),
    )(tab, zmsg, perm_vk, perm_q)


def gather_kernel(cfg, has_vk, tab, chunks, perm_vk, perm_q, zrecv, zsend, *rest):
    recvs, (zs, zr, xs, xr) = rest[:-4], rest[-4:]
    me, ctx = lax.axis_index("dp"), lax.axis_index("ctx")
    greet(cfg, me, ctx)
    rows, n, c = cfg.rows, cfg.n_dp, cfg.n_ctx
    zq = rows if has_vk else 0
    parts = ([(0, rows)] if has_vk else []) + [(zq, rows // 2)]
    cparts = ([(0, cfg.chunk_vk)] if has_vk else []) + [
        (cfg.chunk_vk if has_vk else 0, cfg.chunk_q)
    ]
    zmoves = [exchange("ctx", c, ctx, i, p, zsend, zrecv, zs, zr) for i, p in enumerate(parts)]
    xmoves = [
        exchange("dp", n, me, i, p, chunks, recvs[i], xs, xr, 0) for i, p in enumerate(cparts)
    ]
    for move in xmoves:
        move[0]()
    for i, (at, size) in enumerate(cparts):
        recvs[i][me] = chunks[me, at : at + size]
    width = GROUP * BR

    def picked(block, part):
        return recvs[part][tab[cfg.tab_owner + block]]

    if has_vk:
        xmoves[0][1]()
        for g in range(cfg.blocks // GROUP):
            x = jnp.concatenate(
                [picked(GROUP * g + b, 0) for b in range(GROUP)], axis=0
            )
            y = mm(perm_vk[...], x).astype(BF)
            for i in range(c):
                zsend[i, width * g : width * (g + 1)] = y[width * i : width * (i + 1)]
        zmoves[0][0]()
    xmoves[-1][1]()
    half_blocks = cfg.blocks // 2
    for g in range(half_blocks // GROUP):
        at = zq + width * g
        xl = jnp.concatenate(
            [picked(GROUP * g + b, -1) for b in range(GROUP)], axis=0
        )
        xr_ = jnp.concatenate(
            [picked(half_blocks + GROUP * g + b, -1) for b in range(GROUP)], axis=0
        )
        yl, yr = mm(perm_q[...], xl), mm(perm_q[...], xr_)
        left = join(yl, swap(yr)).astype(BF)
        right = join(swap(yl), yr).astype(BF)
        for i in range(cfg.half):
            cut = slice(width * i, width * (i + 1))
            zsend[i, at : at + width] = left[cut]
            zsend[cfg.half + i, at : at + width] = right[cut]
    zmoves[-1][0]()
    zrecv[ctx] = zsend[ctx]
    for move in xmoves:
        move[2]()
    for move in zmoves:
        move[1]()
    for move in zmoves:
        move[2]()


def gather(cfg, has_vk, collective, tab, chunks, perm_vk, perm_q):
    zrows = (cfg.rows if has_vk else 0) + cfg.rows // 2
    parts = 2 if has_vk else 1
    return pl.pallas_call(
        functools.partial(gather_kernel, cfg, has_vk),
        name="gather",
        out_shape=jax.ShapeDtypeStruct((cfg.n_ctx, zrows, LANES), BF),
        in_specs=[SMEM, VMEM, VMEM, VMEM],
        out_specs=VMEM,
        scratch_shapes=[
            pltpu.VMEM((cfg.n_ctx, zrows, LANES), BF),
            *([pltpu.VMEM((cfg.n_dp, cfg.chunk_vk, LANES), BF)] if has_vk else []),
            pltpu.VMEM((cfg.n_dp, cfg.chunk_q, LANES), BF),
            pltpu.SemaphoreType.DMA((parts, cfg.n_ctx)),
            pltpu.SemaphoreType.DMA((parts, cfg.n_ctx)),
            pltpu.SemaphoreType.DMA((parts, cfg.n_dp)),
            pltpu.SemaphoreType.DMA((parts, cfg.n_dp)),
        ],
        compiler_params=pltpu.CompilerParams(
            collective_id=collective, has_side_effects=True, vmem_limit_bytes=LIMIT
        ),
    )(tab, chunks, perm_vk, perm_q)


def unpack_q(cfg, tab, recv, at, perm_qt, store):
    width = GROUP * BR
    own = tab[cfg.tab_own]
    for g in range(cfg.n_dp // GROUP):
        x = jnp.concatenate(
            [
                recv[lax.rem(own + GROUP * g + b, cfg.n_dp), at : at + cfg.chunk_q]
                for b in range(GROUP)
            ],
            axis=0,
        )
        y = mm(perm_qt[...], x)
        turned = swap(y)
        for i in range(cfg.half):
            cut = slice(width * i, width * (i + 1))
            store(i, g, y[cut], turned[cut])
            store(cfg.half + i, g, turned[cut], y[cut])


def segments(cfg, tab, rows):
    inside = lax.broadcasted_iota(jnp.int32, (rows, LANES), 0)
    first, total = tab[cfg.tab_own + 1], tab[cfg.tab_own + 2]
    return jnp.where(inside < first, 0, jnp.where(inside < total, 1, 2))


def pair_loop(count, body):
    pass


def forward_kernel(cfg, tab, recv, perm_vkt, perm_qt, perm_q, vk, qs, chunks, keys, att):
    width = GROUP * BR
    own = tab[cfg.tab_own]
    segment = segments(cfg, tab, cfg.span)
    which = lane((cfg.span, LANES))
    seg_q = jnp.where(which == segment, -BIG, 0.0)
    seg_k = jnp.where((which < 3) & (which != segment), 1.0, 0.0)
    for g in range(cfg.n_dp // GROUP):
        x = jnp.concatenate(
            [
                recv[lax.rem(own + GROUP * g + b, cfg.n_dp), : cfg.chunk_vk]
                for b in range(GROUP)
            ],
            axis=0,
        )
        y = mm(perm_vkt[...], x)
        inside = slice(width * g, width * (g + 1))
        for i in range(cfg.n_ctx):
            piece = y[width * i : width * (i + 1)]
            cut = slice(cfg.span * i + width * g, cfg.span * i + width * (g + 1))
            vk[cut] = piece.astype(BF)
            keys[cut] = join(seg_k[inside], piece).astype(BF)

    def store(i, g, left, right):
        cut = slice(cfg.span * i + width * g, cfg.span * i + width * (g + 1))
        qs[cut] = join(seg_q[width * g : width * (g + 1)], right * (0.5 * HEAD_DIM**-0.5)).astype(
            BF
        )

    unpack_q(cfg, tab, recv, cfg.chunk_vk, perm_qt, store)
    tile = cfg.tile
    above = lax.broadcasted_iota(jnp.int32, (tile, tile), 1) > lax.broadcasted_iota(
        jnp.int32, (tile, tile), 0
    )

    def one(i, j, diagonal):
        qt = qs[pl.ds(pl.multiple_of(i * tile, tile), tile)]
        at = pl.ds(pl.multiple_of(j * tile, tile), tile)
        h = mm_nt(qt, keys[at])
        if diagonal:
            h = jnp.where(above, -BIG, h)
        weights = (h + h * jnp.tanh(h)).astype(BF)
        return mm(weights, vk[at])

    def outer(i, carry):
        at = pl.ds(pl.multiple_of(i * tile, tile), tile)
        att[at] = one(i, i, True)

        def inner(j, carry):
            att[at] += one(i, j, False)
            return carry

        lax.fori_loop(0, i, inner, 0)
        return carry

    lax.fori_loop(0, cfg.total // tile, outer, 0)
    emit_q(cfg, own, att, perm_q, chunks, 0, False)


def emit_q(cfg, own, source, perm_q, chunks, base, in_right):
    width = GROUP * BR
    for g in range(cfg.n_dp // GROUP):
        xl, xr = (
            jnp.concatenate(
                [
                    source[cfg.span * i + width * g : cfg.span * i + width * (g + 1)]
                    for i in range(lo, lo + cfg.half)
                ],
                axis=0,
            )
            for lo in (0, cfg.half)
        )
        both = join(swap(xl), xr) if in_right else join(xl, swap(xr))
        y = mm(perm_q[...], both.astype(BF)).astype(BF)
        for b in range(GROUP):
            chunks[lax.rem(own + GROUP * g + b, cfg.n_dp), base : base + cfg.chunk_q] = y[
                b * cfg.chunk_q : (b + 1) * cfg.chunk_q
            ]


def forward_attention(cfg, tab, recv, perms):
    return pl.pallas_call(
        functools.partial(forward_kernel, cfg),
        name="attend",
        out_shape=(
            jax.ShapeDtypeStruct((cfg.total, LANES), BF),
            jax.ShapeDtypeStruct((cfg.total, LANES), BF),
            jax.ShapeDtypeStruct((cfg.n_dp, cfg.chunk_q, LANES), BF),
        ),
        in_specs=[SMEM] + [VMEM] * 4,
        out_specs=(VMEM,) * 3,
        scratch_shapes=[
            pltpu.VMEM((cfg.total, LANES), BF),
            pltpu.VMEM((cfg.total, LANES), F32),
        ],
        compiler_params=pltpu.CompilerParams(vmem_limit_bytes=LIMIT),
    )(tab, recv, perms["vk_t"], perms["q_t"], perms["q"])


def backward_kernel(
    cfg, tab, recv, vk, qs, perm_vk, perm_qt, perm_q, chunks, keys, go, qz, dvk, dqt, dq
):
    width = GROUP * BR
    own = tab[cfg.tab_own]
    segment = segments(cfg, tab, cfg.span)
    which = lane((cfg.span, LANES))
    seg_k = jnp.where((which < 3) & (which != segment), 1.0, 0.0).astype(BF)
    zero = jnp.zeros((cfg.span, LANES), BF)
    for i in range(cfg.n_ctx):
        cut = slice(cfg.span * i, cfg.span * (i + 1))
        keys[cut] = join(seg_k, vk[cut])
        qz[cut] = join(zero, qs[cut])

    def store(i, g, left, right):
        cut = slice(cfg.span * i + width * g, cfg.span * i + width * (g + 1))
        go[cut] = join(left, jnp.zeros_like(left)).astype(BF)

    unpack_q(cfg, tab, recv, 0, perm_qt, store)
    tile = cfg.tile
    count = cfg.total // tile
    below = lax.broadcasted_iota(jnp.int32, (tile, tile), 0) > lax.broadcasted_iota(
        jnp.int32, (tile, tile), 1
    )
    dqt[...] = jnp.zeros_like(dqt)

    def outer(j, carry):
        jt = pl.ds(pl.multiple_of(j * tile, tile), tile)
        key, both = keys[jt], vk[jt]
        both_t = both.T

        def one(i, diagonal):
            it = pl.ds(pl.multiple_of(i * tile, tile), tile)
            h = mm_nt(key, qs[it])
            if diagonal:
                h = jnp.where(below, -BIG, h)
            p = 1.0 + jnp.tanh(h)
            a = h * p
            weights = a.astype(BF)
            ga = mm_nt(both, go[it])
            grad_s = (ga * p * ((2.0 * h + 1.0) - a)).astype(BF)
            dqt[:, it] += mm(both_t, grad_s)
            return mm(weights, go[it]) + mm(grad_s, qz[it])

        dvk[jt] = one(j, True)

        def inner(i, carry):
            dvk[jt] += one(i, False)
            return carry

        lax.fori_loop(j + 1, count, inner, 0)
        return carry

    lax.fori_loop(0, count, outer, 0)

    for i in range(count):
        cut = slice(tile * i, tile * (i + 1))
        dq[cut] = dqt[:, cut].T * (0.5 * HEAD_DIM**-0.5)
    for g in range(cfg.n_dp // GROUP):
        x = jnp.concatenate(
            [
                dvk[cfg.span * i + width * g : cfg.span * i + width * (g + 1)]
                for i in range(cfg.n_ctx)
            ],
            axis=0,
        )
        y = mm(perm_vk[...], x.astype(BF)).astype(BF)
        for b in range(GROUP):
            chunks[lax.rem(own + GROUP * g + b, cfg.n_dp), : cfg.chunk_vk] = y[
                b * cfg.chunk_vk : (b + 1) * cfg.chunk_vk
            ]
    emit_q(cfg, own, dq, perm_q, chunks, cfg.chunk_vk, True)


def backward_attention(cfg, tab, recv, vk, qs, perms):
    return pl.pallas_call(
        functools.partial(backward_kernel, cfg),
        name="attend_back",
        out_shape=jax.ShapeDtypeStruct((cfg.n_dp, cfg.chunk_vk + cfg.chunk_q, LANES), BF),
        in_specs=[SMEM] + [VMEM] * 6,
        out_specs=VMEM,
        scratch_shapes=[
            pltpu.VMEM((cfg.total, LANES), BF),
            pltpu.VMEM((cfg.total, LANES), BF),
            pltpu.VMEM((cfg.total, LANES), BF),
            pltpu.VMEM((cfg.total, LANES), F32),
            pltpu.VMEM((LANES, cfg.total), F32),
            pltpu.VMEM((cfg.total, LANES), F32),
        ],
        compiler_params=pltpu.CompilerParams(vmem_limit_bytes=LIMIT),
    )(tab, recv, vk, qs, perms["vk"], perms["q_t"], perms["q"])


def shards(n_dp, n_ctx, embedded, upstream, w_uvqk, w_out, lengths):
    cfg = Cfg(n_dp, n_ctx, embedded.shape[1], embedded.shape[2])
    perm_vk, perm_q = permutation(n_ctx), permutation(n_ctx // 2)
    perms = {
        "vk": jnp.asarray(perm_vk, BF),
        "vk_t": jnp.asarray(perm_vk.T, BF),
        "q": jnp.asarray(perm_q, BF),
        "q_t": jnp.asarray(perm_q.T, BF),
    }
    dp_index = lax.axis_index("dp").astype(jnp.int32).reshape(1)
    tab, pre, zmsg = pre_work(cfg, dp_index, lengths, embedded, w_uvqk)
    recv = scatter(cfg, True, 0, tab, zmsg, perms["vk"], perms["q"])
    vk, qs, chunks = forward_attention(cfg, tab, recv, perms)
    zatt = gather(cfg, False, 1, tab, chunks, perms["vk_t"], perms["q_t"])
    layer_out, zmsg2, gpu, term_out = mid_work(cfg, zatt, pre, embedded, upstream, w_out)
    recv2 = scatter(cfg, False, 2, tab, zmsg2, perms["vk"], perms["q"])
    chunks2 = backward_attention(cfg, tab, recv2, vk, qs, perms)
    zgrad = gather(cfg, True, 3, tab, chunks2, perms["vk_t"], perms["q_t"])
    gradient, grad_w, grad_out = post_work(
        cfg, 4, zgrad, gpu, pre, embedded, upstream, w_uvqk, term_out
    )
    return layer_out, gradient, grad_w, grad_out


def solution(mesh):
    return jax.shard_map(
        functools.partial(shards, mesh.shape["dp"], mesh.shape["ctx"]),
        mesh=mesh,
        in_specs=(P("ctx", "dp", None), P("ctx", "dp", None), P(), P(), P()),
        out_specs=(P("ctx", "dp", None), P("ctx", "dp", None), P("ctx", "dp"), P("ctx", "dp")),
        check_vma=False,
    )
```

```python
import functools
import math

import jax
import jax.numpy as jnp
import numpy as np
from jax import lax
from jax.experimental import pallas as pl
from jax.experimental.pallas import tpu as pltpu
from jax.sharding import PartitionSpec as P

HEAD_DIM = 64
BR = 12
SEQ_DP = 2
GROUP = 4
LANES = 128
EPS = 1e-06
BIG = 1e30
MESH = pl.DeviceIdType.MESH
BF = jnp.bfloat16
F32 = jnp.float32
VMEM = pl.BlockSpec(memory_space=pltpu.VMEM)
SMEM = pl.BlockSpec(memory_space=pltpu.SMEM)
HBM = pl.BlockSpec(memory_space=pltpu.HBM)
LIMIT = 52 * 1024 * 1024
PIECES = (3, 1, 2)


class Cfg:
    def __init__(self, n_dp, n_ctx, rows, width):
        self.n_dp = n_dp
        self.n_ctx = n_ctx
        self.rows = rows
        self.width = width
        self.blocks = rows // BR
        self.heads = n_ctx
        self.hd = self.heads * HEAD_DIM
        self.half = n_ctx // 2
        self.piece_z = rows // 2
        self.piece_c = n_ctx * BR // 2
        self.span = n_dp * BR
        self.side = math.isqrt(n_dp // 2)
        self.total = n_ctx * self.span
        self.tile = min(512, self.total // 3)
        self.tab_owner = n_dp
        self.tab_own = n_dp + self.blocks + 1


def permutation(contexts):
    size = contexts * GROUP * BR
    matrix = np.zeros((size, size), np.float32)
    for block in range(GROUP):
        for context in range(contexts):
            for row in range(BR):
                matrix[
                    (block * contexts + context) * BR + row, (context * GROUP + block) * BR + row
                ] = 1.0
    return matrix


def lane(shape):
    return lax.broadcasted_iota(jnp.int32, shape, len(shape) - 1)


def swap(tensor):
    return pltpu.roll(tensor, HEAD_DIM, 1)


def join(left, right):
    return jnp.where(lane(left.shape) < HEAD_DIM, left, right)


def mm(left, right):
    return jnp.dot(left, right, preferred_element_type=F32)


def mm_nt(left, right):
    return lax.dot_general(left, right, (((1,), (1,)), ((), ())), preferred_element_type=F32)


def layer_normalize(tensor):
    centre = jnp.mean(tensor, -1, keepdims=True)
    centred = tensor - centre
    inverse = lax.rsqrt(jnp.mean(centred * centred, -1, keepdims=True) + EPS)
    return centred * inverse, inverse


def layer_norm_backward(incoming, normal, inverse):
    first = jnp.mean(incoming, -1, keepdims=True)
    second = jnp.mean(incoming * normal, -1, keepdims=True)
    return (incoming - first - normal * second) * inverse


def silu(argument):
    return argument * jax.nn.sigmoid(argument)


def silu_grad(argument):
    sigmoid = jax.nn.sigmoid(argument)
    return sigmoid * (1.0 + argument * (1.0 - sigmoid))


def pack_rows(value):
    mid = value.shape[0] // 2
    top, low = value[:mid], value[mid:]
    return join(top, swap(low)), join(swap(top), low)


def unpack_rows(first, second):
    first, second = first.astype(F32), second.astype(F32)
    return jnp.concatenate([join(first, swap(second)), join(swap(first), second)], axis=0)


def greet(cfg, me, ctx):
    barrier = pltpu.get_barrier_semaphore()

    def along_dp(k, carry):
        pl.semaphore_signal(
            barrier, inc=1, device_id={"dp": lax.rem(me + k, cfg.n_dp)}, device_id_type=MESH
        )
        return carry

    def along_ctx(k, carry):
        pl.semaphore_signal(
            barrier, inc=1, device_id={"ctx": lax.rem(ctx + k, cfg.n_ctx)}, device_id_type=MESH
        )
        return carry

    lax.fori_loop(1, cfg.n_dp, along_dp, 0)
    lax.fori_loop(1, cfg.n_ctx, along_ctx, 0)
    return barrier, cfg.n_dp + cfg.n_ctx - 2


class Part:
    def __init__(self, ref, *prefix):
        self.ref, self.prefix = ref, prefix

    def whole(self, index):
        return (*self.prefix, *(index if isinstance(index, tuple) else (index,)))

    def at(self, index):
        return self.ref.at[self.whole(index)]

    def __getitem__(self, index):
        return self.ref[self.whole(index)]

    def __setitem__(self, index, value):
        self.ref[self.whole(index)] = value


class Exchange:
    def __init__(self, axis, count, mine, source, target, send_sem, recv_sem):
        self.axis, self.count, self.mine = axis, count, mine
        self.source, self.target = source, target
        self.send_sem, self.recv_sem = send_sem, recv_sem

    def copy(self, other, slot):
        return pltpu.make_async_remote_copy(
            src_ref=self.source.at(other),
            dst_ref=self.target.at(slot),
            send_sem=self.send_sem.at(other),
            recv_sem=self.recv_sem.at(slot),
            device_id={self.axis: other},
            device_id_type=MESH,
        )

    def each(self, act):
        def step(k, carry):
            act(lax.rem(self.mine + k, self.count))
            return carry

        lax.fori_loop(1, self.count, step, 0)

    def start(self, before=None):
        def act(other):
            if before is not None:
                before(other)
            self.copy(other, self.mine).start()

        self.each(act)

    def wait_recv(self):
        self.each(lambda other: self.copy(other, other).wait_recv())

    def wait_send(self):
        self.each(lambda other: self.copy(other, self.mine).wait_send())


def regroup_in(cfg, g, source, perm, chunks):
    half_blocks = cfg.blocks // 2
    yl, yr = (
        mm(perm[...], jnp.concatenate([source(i) for i in range(lo, lo + cfg.half)], axis=0))
        for lo in (0, cfg.half)
    )
    left = join(yl, swap(yr)).astype(BF)
    right = join(swap(yl), yr).astype(BF)
    for b in range(GROUP):
        rows = slice(b * cfg.piece_c, (b + 1) * cfg.piece_c)
        chunks[GROUP * g + b] = left[rows]
        chunks[half_blocks + GROUP * g + b] = right[rows]


def regroup_out(cfg, g, picked, perm_t, store):
    width = GROUP * BR
    yl, yr = (
        mm(
            perm_t[...],
            jnp.concatenate([picked(lo + GROUP * g + b) for b in range(GROUP)], axis=0),
        )
        for lo in (0, cfg.blocks // 2)
    )
    left = join(yl, swap(yr)).astype(BF)
    right = join(swap(yl), yr).astype(BF)
    for i in range(cfg.half):
        rows = slice(width * i, width * (i + 1))
        store(i, left[rows])
        store(cfg.half + i, right[rows])


def unstream(cfg, own, piece, perm_t, store):
    width = GROUP * BR
    for g in range(cfg.n_dp // GROUP):
        rows = [piece[lax.rem(own + GROUP * g + b, cfg.n_dp)] for b in range(GROUP)]
        straight = mm(perm_t[...], jnp.concatenate(rows, axis=0))
        turned = swap(straight)
        for i in range(cfg.half):
            cut = slice(width * i, width * (i + 1))
            for c, one, two in ((i, straight, turned), (cfg.half + i, turned, straight)):
                at = cfg.span * c + width * g
                store(slice(at, at + width), g, one[cut], two[cut])


def to_stream(cfg, source, perm, stream, in_right):
    width = GROUP * BR
    for g in range(cfg.n_dp // GROUP):
        xl, xr = (
            jnp.concatenate(
                [
                    source[cfg.span * i + width * g : cfg.span * i + width * (g + 1)]
                    for i in range(lo, lo + cfg.half)
                ],
                axis=0,
            )
            for lo in (0, cfg.half)
        )
        both = join(swap(xl), xr) if in_right else join(xl, swap(xr))
        y = mm(perm[...], both.astype(BF)).astype(BF)
        for b in range(GROUP):
            stream[GROUP * g + b] = y[b * cfg.piece_c : (b + 1) * cfg.piece_c]


def dma(*shape):
    return pltpu.SemaphoreType.DMA(shape)


def params(collective):
    return pltpu.CompilerParams(
        collective_id=collective, has_side_effects=True, vmem_limit_bytes=LIMIT
    )


def table(cfg, me, lengths, tab):
    n = cfg.n_dp
    wrap = n * cfg.blocks * n

    def owner(o, carry):
        start, own, own_first, own_total, owners = carry
        first = lengths[SEQ_DP * o]
        total = first + lengths[SEQ_DP * o + 1]
        block = start + lax.rem(me - start + wrap, n)
        tab[o] = jnp.clip((block - me) // n, 0, cfg.blocks - 1)
        mine = o == me
        own = jnp.where(mine, start, own)
        own_first = jnp.where(mine, first, own_first)
        own_total = jnp.where(mine, total, own_total)
        owners = tuple(
            count + jnp.where(start <= me + n * j, 1, 0) for j, count in enumerate(owners)
        )
        return start + total, own, own_first, own_total, owners

    zero = jnp.int32(0)
    _, own, first, total, owners = lax.fori_loop(
        0, n, owner, (zero, zero, zero, zero, (jnp.int32(-1),) * cfg.blocks)
    )
    for j, count in enumerate(owners):
        tab[cfg.tab_owner + j] = count
    tab[cfg.tab_own] = lax.rem(own, n)
    tab[cfg.tab_own + 1] = first * BR
    tab[cfg.tab_own + 2] = total * BR


def segments(cfg, tab):
    shape = (cfg.span, LANES)
    inside = lax.broadcasted_iota(jnp.int32, shape, 0)
    first, total = tab[cfg.tab_own + 1], tab[cfg.tab_own + 2]
    segment = jnp.where(inside < first, 0, jnp.where(inside < total, 1, 2))
    which = lane(shape)
    seg_q = jnp.where(which == segment, -BIG, 0.0)
    seg_k = jnp.where((which < 3) & (which != segment), 1.0, 0.0)
    return seg_q, seg_k


def pack_out_term(cfg, term, t_out):
    side = cfg.side
    for tile in range(cfg.width // LANES):
        straight = term[:, tile * LANES : (tile + 1) * LANES]
        turned = swap(straight)
        for c in range(cfg.n_ctx):
            at = c * HEAD_DIM
            mid, end = at + HEAD_DIM // 2, at + HEAD_DIM
            pieces = (
                join(straight[at:mid], turned[mid:end]),
                join(turned[at:mid], straight[mid:end]),
            )
            for odd, piece in enumerate(pieces):
                s, t = divmod(2 * tile + odd, side)
                place = (0, t, s) if c < cfg.half else (1, (s + t) % side, s)
                t_out[(*place, c % cfg.half)] = piece.astype(BF)


def attend(cfg, vk, qs, keys, att):
    tile = cfg.tile
    above = lax.broadcasted_iota(jnp.int32, (tile, tile), 1) > lax.broadcasted_iota(
        jnp.int32, (tile, tile), 0
    )

    def one(i, j):
        at = slice(j * tile, (j + 1) * tile)
        h = mm_nt(qs[i * tile : (i + 1) * tile], keys[at])
        if i == j:
            h = jnp.where(above, -BIG, h)
        weights = (h + h * jnp.tanh(h)).astype(BF)
        return mm(weights, vk[at])

    for i in range(cfg.total // tile):
        total = one(i, i)
        for j in range(i):
            total = total + one(i, j)
        att[i * tile : (i + 1) * tile] = total


def attend_back(cfg, vk, qs, keys, go, qz, dvk, dqt):
    tile = cfg.tile
    count = cfg.total // tile
    below = lax.broadcasted_iota(jnp.int32, (tile, tile), 0) > lax.broadcasted_iota(
        jnp.int32, (tile, tile), 1
    )

    for j in range(count):
        jt = slice(j * tile, (j + 1) * tile)
        key, both = keys[jt], vk[jt]
        both_t = both.T
        total = None
        for i in range(j, count):
            it = slice(i * tile, (i + 1) * tile)
            h = mm_nt(key, qs[it])
            if i == j:
                h = jnp.where(below, -BIG, h)
            p = 1.0 + jnp.tanh(h)
            a = h * p
            ga = mm_nt(both, go[it])
            grad_s = (ga * p * ((2.0 * h + 1.0) - a)).astype(BF)
            step = mm(both_t, grad_s)
            dqt[:, it] = step if j == 0 else dqt[:, it] + step
            step = mm(
                jnp.concatenate([a.astype(BF), grad_s], axis=1),
                jnp.concatenate([go[it], qz[it]], axis=0),
            )
            total = step if total is None else total + step
        dvk[jt] = total


def scratch(cfg):
    side, half, block, count = cfg.side, cfg.half, cfg.width // cfg.n_ctx, len(PIECES)
    deep, line, tiles, groups = block + 32, 2 * cfg.side, cfg.hd // LANES, cfg.blocks // 2 // GROUP
    chunk = (cfg.piece_c, LANES)
    zpart = (cfg.piece_z, LANES)
    zhalf = (groups, cfg.n_ctx, cfg.piece_z // groups, LANES)
    stream = (cfg.total, LANES)
    buffers = {
        "xv": ((cfg.rows, cfg.width), BF),
        "upv": ((cfg.rows, cfg.width), BF),
        "wv": ((cfg.width, 4 * cfg.hd), BF),
        "wov": ((cfg.hd, cfg.width), BF),
        "pre": ((cfg.rows, 4 * cfg.hd), F32),
        "normed": ((2, cfg.rows, cfg.width // 2), BF),
        "zsend0": ((count, cfg.n_ctx, *zpart), BF),
        "zland0": ((count, cfg.n_ctx, *zpart), BF),
        "chunks": ((count, cfg.blocks, *chunk), BF),
        "send0": ((count, cfg.n_dp, *chunk), BF),
        "land00": ((cfg.n_dp, *chunk), BF),
        "land01": ((cfg.n_dp, *chunk), BF),
        "land02": ((cfg.n_dp, *chunk), BF),
        "vk": (stream, BF),
        "qs": (stream, BF),
        "keys": (stream, BF),
        "qz": (stream, BF),
        "go": (stream, BF),
        "rows32": (stream, F32),
        "dqt": ((LANES, cfg.total), F32),
        "stream": ((count, cfg.n_dp, *chunk), BF),
        "send1": ((cfg.n_dp, *chunk), BF),
        "land1": ((cfg.n_dp, *chunk), BF),
        "zsend1": (zhalf, BF),
        "zland1": (zhalf, BF),
        "zsend2": (zhalf, BF),
        "zland2": (zhalf, BF),
        "chunks2": ((cfg.blocks, *chunk), BF),
        "send2": ((cfg.n_dp, *chunk), BF),
        "land2": ((cfg.n_dp, *chunk), BF),
        "att_norm": ((cfg.rows, cfg.hd), F32),
        "gpu": ((tiles, cfg.rows, LANES), BF),
        "t_out": ((2, side, side, half, 32, LANES), BF),
        "send3": ((count, cfg.n_dp, *chunk), BF),
        "land30": ((cfg.n_dp, *chunk), BF),
        "land31": ((cfg.n_dp, *chunk), BF),
        "land32": ((cfg.n_dp, *chunk), BF),
        "zsend3": ((count, cfg.n_ctx, *zpart), BF),
        "zland3": ((count, cfg.n_ctx, *zpart), BF),
        "gp": ((cfg.rows, 4 * cfg.hd), BF),
        "gpt": ((count, tiles, cfg.rows, LANES), BF),
        "lrecv": ((line, cfg.rows, cfg.width // 2), BF),
        "grecv": ((side, line, cfg.rows, LANES), BF),
        "trecv": ((line, side, half, 32, LANES), BF),
        "normal_t": ((cfg.width // 2, line * cfg.rows), BF),
        "bsend": ((side, half, deep, LANES), BF),
        "brecv": ((side, half, deep, LANES), BF),
        "acc": ((half, deep, LANES), F32),
        "fsend": ((half, 2, deep // 2, LANES), BF),
        "frecv": ((cfg.n_ctx, deep // 2, LANES), BF),
    }
    sems = {
        "in": (7,),
        "ls": (6, line - 1),
        "lr": (6, line),
        "bs": (side,),
        "br": (side,),
        "fs": (half, 2),
        "fr": (cfg.n_ctx,),
    }
    for name, size, parts in (
        ("z0", cfg.n_ctx, count),
        ("x0", cfg.n_dp, count),
        ("x1", cfg.n_dp, 1),
        ("z1", cfg.n_ctx, groups),
        ("z2", cfg.n_ctx, groups),
        ("x2", cfg.n_dp, 1),
        ("x3", cfg.n_dp, count),
        ("z3", cfg.n_ctx, count),
    ):
        sems[name + "s"] = (parts, size)
        sems[name + "r"] = (parts, size)
    shapes = {name: pltpu.VMEM(*spec) for name, spec in buffers.items()}
    shapes["tab"] = pltpu.SMEM((cfg.tab_own + 3,), jnp.int32)
    shapes.update({name: dma(*size) for name, size in sems.items()})
    return shapes


def layer_kernel(cfg, names, *refs):
    r = dict(zip(names, refs))
    perm, perm_t, tab = r["perm"], r["perm_t"], r["tab"]
    hd, rows, side, half, n, n_ctx = cfg.hd, cfg.rows, cfg.side, cfg.half, cfg.n_dp, cfg.n_ctx
    count, width, groups = len(PIECES), GROUP * BR, cfg.blocks // 2 // GROUP
    me, ctx = lax.axis_index("dp"), lax.axis_index("ctx")
    core = lax.rem(me, 2)
    other = 1 - core
    chip_x, chip_y = me // (2 * side), lax.rem(me // 2, side)
    a_own = chip_x * other + chip_y * core
    b_own = chip_y * other + chip_x * core
    along_a = 2 * side - core * (2 * side - 2)
    along_b = 2 + core * (2 * side - 2)
    home = ctx // half
    m_own = 2 * a_own + core

    def device(a, b):
        return a * along_a + b * along_b + core

    adder = (chip_y * side + lax.rem(chip_x + chip_y, side)) * 2 + home
    s_own = lax.rem(chip_y - chip_x + side, side)
    owner = (s_own * side + chip_x) * 2

    def load(number, source, target):
        return pltpu.make_async_copy(source, target, r["in"].at[number])

    loads = [load(0, r["x"].at[0], r["xv"])]
    for i, s in enumerate((*PIECES, 0)):
        cut = pl.ds(s * hd, hd)
        loads.append(load(1 + i, r["w"].at[:, cut], r["wv"].at[:, cut]))
    loads.append(load(5, r["up"].at[0], r["upv"]))
    loads.append(load(6, r["w_out"], r["wov"]))
    for item in loads:
        item.start()

    barrier, greetings = greet(cfg, me, ctx)
    for z in range(n_ctx):

        @pl.when(jnp.logical_or(z != ctx, adder != me))
        def _():
            pl.semaphore_signal(
                barrier, inc=1, device_id={"dp": adder, "ctx": z}, device_id_type=MESH
            )

    table(cfg, me, r["lengths"], tab)
    own = tab[cfg.tab_own]

    def moves(axis, source, target, sems, parts):
        size, mine = (n, me) if axis == "dp" else (n_ctx, ctx)
        return [
            Exchange(
                axis,
                size,
                mine,
                source(t),
                target(t),
                Part(r[sems + "s"], t),
                Part(r[sems + "r"], t),
            )
            for t in range(parts)
        ]

    def part(name):
        return lambda t: Part(r[name], t)

    z0 = moves("ctx", part("zsend0"), part("zland0"), "z0", count)
    x0 = moves("dp", part("send0"), lambda t: Part(r["land0" + str(t)]), "x0", count)
    x1 = moves("dp", lambda t: Part(r["send1"]), lambda t: Part(r["land1"]), "x1", 1)[0]
    z1 = moves("ctx", part("zsend1"), part("zland1"), "z1", groups)
    z2 = moves("ctx", part("zsend2"), part("zland2"), "z2", groups)
    x2 = moves("dp", lambda t: Part(r["send2"]), lambda t: Part(r["land2"]), "x2", 1)[0]
    x3 = moves("dp", part("send3"), lambda t: Part(r["land3" + str(t)]), "x3", count)
    z3 = moves("ctx", part("zsend3"), part("zland3"), "z3", count)

    xv, upv, wv, wov, pre = r["xv"], r["upv"], r["wv"], r["wov"], r["pre"]
    normed_ref = r["normed"]
    loads[0].wait()
    normal, inverse = layer_normalize(xv[...].astype(F32))
    normed = normal.astype(BF)
    normed_ref[0] = normed[:, : cfg.width // 2]
    normed_ref[1] = normed[:, cfg.width // 2 :]
    zsend0, zland0, chunks, send0 = r["zsend0"], r["zland0"], r["chunks"], r["send0"]
    step = min(256, hd)

    def section(number, t):
        for base in range(0, hd, step):
            at = number * hd + base
            value = mm(normed, wv[:, at : at + step])
            pre[:, at : at + step] = value
            if t is None:
                continue
            act = silu(value)
            for tile in range(step // LANES):
                head = (base + tile * LANES) // HEAD_DIM
                one, two = pack_rows(act[:, tile * LANES : (tile + 1) * LANES])
                zsend0[t, head] = one.astype(BF)
                zsend0[t, head + 1] = two.astype(BF)

    for t, number in enumerate(PIECES):
        loads[1 + t].wait()
        section(number, t)
        if t == 0:
            pl.semaphore_wait(
                barrier, greetings + n_ctx - jnp.where(adder == me, 1, 0).astype(jnp.int32)
            )
        z0[t].start()
        zland0[t, ctx] = zsend0[t, ctx]
    loads[4].wait()
    section(0, None)
    loads[5].wait()
    loads[6].wait()
    back_gated = mm_nt(upv[...], wov[...])
    gate = silu(pre[:, :hd]).astype(BF).astype(F32)
    for t in range(count):
        z0[t].wait_recv()
        for g in range(groups):
            cut = slice(width * g, width * (g + 1))
            regroup_in(
                cfg, g, lambda i, t=t, cut=cut: zland0[t, i, cut], perm, Part(chunks, t)
            )

        def fill(device_at, t=t):
            send0[t, device_at] = chunks[t, tab[device_at]]

        x0[t].start(fill)
        r["land0" + str(t)][me] = chunks[t, tab[me]]

    vk, qs, keys, qz, go = r["vk"], r["qs"], r["keys"], r["qz"], r["go"]
    seg_q, seg_k = segments(cfg, tab)

    def store_k(cut, g, straight, turned):
        keys[cut] = join(seg_k[width * g : width * (g + 1)], turned).astype(BF)

    def store_v(cut, g, straight, turned):
        vk[cut] = join(straight.astype(BF), keys[cut])

    def store_q(cut, g, straight, turned):
        value = turned * (0.5 * HEAD_DIM**-0.5)
        qs[cut] = join(seg_q[width * g : width * (g + 1)], value).astype(BF)
        qz[cut] = join(jnp.zeros_like(value), value).astype(BF)

    for t, store in enumerate((store_k, store_v, store_q)):
        x0[t].wait_recv()
        unstream(cfg, own, r["land0" + str(t)], perm_t, store)

    gpu, t_out, gpt = r["gpu"], r["t_out"], r["gpt"]
    lrecv, grecv, trecv = r["lrecv"], r["grecv"], r["trecv"]
    def tile_of(a, kind, s):
        return lax.rem(a - s * kind + side, side)

    def line_copy(what, j):
        if j < side - 1:
            kind, a = 0, lax.rem(chip_x + 1 + j, side)
            target, slot = (a * side + chip_y) * 2, 2 * chip_x + core
        elif j < 2 * (side - 1):
            kind, a = 1, lax.rem(chip_y + 1 + j - (side - 1), side)
            target, slot = (chip_x * side + a) * 2 + 1, 2 * chip_y + core
        else:
            kind, a = other, b_own
            target, slot = me + 1 - 2 * core, 2 * b_own + core
        if what == 4:
            source, target_ref = normed_ref.at[kind], lrecv.at[slot]
        elif what == 5:
            source, target_ref = t_out.at[kind, a], trecv.at[slot]
        elif what == 0:
            source, target_ref = gpu.at[tile_of(a, kind, 0)], grecv.at[0, slot]
        else:
            source, target_ref = gpt.at[what - 1, tile_of(a, kind, what)], grecv.at[what, slot]
        return pltpu.make_async_remote_copy(
            src_ref=source,
            dst_ref=target_ref,
            send_sem=r["ls"].at[what, j],
            recv_sem=r["lr"].at[what, slot],
            device_id={"dp": target},
            device_id_type=MESH,
        )

    def line_start(what):
        for j in range(2 * side - 1):
            line_copy(what, j).start()

    def line_wait(what):
        ref = {4: lrecv, 5: trecv}.get(what, None)
        for i in range(1, 2 * side):
            slot = lax.rem(m_own + i, 2 * side)
            place = grecv.at[what, slot] if ref is None else ref.at[slot]
            pltpu.make_async_remote_copy(
                src_ref=place,
                dst_ref=place,
                send_sem=r["ls"].at[what, 0],
                recv_sem=r["lr"].at[what, slot],
                device_id={"dp": me + 1 - 2 * core},
                device_id_type=MESH,
            ).wait_recv()


    line_start(4)
    rows32 = r["rows32"]
    attend(cfg, vk, qs, keys, rows32)

    stream, send1, land1 = r["stream"], r["send1"], r["land1"]
    to_stream(cfg, rows32, perm, Part(stream, 0), False)

    def place(t, device_at):
        return stream[t, lax.rem(device_at - own + n, n)]

    def fill1(device_at):
        send1[device_at] = place(0, device_at)

    x1.start(fill1)
    land1[me] = place(0, me)
    backward_gate = back_gated * gate
    lrecv[m_own] = normed_ref[core]
    line_wait(4)
    normal_t = r["normal_t"]
    for i in range(side):
        pair = jnp.concatenate([lrecv[2 * i], lrecv[2 * i + 1]], axis=0)
        normal_t[:, 2 * rows * i : 2 * rows * (i + 1)] = pair.T

    x1.wait_recv()
    zsend1, zland1, zsend2, zland2 = r["zsend1"], r["zland1"], r["zsend2"], r["zland2"]
    for g in range(groups):

        def store1(i, value, g=g):
            zsend1[g, i] = value

        regroup_out(cfg, g, lambda block: land1[tab[cfg.tab_owner + block]], perm_t, store1)
        z1[g].start()
        zland1[g, ctx] = zsend1[g, ctx]
    att_norm = r["att_norm"]
    mid = rows // 2
    for g in range(groups):
        z1[g].wait_recv()
        att_rows = jnp.concatenate(
            [
                unpack_rows(zland1[g, head], zland1[g, head + 1])
                for head in range(0, cfg.heads, 2)
            ],
            axis=1,
        )
        norm_part, att_inverse = layer_normalize(att_rows)
        top, low = slice(width * g, width * (g + 1)), slice(mid + width * g, mid + width * (g + 1))
        att_norm[top] = norm_part[:width]
        att_norm[low] = norm_part[width:]
        incoming = jnp.concatenate([backward_gate[top], backward_gate[low]], axis=0)
        grad_att = layer_norm_backward(incoming, norm_part, att_inverse)
        for tile in range(hd // LANES):
            one, two = pack_rows(grad_att[:, tile * LANES : (tile + 1) * LANES])
            zsend2[g, 2 * tile] = one.astype(BF)
            zsend2[g, 2 * tile + 1] = two.astype(BF)
        z2[g].start()
        zland2[g, ctx] = zsend2[g, ctx]

    gated = (att_norm[...] * gate).astype(BF)
    r["out"][0] = (xv[...].astype(F32) + mm(gated, wov[...])).astype(BF)
    chunks2, send2, land2 = r["chunks2"], r["send2"], r["land2"]
    for g in range(groups):
        z2[g].wait_recv()
        regroup_in(cfg, g, lambda i, g=g: zland2[g, i], perm, chunks2)

    def fill2(device_at):
        send2[device_at] = chunks2[tab[device_at]]

    x2.start(fill2)
    land2[me] = chunks2[tab[me]]
    gp = r["gp"]
    grad_u = (back_gated * att_norm[...] * silu_grad(pre[:, :hd])).astype(BF)
    gp[:, :hd] = grad_u
    for tile in range(hd // LANES):
        gpu[tile] = grad_u[:, tile * LANES : (tile + 1) * LANES]
    pack_out_term(
        cfg,
        lax.dot_general(gated, upv[...], (((0,), (0,)), ((), ())), preferred_element_type=F32),
        t_out,
    )
    x2.wait_recv()

    def store_go(cut, g, straight, turned):
        go[cut] = join(straight, jnp.zeros_like(straight)).astype(BF)

    line_start(0)
    line_start(5)
    unstream(cfg, own, land2, perm_t, store_go)
    dqt = r["dqt"]
    attend_back(cfg, vk, qs, keys, go, qz, rows32, dqt)

    send3, zsend3, zland3 = r["send3"], r["zsend3"], r["zland3"]
    for t in range(count):
        if t == 2:
            for i in range(cfg.total // cfg.tile):
                cut = slice(cfg.tile * i, cfg.tile * (i + 1))
                rows32[cut] = dqt[:, cut].T * (0.5 * HEAD_DIM**-0.5)
        to_stream(cfg, rows32, perm, Part(stream, t), t != 1)

        def fill3(device_at, t=t):
            send3[t, device_at] = place(t, device_at)

        x3[t].start(fill3)
        r["land3" + str(t)][me] = place(t, me)

    send_b, recv_b, acc = r["bsend"], r["brecv"], r["acc"]
    block = cfg.width // n_ctx
    grecv[0, m_own] = gpu[tile_of(a_own, core, 0)]
    trecv[m_own] = t_out[core, a_own]
    line_wait(0)
    line_wait(5)

    def add_copy(s):
        b = lax.rem(a_own + s * (1 - 2 * core) + side, side)
        slot = lax.rem(b_own - b + 2 * side - 1, side)
        return b == b_own, pltpu.make_async_remote_copy(
            src_ref=send_b.at[s],
            dst_ref=recv_b.at[slot],
            send_sem=r["bs"].at[s],
            recv_sem=r["br"].at[slot],
            device_id={"dp": device(a_own, b)},
            device_id_type=MESH,
        )

    def add_section(s):
        value = mm(normal_t[...], grecv[s].reshape(2 * side * rows, LANES))
        value = value.reshape(half, block, LANES)
        low = trecv[0, s].astype(F32)
        for m in range(1, 2 * side):
            low = low + trecv[m, s].astype(F32)
        mine, copy = add_copy(s)

        @pl.when(mine)
        def _():
            acc[:, :block] = value
            acc[:, block:] = low

        @pl.when(jnp.logical_not(mine))
        def _():
            send_b[s, :, :block] = value.astype(BF)
            send_b[s, :, block:] = low.astype(BF)
            copy.start()

    add_section(0)
    for t in range(count):
        x3[t].wait_recv()
        land = r["land3" + str(t)]
        for g in range(groups):

            def store3(i, value, t=t, g=g):
                zsend3[t, i, width * g : width * (g + 1)] = value

            regroup_out(
                cfg, g, lambda b, land=land: land[tab[cfg.tab_owner + b]], perm_t, store3
            )
        z3[t].start()
        zland3[t, ctx] = zsend3[t, ctx]

    def give_section(t):
        s = PIECES[t]
        z3[t].wait_recv()
        for head in range(0, cfg.heads, 2):
            tile = head // 2
            at = s * hd + tile * LANES
            cut = slice(at, at + LANES)
            value = unpack_rows(zland3[t, head], zland3[t, head + 1])
            value = (value * silu_grad(pre[:, cut])).astype(BF)
            gp[:, cut] = value
            gpt[s - 1, tile] = value
        line_start(s)
        grecv[s, m_own] = gpt[s - 1, tile_of(a_own, core, s)]

    give_section(0)
    give_section(1)
    line_wait(PIECES[0])
    add_section(PIECES[0])
    give_section(2)
    line_wait(PIECES[1])
    add_section(PIECES[1])

    back = mm_nt(gp[...], wv[...])
    r["gradient"][0] = (
        upv[...].astype(F32) + layer_norm_backward(back, normal, inverse)
    ).astype(BF)
    line_wait(PIECES[2])
    add_section(PIECES[2])

    for slot in range(side - 1):
        pltpu.make_async_remote_copy(
            src_ref=send_b.at[0],
            dst_ref=recv_b.at[slot],
            send_sem=r["bs"].at[0],
            recv_sem=r["br"].at[slot],
            device_id={"dp": me + 1 - 2 * core},
            device_id_type=MESH,
        ).wait_recv()
    total = acc[...]
    for slot in range(side - 1):
        total = total + recv_b[slot].astype(F32)

    fsend, frecv = r["fsend"], r["frecv"]
    quarter = lax.rem(lane((16, LANES)), HEAD_DIM) < 32
    for h in range(half):
        top, low = total[h, : block // 2], total[h, block // 2 : block]
        u, v = total[h, block : block + 16], total[h, block + 16 :]
        fsend[h, 0, : block // 2] = join(top, swap(low)).astype(BF)
        fsend[h, 1, : block // 2] = join(swap(top), low).astype(BF)
        fsend[h, 0, block // 2 :] = jnp.where(quarter, u, pltpu.roll(v, 32, 1)).astype(BF)
        fsend[h, 1, block // 2 :] = jnp.where(quarter, pltpu.roll(u, 96, 1), v).astype(BF)

    def last_copy(h, kind):
        return pltpu.make_async_remote_copy(
            src_ref=fsend.at[h, kind],
            dst_ref=frecv.at[ctx],
            send_sem=r["fs"].at[h, kind],
            recv_sem=r["fr"].at[ctx],
            device_id={"dp": owner + kind, "ctx": half * core + h},
            device_id_type=MESH,
        )

    def stays(h, kind):
        return jnp.logical_and(half * core + h == ctx, owner + kind == me)

    for h in range(half):
        for kind in range(2):

            @pl.when(stays(h, kind))
            def _():
                frecv[ctx] = fsend[h, kind]

            @pl.when(jnp.logical_not(stays(h, kind)))
            def _():
                last_copy(h, kind).start()

    for z in range(n_ctx):

        @pl.when(jnp.logical_or(z != ctx, adder != me))
        def _():
            pltpu.make_async_remote_copy(
                src_ref=fsend.at[0, 0],
                dst_ref=frecv.at[z],
                send_sem=r["fs"].at[0, 0],
                recv_sem=r["fr"].at[z],
                device_id={"dp": me + 1 - 2 * core},
                device_id_type=MESH,
            ).wait_recv()

    total = frecv[0].astype(F32)
    for z in range(1, n_ctx):
        total = total + frecv[z].astype(F32)
    r["last"][...] = total * (rows * n * n_ctx) ** -0.5

    for move in (*z0, *x0, x1, *z1, *z2, x2, *x3, *z3):
        move.wait_send()
    for what in range(6):
        for j in range(2 * side - 1):
            line_copy(what, j).wait_send()
    for s in range(side):
        mine, copy = add_copy(s)

        @pl.when(jnp.logical_not(mine))
        def _():
            copy.wait_send()

    for h in range(half):
        for kind in range(2):

            @pl.when(jnp.logical_not(stays(h, kind)))
            def _():
                last_copy(h, kind).wait_send()


def layer(cfg, lengths, x, up, w, w_out, perm, perm_t):
    block = cfg.width // cfg.n_ctx
    inputs = {
        "lengths": SMEM,
        "x": HBM,
        "up": HBM,
        "w": HBM,
        "w_out": HBM,
        "perm": VMEM,
        "perm_t": VMEM,
    }
    outputs = {
        "out": jax.ShapeDtypeStruct(x.shape, BF),
        "gradient": jax.ShapeDtypeStruct(x.shape, BF),
        "last": jax.ShapeDtypeStruct((block // 2 + 16, LANES), F32),
    }
    shapes = scratch(cfg)
    return pl.pallas_call(
        functools.partial(layer_kernel, cfg, [*inputs, *outputs, *shapes]),
        name="layer",
        out_shape=tuple(outputs.values()),
        in_specs=list(inputs.values()),
        out_specs=(VMEM,) * len(outputs),
        scratch_shapes=list(shapes.values()),
        compiler_params=params(0),
    )(lengths, x, up, w, w_out, perm, perm_t)


def finish_kernel(half_block, last, gw, go):
    front, low = last[:half_block].T, last[half_block:].T
    gw[...] = jnp.concatenate([front[:HEAD_DIM], front[HEAD_DIM:]], axis=1)
    go[...] = jnp.concatenate([low[32 * i : 32 * (i + 1)] for i in range(4)], axis=1)


def finish(cfg, last):
    block = cfg.width // cfg.n_ctx
    return pl.pallas_call(
        functools.partial(finish_kernel, block // 2),
        name="finish",
        out_shape=(
            jax.ShapeDtypeStruct((HEAD_DIM, block), F32),
            jax.ShapeDtypeStruct((32, HEAD_DIM), F32),
        ),
        in_specs=[VMEM],
        out_specs=(VMEM, VMEM),
    )(last)


def shards(n_dp, n_ctx, embedded, upstream, w_uvqk, w_out, lengths):
    cfg = Cfg(n_dp, n_ctx, embedded.shape[1], embedded.shape[2])
    matrix = permutation(cfg.half)
    perm, perm_t = jnp.asarray(matrix, BF), jnp.asarray(matrix.T, BF)
    out, gradient, last = layer(cfg, lengths, embedded, upstream, w_uvqk, w_out, perm, perm_t)
    grad_w, grad_out = finish(cfg, last)
    return out, gradient, grad_w.T, grad_out.T


def solution(mesh):
    return jax.shard_map(
        functools.partial(shards, mesh.shape["dp"], mesh.shape["ctx"]),
        mesh=mesh,
        in_specs=(P("ctx", "dp", None), P("ctx", "dp", None), P(), P(), P()),
        out_specs=(P("ctx", "dp", None), P("ctx", "dp", None), P("ctx", "dp"), P("ctx", "dp")),
        check_vma=False,
    )
```

```python
import functools
import math

import jax
import jax.numpy as jnp
import numpy as np
from jax import lax
from jax.experimental import pallas as pl
from jax.experimental.pallas import tpu as pltpu
from jax.sharding import PartitionSpec as P

HEAD_DIM = 64
BR = 12
SEQ_DP = 2
GROUP = 4
LANES = 128
EPS = 1e-06
BIG = 1e30
MESH = pl.DeviceIdType.MESH
BF = jnp.bfloat16
F32 = jnp.float32
VMEM = pl.BlockSpec(memory_space=pltpu.VMEM)
SMEM = pl.BlockSpec(memory_space=pltpu.SMEM)
HBM = pl.BlockSpec(memory_space=pltpu.HBM)
LIMIT = 62 * 1024 * 1024
PIECES = 3
OUT = (3, 2, 1)
EARLY = 12
EARLY_BACK = (6, 4, 2, 2)
BACK = (3, 1, 2)


class Cfg:
    def __init__(self, n_dp, n_ctx, rows, width):
        self.n_dp = n_dp
        self.n_ctx = n_ctx
        self.rows = rows
        self.width = width
        self.blocks = rows // BR
        self.heads = n_ctx
        self.hd = self.heads * HEAD_DIM
        self.half = n_ctx // 2
        self.piece_z = rows // 2
        self.piece_c = n_ctx * BR // 2
        self.span = n_dp * BR
        self.side = math.isqrt(n_dp // 2)
        self.total = n_ctx * self.span
        self.tile = min(512, self.total // 3)
        self.tab_owner = n_dp
        self.tab_own = n_dp + self.blocks + 1


def permutation(contexts):
    size = contexts * GROUP * BR
    matrix = np.zeros((size, size), np.float32)
    for block in range(GROUP):
        for context in range(contexts):
            for row in range(BR):
                matrix[
                    (block * contexts + context) * BR + row, (context * GROUP + block) * BR + row
                ] = 1.0
    return matrix


def lane(shape):
    return lax.broadcasted_iota(jnp.int32, shape, len(shape) - 1)


def swap(tensor):
    return pltpu.roll(tensor, HEAD_DIM, 1)


def join(left, right):
    return jnp.where(lane(left.shape) < HEAD_DIM, left, right)


def mm(left, right):
    return jnp.dot(left, right, preferred_element_type=F32)


def mm_nt(left, right):
    return lax.dot_general(left, right, (((1,), (1,)), ((), ())), preferred_element_type=F32)


def layer_normalize(tensor):
    centre = jnp.mean(tensor, -1, keepdims=True)
    centred = tensor - centre
    inverse = lax.rsqrt(jnp.mean(centred * centred, -1, keepdims=True) + EPS)
    return centred * inverse, inverse


def layer_norm_backward(incoming, normal, inverse):
    first = jnp.mean(incoming, -1, keepdims=True)
    second = jnp.mean(incoming * normal, -1, keepdims=True)
    return (incoming - first - normal * second) * inverse


def silu(argument):
    return argument * jax.nn.sigmoid(argument)


def silu_grad(argument):
    sigmoid = jax.nn.sigmoid(argument)
    return sigmoid * (1.0 + argument * (1.0 - sigmoid))


def pack_rows(value):
    mid = value.shape[0] // 2
    top, low = value[:mid], value[mid:]
    return join(top, swap(low)), join(swap(top), low)


def unpack_rows(first, second):
    first, second = first.astype(F32), second.astype(F32)
    return jnp.concatenate([join(first, swap(second)), join(swap(first), second)], axis=0)


def greet(cfg, me, ctx):
    barrier = pltpu.get_barrier_semaphore()

    def along_dp(k, carry):
        pl.semaphore_signal(
            barrier, inc=1, device_id={"dp": lax.rem(me + k, cfg.n_dp)}, device_id_type=MESH
        )
        return carry

    def along_ctx(k, carry):
        pl.semaphore_signal(
            barrier, inc=1, device_id={"ctx": lax.rem(ctx + k, cfg.n_ctx)}, device_id_type=MESH
        )
        return carry

    lax.fori_loop(1, cfg.n_dp, along_dp, 0)
    lax.fori_loop(1, cfg.n_ctx, along_ctx, 0)
    return barrier, cfg.n_dp + cfg.n_ctx - 2


class Part:
    def __init__(self, ref, *prefix):
        self.ref, self.prefix = ref, prefix

    def whole(self, index):
        return (*self.prefix, *(index if isinstance(index, tuple) else (index,)))

    def at(self, index):
        return self.ref.at[self.whole(index)]

    def __getitem__(self, index):
        return self.ref[self.whole(index)]

    def __setitem__(self, index, value):
        self.ref[self.whole(index)] = value


class Exchange:
    def __init__(self, axis, count, mine, source, target, send_sem, recv_sem):
        self.axis, self.count, self.mine = axis, count, mine
        self.source, self.target = source, target
        self.send_sem, self.recv_sem = send_sem, recv_sem

    def copy(self, other, slot):
        return pltpu.make_async_remote_copy(
            src_ref=self.source.at(other),
            dst_ref=self.target.at(slot),
            send_sem=self.send_sem.at(other),
            recv_sem=self.recv_sem.at(slot),
            device_id={self.axis: other},
            device_id_type=MESH,
        )

    def each(self, act):
        def step(k, carry):
            act(lax.rem(self.mine + k, self.count))
            return carry

        lax.fori_loop(1, self.count, step, 0)

    def start(self, before=None):
        def act(other):
            if before is not None:
                before(other)
            self.copy(other, self.mine).start()

        self.each(act)

    def wait_recv(self):
        self.each(lambda other: self.copy(other, other).wait_recv())

    def wait_send(self):
        self.each(lambda other: self.copy(other, self.mine).wait_send())


def regroup_in(cfg, g, source, perm, chunks):
    half_blocks = cfg.blocks // 2
    yl, yr = (
        mm(perm[...], jnp.concatenate([source(i) for i in range(lo, lo + cfg.half)], axis=0))
        for lo in (0, cfg.half)
    )
    left = join(yl, swap(yr)).astype(BF)
    right = join(swap(yl), yr).astype(BF)
    for b in range(GROUP):
        rows = slice(b * cfg.piece_c, (b + 1) * cfg.piece_c)
        chunks[GROUP * g + b] = left[rows]
        chunks[half_blocks + GROUP * g + b] = right[rows]


def regroup_out(cfg, g, picked, perm_t, store):
    width = GROUP * BR
    yl, yr = (
        mm(
            perm_t[...],
            jnp.concatenate([picked(lo + GROUP * g + b) for b in range(GROUP)], axis=0),
        )
        for lo in (0, cfg.blocks // 2)
    )
    left = join(yl, swap(yr)).astype(BF)
    right = join(swap(yl), yr).astype(BF)
    for i in range(cfg.half):
        rows = slice(width * i, width * (i + 1))
        store(i, left[rows])
        store(cfg.half + i, right[rows])


def unstream(cfg, own, piece, perm_t, store):
    width = GROUP * BR
    for g in range(cfg.n_dp // GROUP):
        rows = [piece[lax.rem(own + GROUP * g + b, cfg.n_dp)] for b in range(GROUP)]
        straight = mm(perm_t[...], jnp.concatenate(rows, axis=0))
        turned = swap(straight)
        for i in range(cfg.half):
            cut = slice(width * i, width * (i + 1))
            for c, one, two in ((i, straight, turned), (cfg.half + i, turned, straight)):
                at = cfg.span * c + width * g
                store(slice(at, at + width), g, one[cut], two[cut])


def to_stream(cfg, source, perm, stream, in_right):
    width = GROUP * BR
    for g in range(cfg.n_dp // GROUP):
        xl, xr = (
            jnp.concatenate(
                [
                    source[cfg.span * i + width * g : cfg.span * i + width * (g + 1)]
                    for i in range(lo, lo + cfg.half)
                ],
                axis=0,
            )
            for lo in (0, cfg.half)
        )
        both = join(swap(xl), xr) if in_right else join(xl, swap(xr))
        y = mm(perm[...], both.astype(BF)).astype(BF)
        for b in range(GROUP):
            stream[GROUP * g + b] = y[b * cfg.piece_c : (b + 1) * cfg.piece_c]


def dma(*shape):
    return pltpu.SemaphoreType.DMA(shape)


def params(collective):
    return pltpu.CompilerParams(
        collective_id=collective, has_side_effects=True, vmem_limit_bytes=LIMIT
    )


def table(cfg, me, lengths, tab):
    n = cfg.n_dp
    wrap = n * cfg.blocks * n

    def owner(o, carry):
        start, own, own_first, own_total, owners = carry
        first = lengths[SEQ_DP * o]
        total = first + lengths[SEQ_DP * o + 1]
        block = start + lax.rem(me - start + wrap, n)
        tab[o] = jnp.clip((block - me) // n, 0, cfg.blocks - 1)
        mine = o == me
        own = jnp.where(mine, start, own)
        own_first = jnp.where(mine, first, own_first)
        own_total = jnp.where(mine, total, own_total)
        owners = tuple(
            count + jnp.where(start <= me + n * j, 1, 0) for j, count in enumerate(owners)
        )
        return start + total, own, own_first, own_total, owners

    zero = jnp.int32(0)
    _, own, first, total, owners = lax.fori_loop(
        0, n, owner, (zero, zero, zero, zero, (jnp.int32(-1),) * cfg.blocks)
    )
    for j, count in enumerate(owners):
        tab[cfg.tab_owner + j] = count
    tab[cfg.tab_own] = lax.rem(own, n)
    tab[cfg.tab_own + 1] = first * BR
    tab[cfg.tab_own + 2] = total * BR


def segments(cfg, tab):
    shape = (cfg.span, LANES)
    inside = lax.broadcasted_iota(jnp.int32, shape, 0)
    first, total = tab[cfg.tab_own + 1], tab[cfg.tab_own + 2]
    segment = jnp.where(inside < first, 0, jnp.where(inside < total, 1, 2))
    which = lane(shape)
    seg_q = jnp.where(which == segment, -BIG, 0.0)
    seg_k = jnp.where((which < 3) & (which != segment), 1.0, 0.0)
    return seg_q, seg_k


def pack_out_term(cfg, term, t_out):
    side = cfg.side
    for tile in range(cfg.width // LANES):
        straight = term[:, tile * LANES : (tile + 1) * LANES]
        turned = swap(straight)
        for c in range(cfg.n_ctx):
            at = c * HEAD_DIM
            mid, end = at + HEAD_DIM // 2, at + HEAD_DIM
            pieces = (
                join(straight[at:mid], turned[mid:end]),
                join(turned[at:mid], straight[mid:end]),
            )
            for odd, piece in enumerate(pieces):
                s, t = divmod(2 * tile + odd, side)
                place = (0, t, s) if c < cfg.half else (1, (s + t) % side, s)
                t_out[(*place, c % cfg.half)] = piece.astype(BF)


def triangle(cfg, axis):
    shape = (cfg.tile, cfg.tile)
    query = lax.broadcasted_iota(jnp.int32, shape, axis)
    return lax.broadcasted_iota(jnp.int32, shape, 1 - axis) > query


def tiles_of(cfg):
    count = cfg.total // cfg.tile
    return [(i, j) for i in range(count) for j in range(i + 1)]


def span_of(cfg, index):
    return slice(index * cfg.tile, (index + 1) * cfg.tile)


def weigh(cfg, qs, keys, i, j):
    h = mm_nt(qs[span_of(cfg, i)], keys[span_of(cfg, j)])
    if i == j:
        h = jnp.where(triangle(cfg, 0), -BIG, h)
    return (h + h * jnp.tanh(h)).astype(BF)


def attend(cfg, vk, qs, keys, att, ready, tiles):
    for i in range(cfg.total // cfg.tile):
        total = None
        for j in range(i + 1):
            if (i, j) in ready:
                weights = tiles[ready[i, j]]
            else:
                weights = weigh(cfg, qs, keys, i, j)
            step = mm(weights, vk[span_of(cfg, j)])
            total = step if total is None else total + step
        att[span_of(cfg, i)] = total


def weigh_back(cfg, qs, keys, i, j):
    h = mm_nt(keys[span_of(cfg, j)], qs[span_of(cfg, i)])
    if i == j:
        h = jnp.where(triangle(cfg, 1), -BIG, h)
    p = 1.0 + jnp.tanh(h)
    a = h * p
    return a.astype(BF), p * ((2.0 * h + 1.0) - a)


def attend_back(cfg, vk, qs, keys, go, qz, dvk, dqt, ready, tiles):
    for j in range(cfg.total // cfg.tile):
        jt = span_of(cfg, j)
        both = vk[jt]
        both_t = both.T
        total = None
        for i in range(j, cfg.total // cfg.tile):
            it = span_of(cfg, i)
            if (i, j) in ready:
                at = ready[i, j]
                weights, slope = tiles[at], tiles[at + 1].astype(F32)
            else:
                weights, slope = weigh_back(cfg, qs, keys, i, j)
            grad_s = (mm_nt(both, go[it]) * slope).astype(BF)
            step = mm(both_t, grad_s)
            dqt[:, it] = step if j == 0 else dqt[:, it] + step
            step = mm(
                jnp.concatenate([weights, grad_s], axis=1),
                jnp.concatenate([go[it], qz[it]], axis=0),
            )
            total = step if total is None else total + step
        dvk[jt] = total


def scratch(cfg):
    side, half, block, count = cfg.side, cfg.half, cfg.width // cfg.n_ctx, PIECES
    deep, line, tiles, groups = block + 32, 2 * cfg.side, cfg.hd // LANES, cfg.blocks // 2 // GROUP
    chunk = (cfg.piece_c, LANES)
    zpart = (cfg.piece_z, LANES)
    zhalf = (groups, cfg.n_ctx, cfg.piece_z // groups, LANES)
    stream = (cfg.total, LANES)
    buffers = {
        "xv": ((cfg.rows, cfg.width), BF),
        "upv": ((cfg.rows, cfg.width), BF),
        "wv": ((cfg.width, 4 * cfg.hd), BF),
        "wov": ((cfg.hd, cfg.width), BF),
        "pre": ((cfg.rows, 4 * cfg.hd), F32),
        "normed": ((2, cfg.rows, cfg.width // 2), BF),
        "zsend0": ((count, cfg.n_ctx, *zpart), BF),
        "zland0": ((count, cfg.n_ctx, *zpart), BF),
        "chunks": ((count, cfg.blocks, *chunk), BF),
        "send0": ((count, cfg.n_dp, *chunk), BF),
        "land00": ((cfg.n_dp, *chunk), BF),
        "land01": ((cfg.n_dp, *chunk), BF),
        "land02": ((cfg.n_dp, *chunk), BF),
        "vk": (stream, BF),
        "qs": (stream, BF),
        "keys": (stream, BF),
        "qz": (stream, BF),
        "go": (stream, BF),
        "rows32": (stream, F32),
        "dqt": ((LANES, cfg.total), F32),
        "stream": ((count, cfg.n_dp, *chunk), BF),
        "send1": ((cfg.n_dp, *chunk), BF),
        "land1": ((cfg.n_dp, *chunk), BF),
        "zsend1": (zhalf, BF),
        "zland1": (zhalf, BF),
        "zsend2": (zhalf, BF),
        "zland2": (zhalf, BF),
        "chunks2": ((cfg.blocks, *chunk), BF),
        "send2": ((cfg.n_dp, *chunk), BF),
        "land2": ((cfg.n_dp, *chunk), BF),
        "att_norm": ((cfg.rows, cfg.hd), F32),
        "gpu": ((tiles, cfg.rows, LANES), BF),
        "t_out": ((2, side, side, half, 32, LANES), BF),
        "send3": ((count, cfg.n_dp, *chunk), BF),
        "land30": ((cfg.n_dp, *chunk), BF),
        "land31": ((cfg.n_dp, *chunk), BF),
        "land32": ((cfg.n_dp, *chunk), BF),
        "zsend3": ((count, cfg.n_ctx, *zpart), BF),
        "zland3": ((count, cfg.n_ctx, *zpart), BF),
        "gp": ((cfg.rows, 4 * cfg.hd), BF),
        "gpt": ((count, tiles, cfg.rows, LANES), BF),
        "lrecv": ((line, cfg.rows, cfg.width // 2), BF),
        "grecv": ((side, line, cfg.rows, LANES), BF),
        "trecv": ((line, side, half, 32, LANES), BF),
        "normal_t": ((cfg.width // 2, line * cfg.rows), BF),
        "bsend": ((side, half, block, LANES), BF),
        "brecv": ((side, half, block, LANES), BF),
        "acc": ((half, deep, LANES), F32),
        "tiles": ((2 * sum(EARLY_BACK), cfg.tile, cfg.tile), BF),
        "bsend_o": ((side, half, 32, LANES), BF),
        "brecv_o": ((side, half, 32, LANES), BF),
        "fsend": ((half, 2, deep // 2, LANES), BF),
        "frecv": ((cfg.n_ctx, deep // 2, LANES), BF),
    }
    sems = {
        "in": (7,),
        "ls": (6, line - 1),
        "lr": (6, line),
        "bs": (2, side),
        "br": (2, side),
        "fs": (half, 2),
        "fr": (cfg.n_ctx,),
    }
    for name, size, parts in (
        ("z0", cfg.n_ctx, count),
        ("x0", cfg.n_dp, count),
        ("x1", cfg.n_dp, 1),
        ("z1", cfg.n_ctx, groups),
        ("z2", cfg.n_ctx, groups),
        ("x2", cfg.n_dp, 1),
        ("x3", cfg.n_dp, count),
        ("z3", cfg.n_ctx, count),
    ):
        sems[name + "s"] = (parts, size)
        sems[name + "r"] = (parts, size)
    shapes = {name: pltpu.VMEM(*spec) for name, spec in buffers.items()}
    shapes["tab"] = pltpu.SMEM((cfg.tab_own + 3,), jnp.int32)
    shapes.update({name: dma(*size) for name, size in sems.items()})
    return shapes


def layer_kernel(cfg, names, *refs):
    r = dict(zip(names, refs))
    perm, perm_t, tab = r["perm"], r["perm_t"], r["tab"]
    hd, rows, side, half, n, n_ctx = cfg.hd, cfg.rows, cfg.side, cfg.half, cfg.n_dp, cfg.n_ctx
    count, width, groups = PIECES, GROUP * BR, cfg.blocks // 2 // GROUP
    me, ctx = lax.axis_index("dp"), lax.axis_index("ctx")
    core = lax.rem(me, 2)
    other = 1 - core
    chip_x, chip_y = me // (2 * side), lax.rem(me // 2, side)
    a_own = chip_x * other + chip_y * core
    b_own = chip_y * other + chip_x * core
    along_a = 2 * side - core * (2 * side - 2)
    along_b = 2 + core * (2 * side - 2)
    home = ctx // half
    m_own = 2 * a_own + core

    def device(a, b):
        return a * along_a + b * along_b + core

    adder = (chip_y * side + lax.rem(chip_x + chip_y, side)) * 2 + home
    s_own = lax.rem(chip_y - chip_x + side, side)
    owner = (s_own * side + chip_x) * 2

    def load(number, source, target):
        return pltpu.make_async_copy(source, target, r["in"].at[number])

    loads = [load(0, r["x"].at[0], r["xv"])]
    for i, s in enumerate((*OUT, 0)):
        cut = pl.ds(s * hd, hd)
        loads.append(load(1 + i, r["w"].at[:, cut], r["wv"].at[:, cut]))
    loads.append(load(5, r["up"].at[0], r["upv"]))
    loads.append(load(6, r["w_out"], r["wov"]))
    for item in loads:
        item.start()

    barrier, greetings = greet(cfg, me, ctx)
    for z in range(n_ctx):

        @pl.when(jnp.logical_or(z != ctx, adder != me))
        def _():
            pl.semaphore_signal(
                barrier, inc=1, device_id={"dp": adder, "ctx": z}, device_id_type=MESH
            )

    table(cfg, me, r["lengths"], tab)
    own = tab[cfg.tab_own]

    def moves(axis, source, target, sems, parts):
        size, mine = (n, me) if axis == "dp" else (n_ctx, ctx)
        return [
            Exchange(
                axis,
                size,
                mine,
                source(t),
                target(t),
                Part(r[sems + "s"], t),
                Part(r[sems + "r"], t),
            )
            for t in range(parts)
        ]

    def part(name):
        return lambda t: Part(r[name], t)

    z0 = moves("ctx", part("zsend0"), part("zland0"), "z0", count)
    x0 = moves("dp", part("send0"), lambda t: Part(r["land0" + str(t)]), "x0", count)
    x1 = moves("dp", lambda t: Part(r["send1"]), lambda t: Part(r["land1"]), "x1", 1)[0]
    z1 = moves("ctx", part("zsend1"), part("zland1"), "z1", groups)
    z2 = moves("ctx", part("zsend2"), part("zland2"), "z2", groups)
    x2 = moves("dp", lambda t: Part(r["send2"]), lambda t: Part(r["land2"]), "x2", 1)[0]
    x3 = moves("dp", part("send3"), lambda t: Part(r["land3" + str(t)]), "x3", count)
    z3 = moves("ctx", part("zsend3"), part("zland3"), "z3", count)

    xv, upv, wv, wov, pre = r["xv"], r["upv"], r["wv"], r["wov"], r["pre"]
    normed_ref = r["normed"]
    loads[0].wait()
    normal, inverse = layer_normalize(xv[...].astype(F32))
    normed = normal.astype(BF)
    normed_ref[0] = normed[:, : cfg.width // 2]
    normed_ref[1] = normed[:, cfg.width // 2 :]
    zsend0, zland0, chunks, send0 = r["zsend0"], r["zland0"], r["chunks"], r["send0"]
    step = min(256, hd)

    def section(number, t):
        for base in range(0, hd, step):
            at = number * hd + base
            value = mm(normed, wv[:, at : at + step])
            pre[:, at : at + step] = value
            if t is None:
                continue
            act = silu(value)
            for tile in range(step // LANES):
                head = (base + tile * LANES) // HEAD_DIM
                one, two = pack_rows(act[:, tile * LANES : (tile + 1) * LANES])
                zsend0[t, head] = one.astype(BF)
                zsend0[t, head + 1] = two.astype(BF)

    for t, number in enumerate(OUT):
        loads[1 + t].wait()
        section(number, t)
        if t == 0:
            pl.semaphore_wait(
                barrier, greetings + n_ctx - jnp.where(adder == me, 1, 0).astype(jnp.int32)
            )
        z0[t].start()
        zland0[t, ctx] = zsend0[t, ctx]
    loads[4].wait()
    section(0, None)
    loads[5].wait()
    loads[6].wait()
    back_gated = mm_nt(upv[...], wov[...])
    gate = silu(pre[:, :hd]).astype(BF).astype(F32)
    for t in range(count):
        z0[t].wait_recv()
        for g in range(groups):
            cut = slice(width * g, width * (g + 1))
            regroup_in(
                cfg, g, lambda i, t=t, cut=cut: zland0[t, i, cut], perm, Part(chunks, t)
            )

        def fill(device_at, t=t):
            send0[t, device_at] = chunks[t, tab[device_at]]

        x0[t].start(fill)
        r["land0" + str(t)][me] = chunks[t, tab[me]]

    vk, qs, keys, qz, go = r["vk"], r["qs"], r["keys"], r["qz"], r["go"]
    seg_q, seg_k = segments(cfg, tab)

    def store_k(cut, g, straight, turned):
        keys[cut] = join(seg_k[width * g : width * (g + 1)], turned).astype(BF)

    def store_v(cut, g, straight, turned):
        vk[cut] = join(straight.astype(BF), keys[cut])

    def store_q(cut, g, straight, turned):
        value = turned * (0.5 * HEAD_DIM**-0.5)
        qs[cut] = join(seg_q[width * g : width * (g + 1)], value).astype(BF)
        qz[cut] = join(jnp.zeros_like(value), value).astype(BF)

    pairs, tiles, ready = tiles_of(cfg), r["tiles"], {}
    for t, store in enumerate((store_k, store_q, store_v)):
        if t == 2:
            for i, j in pairs[:EARLY]:
                ready[i, j] = len(ready)
                tiles[ready[i, j]] = weigh(cfg, qs, keys, i, j)
        x0[t].wait_recv()
        unstream(cfg, own, r["land0" + str(t)], perm_t, store)

    gpu, t_out, gpt = r["gpu"], r["t_out"], r["gpt"]
    lrecv, grecv, trecv = r["lrecv"], r["grecv"], r["trecv"]
    def tile_of(a, kind, s):
        return lax.rem(a - s * kind + side, side)

    def line_copy(what, j):
        if j < side - 1:
            kind, a = 0, lax.rem(chip_x + 1 + j, side)
            target, slot = (a * side + chip_y) * 2, 2 * chip_x + core
        elif j < 2 * (side - 1):
            kind, a = 1, lax.rem(chip_y + 1 + j - (side - 1), side)
            target, slot = (chip_x * side + a) * 2 + 1, 2 * chip_y + core
        else:
            kind, a = other, b_own
            target, slot = me + 1 - 2 * core, 2 * b_own + core
        if what == 4:
            source, target_ref = normed_ref.at[kind], lrecv.at[slot]
        elif what == 5:
            source, target_ref = t_out.at[kind, a], trecv.at[slot]
        elif what == 0:
            source, target_ref = gpu.at[tile_of(a, kind, 0)], grecv.at[0, slot]
        else:
            source, target_ref = gpt.at[what - 1, tile_of(a, kind, what)], grecv.at[what, slot]
        return pltpu.make_async_remote_copy(
            src_ref=source,
            dst_ref=target_ref,
            send_sem=r["ls"].at[what, j],
            recv_sem=r["lr"].at[what, slot],
            device_id={"dp": target},
            device_id_type=MESH,
        )

    def line_start(what):
        for j in range(2 * side - 1):
            line_copy(what, j).start()

    def line_wait(what):
        ref = {4: lrecv, 5: trecv}.get(what, None)
        for i in range(1, 2 * side):
            slot = lax.rem(m_own + i, 2 * side)
            place = grecv.at[what, slot] if ref is None else ref.at[slot]
            pltpu.make_async_remote_copy(
                src_ref=place,
                dst_ref=place,
                send_sem=r["ls"].at[what, 0],
                recv_sem=r["lr"].at[what, slot],
                device_id={"dp": me + 1 - 2 * core},
                device_id_type=MESH,
            ).wait_recv()


    line_start(4)
    rows32 = r["rows32"]
    attend(cfg, vk, qs, keys, rows32, ready, tiles)
    ready_back = {}

    def prepare(window):
        for i, j in pairs[len(ready_back) :][: EARLY_BACK[window]]:
            at = 2 * len(ready_back)
            ready_back[i, j] = at
            weights, slope = weigh_back(cfg, qs, keys, i, j)
            tiles[at] = weights
            tiles[at + 1] = slope.astype(BF)

    stream, send1, land1 = r["stream"], r["send1"], r["land1"]
    to_stream(cfg, rows32, perm, Part(stream, 0), False)

    def place(t, device_at):
        return stream[t, lax.rem(device_at - own + n, n)]

    def fill1(device_at):
        send1[device_at] = place(0, device_at)

    x1.start(fill1)
    land1[me] = place(0, me)
    backward_gate = back_gated * gate
    lrecv[m_own] = normed_ref[core]
    line_wait(4)
    normal_t = r["normal_t"]
    for i in range(side):
        pair = jnp.concatenate([lrecv[2 * i], lrecv[2 * i + 1]], axis=0)
        normal_t[:, 2 * rows * i : 2 * rows * (i + 1)] = pair.T

    prepare(0)
    x1.wait_recv()
    zsend1, zland1, zsend2, zland2 = r["zsend1"], r["zland1"], r["zsend2"], r["zland2"]
    for g in range(groups):

        def store1(i, value, g=g):
            zsend1[g, i] = value

        regroup_out(cfg, g, lambda block: land1[tab[cfg.tab_owner + block]], perm_t, store1)
        z1[g].start()
        zland1[g, ctx] = zsend1[g, ctx]
    att_norm = r["att_norm"]
    mid = rows // 2
    prepare(1)
    for g in range(groups):
        z1[g].wait_recv()
        att_rows = jnp.concatenate(
            [
                unpack_rows(zland1[g, head], zland1[g, head + 1])
                for head in range(0, cfg.heads, 2)
            ],
            axis=1,
        )
        norm_part, att_inverse = layer_normalize(att_rows)
        top, low = slice(width * g, width * (g + 1)), slice(mid + width * g, mid + width * (g + 1))
        att_norm[top] = norm_part[:width]
        att_norm[low] = norm_part[width:]
        incoming = jnp.concatenate([backward_gate[top], backward_gate[low]], axis=0)
        grad_att = layer_norm_backward(incoming, norm_part, att_inverse)
        for tile in range(hd // LANES):
            one, two = pack_rows(grad_att[:, tile * LANES : (tile + 1) * LANES])
            zsend2[g, 2 * tile] = one.astype(BF)
            zsend2[g, 2 * tile + 1] = two.astype(BF)
        z2[g].start()
        zland2[g, ctx] = zsend2[g, ctx]

    gated = (att_norm[...] * gate).astype(BF)
    r["out"][0] = (xv[...].astype(F32) + mm(gated, wov[...])).astype(BF)
    prepare(2)
    chunks2, send2, land2 = r["chunks2"], r["send2"], r["land2"]
    for g in range(groups):
        z2[g].wait_recv()
        regroup_in(cfg, g, lambda i, g=g: zland2[g, i], perm, chunks2)

    def fill2(device_at):
        send2[device_at] = chunks2[tab[device_at]]

    x2.start(fill2)
    land2[me] = chunks2[tab[me]]
    gp = r["gp"]
    grad_u = (back_gated * att_norm[...] * silu_grad(pre[:, :hd])).astype(BF)
    gp[:, :hd] = grad_u
    for tile in range(hd // LANES):
        gpu[tile] = grad_u[:, tile * LANES : (tile + 1) * LANES]
    pack_out_term(
        cfg,
        lax.dot_general(gated, upv[...], (((0,), (0,)), ((), ())), preferred_element_type=F32),
        t_out,
    )
    prepare(3)
    x2.wait_recv()

    def store_go(cut, g, straight, turned):
        go[cut] = join(straight, jnp.zeros_like(straight)).astype(BF)

    line_start(0)
    line_start(5)
    unstream(cfg, own, land2, perm_t, store_go)
    dqt = r["dqt"]
    attend_back(cfg, vk, qs, keys, go, qz, rows32, dqt, ready_back, tiles)

    send3, zsend3, zland3 = r["send3"], r["zsend3"], r["zland3"]
    for t in range(count):
        if t == 2:
            for i in range(cfg.total // cfg.tile):
                cut = slice(cfg.tile * i, cfg.tile * (i + 1))
                rows32[cut] = dqt[:, cut].T * (0.5 * HEAD_DIM**-0.5)
        to_stream(cfg, rows32, perm, Part(stream, t), t != 1)

        def fill3(device_at, t=t):
            send3[t, device_at] = place(t, device_at)

        x3[t].start(fill3)
        r["land3" + str(t)][me] = place(t, me)

    send_b, recv_b, acc = r["bsend"], r["brecv"], r["acc"]
    block = cfg.width // n_ctx
    grecv[0, m_own] = gpu[tile_of(a_own, core, 0)]
    trecv[m_own] = t_out[core, a_own]
    line_wait(0)
    line_wait(5)

    def add_copy(part, s):
        b = lax.rem(a_own + s * (1 - 2 * core) + side, side)
        slot = lax.rem(b_own - b + 2 * side - 1, side)
        source, target = ((send_b, recv_b), (r["bsend_o"], r["brecv_o"]))[part]
        return b == b_own, pltpu.make_async_remote_copy(
            src_ref=source.at[s],
            dst_ref=target.at[slot],
            send_sem=r["bs"].at[part, s],
            recv_sem=r["br"].at[part, slot],
            device_id={"dp": device(a_own, b)},
            device_id_type=MESH,
        )

    def add_part(part, s, value):
        mine, copy = add_copy(part, s)

        @pl.when(mine)
        def _():
            if part == 0:
                acc[:, :block] = value
            else:
                acc[:, block:] = value

        @pl.when(jnp.logical_not(mine))
        def _():
            if part == 0:
                send_b[s] = value.astype(BF)
            else:
                r["bsend_o"][s] = value.astype(BF)
            copy.start()

    def add_section(s):
        value = mm(normal_t[...], grecv[s].reshape(2 * side * rows, LANES))
        add_part(0, s, value.reshape(half, block, LANES))

    for s in range(side):
        low = trecv[0, s].astype(F32)
        for m in range(1, 2 * side):
            low = low + trecv[m, s].astype(F32)
        add_part(1, s, low)
    add_section(0)
    for t in range(count):
        x3[t].wait_recv()
        land = r["land3" + str(t)]
        for g in range(groups):

            def store3(i, value, t=t, g=g):
                zsend3[t, i, width * g : width * (g + 1)] = value

            regroup_out(
                cfg, g, lambda b, land=land: land[tab[cfg.tab_owner + b]], perm_t, store3
            )
        z3[t].start()
        zland3[t, ctx] = zsend3[t, ctx]

    def give_section(t):
        s = BACK[t]
        z3[t].wait_recv()
        for head in range(0, cfg.heads, 2):
            tile = head // 2
            at = s * hd + tile * LANES
            cut = slice(at, at + LANES)
            value = unpack_rows(zland3[t, head], zland3[t, head + 1])
            value = (value * silu_grad(pre[:, cut])).astype(BF)
            gp[:, cut] = value
            gpt[s - 1, tile] = value
        line_start(s)
        grecv[s, m_own] = gpt[s - 1, tile_of(a_own, core, s)]

    back = mm_nt(gp[:, :hd], wv[:, :hd])
    give_section(0)
    back = back + mm_nt(gp[:, 3 * hd :], wv[:, 3 * hd :])
    give_section(1)
    line_wait(BACK[0])
    add_section(BACK[0])
    give_section(2)
    line_wait(BACK[1])
    add_section(BACK[1])
    back = back + mm_nt(gp[:, hd : 2 * hd], wv[:, hd : 2 * hd])

    back = back + mm_nt(gp[:, 2 * hd : 3 * hd], wv[:, 2 * hd : 3 * hd])
    r["gradient"][0] = (
        upv[...].astype(F32) + layer_norm_backward(back, normal, inverse)
    ).astype(BF)
    line_wait(BACK[2])
    add_section(BACK[2])

    total = acc[...]
    for slot in range(side - 1):
        for part, target in enumerate((recv_b, r["brecv_o"])):
            pltpu.make_async_remote_copy(
                src_ref=target.at[slot],
                dst_ref=target.at[slot],
                send_sem=r["bs"].at[part, 0],
                recv_sem=r["br"].at[part, slot],
                device_id={"dp": me + 1 - 2 * core},
                device_id_type=MESH,
            ).wait_recv()
        arrived = jnp.concatenate([recv_b[slot], r["brecv_o"][slot]], axis=1)
        total = total + arrived.astype(F32)

    fsend, frecv = r["fsend"], r["frecv"]
    quarter = lax.rem(lane((16, LANES)), HEAD_DIM) < 32
    for h in range(half):
        top, low = total[h, : block // 2], total[h, block // 2 : block]
        u, v = total[h, block : block + 16], total[h, block + 16 :]
        fsend[h, 0, : block // 2] = join(top, swap(low)).astype(BF)
        fsend[h, 1, : block // 2] = join(swap(top), low).astype(BF)
        fsend[h, 0, block // 2 :] = jnp.where(quarter, u, pltpu.roll(v, 32, 1)).astype(BF)
        fsend[h, 1, block // 2 :] = jnp.where(quarter, pltpu.roll(u, 96, 1), v).astype(BF)

    def last_copy(h, kind):
        return pltpu.make_async_remote_copy(
            src_ref=fsend.at[h, kind],
            dst_ref=frecv.at[ctx],
            send_sem=r["fs"].at[h, kind],
            recv_sem=r["fr"].at[ctx],
            device_id={"dp": owner + kind, "ctx": half * core + h},
            device_id_type=MESH,
        )

    def stays(h, kind):
        return jnp.logical_and(half * core + h == ctx, owner + kind == me)

    for h in range(half):
        for kind in range(2):

            @pl.when(stays(h, kind))
            def _():
                frecv[ctx] = fsend[h, kind]

            @pl.when(jnp.logical_not(stays(h, kind)))
            def _():
                last_copy(h, kind).start()

    for z in range(n_ctx):

        @pl.when(jnp.logical_or(z != ctx, adder != me))
        def _():
            pltpu.make_async_remote_copy(
                src_ref=fsend.at[0, 0],
                dst_ref=frecv.at[z],
                send_sem=r["fs"].at[0, 0],
                recv_sem=r["fr"].at[z],
                device_id={"dp": me + 1 - 2 * core},
                device_id_type=MESH,
            ).wait_recv()

    total = frecv[0].astype(F32)
    for z in range(1, n_ctx):
        total = total + frecv[z].astype(F32)
    r["last"][...] = total * (rows * n * n_ctx) ** -0.5

    for move in (*z0, *x0, x1, *z1, *z2, x2, *x3, *z3):
        move.wait_send()
    for what in range(6):
        for j in range(2 * side - 1):
            line_copy(what, j).wait_send()
    for part in range(2):
        for s in range(side):
            mine, copy = add_copy(part, s)

            @pl.when(jnp.logical_not(mine))
            def _():
                copy.wait_send()

    for h in range(half):
        for kind in range(2):

            @pl.when(jnp.logical_not(stays(h, kind)))
            def _():
                last_copy(h, kind).wait_send()


def layer(cfg, lengths, x, up, w, w_out, perm, perm_t):
    block = cfg.width // cfg.n_ctx
    inputs = {
        "lengths": SMEM,
        "x": HBM,
        "up": HBM,
        "w": HBM,
        "w_out": HBM,
        "perm": VMEM,
        "perm_t": VMEM,
    }
    outputs = {
        "out": jax.ShapeDtypeStruct(x.shape, BF),
        "gradient": jax.ShapeDtypeStruct(x.shape, BF),
        "last": jax.ShapeDtypeStruct((block // 2 + 16, LANES), F32),
    }
    shapes = scratch(cfg)
    return pl.pallas_call(
        functools.partial(layer_kernel, cfg, [*inputs, *outputs, *shapes]),
        name="layer",
        out_shape=tuple(outputs.values()),
        in_specs=list(inputs.values()),
        out_specs=(VMEM,) * len(outputs),
        scratch_shapes=list(shapes.values()),
        compiler_params=params(0),
    )(lengths, x, up, w, w_out, perm, perm_t)


def finish_kernel(half_block, last, out, gradient, gw, go, out_copy, gradient_copy, sems):
    copies = [
        pltpu.make_async_copy(out, out_copy, sems.at[0]),
        pltpu.make_async_copy(gradient, gradient_copy, sems.at[1]),
    ]
    for copy in copies:
        copy.start()
    front, low = last[:half_block].T, last[half_block:].T
    gw[...] = jnp.concatenate([front[:HEAD_DIM], front[HEAD_DIM:]], axis=1)
    go[...] = jnp.concatenate([low[32 * i : 32 * (i + 1)] for i in range(4)], axis=1)
    for copy in copies:
        copy.wait()


def finish(cfg, last, out, gradient):
    block = cfg.width // cfg.n_ctx
    anywhere = pl.BlockSpec(memory_space=pl.ANY)
    return pl.pallas_call(
        functools.partial(finish_kernel, block // 2),
        name="finish",
        out_shape=(
            jax.ShapeDtypeStruct((HEAD_DIM, block), F32),
            jax.ShapeDtypeStruct((32, HEAD_DIM), F32),
            jax.ShapeDtypeStruct(out.shape, BF),
            jax.ShapeDtypeStruct(out.shape, BF),
        ),
        in_specs=[VMEM, anywhere, anywhere],
        out_specs=(VMEM, VMEM, anywhere, anywhere),
        scratch_shapes=[dma(2)],
        compiler_params=pltpu.CompilerParams(vmem_limit_bytes=LIMIT),
    )(last, out, gradient)


def shards(n_dp, n_ctx, embedded, upstream, w_uvqk, w_out, lengths):
    cfg = Cfg(n_dp, n_ctx, embedded.shape[1], embedded.shape[2])
    matrix = permutation(cfg.half)
    perm, perm_t = jnp.asarray(matrix, BF), jnp.asarray(matrix.T, BF)
    out, gradient, last = layer(cfg, lengths, embedded, upstream, w_uvqk, w_out, perm, perm_t)
    grad_w, grad_out, out, gradient = finish(cfg, last, out, gradient)
    return out, gradient, grad_w.T, grad_out.T


def solution(mesh):
    return jax.shard_map(
        functools.partial(shards, mesh.shape["dp"], mesh.shape["ctx"]),
        mesh=mesh,
        in_specs=(P("ctx", "dp", None), P("ctx", "dp", None), P(), P(), P()),
        out_specs=(P("ctx", "dp", None), P("ctx", "dp", None), P("ctx", "dp"), P("ctx", "dp")),
        check_vma=False,
    )
```

```python
import functools
import math

import jax
import jax.numpy as jnp
import numpy as np
from jax import lax
from jax.experimental import pallas as pl
from jax.experimental.pallas import tpu as pltpu
from jax.sharding import PartitionSpec as P

HEAD_DIM = 64
BR = 12
SEQ_DP = 2
GROUP = 4
LANES = 128
EPS = 1e-06
BIG = 1e30
MESH = pl.DeviceIdType.MESH
BF = jnp.bfloat16
F32 = jnp.float32
VMEM = pl.BlockSpec(memory_space=pltpu.VMEM)
SMEM = pl.BlockSpec(memory_space=pltpu.SMEM)
HBM = pl.BlockSpec(memory_space=pltpu.HBM)
LIMIT = 62 * 1024 * 1024
PIECES = 3
OUT = (3, 2, 1)
PREPARED = True
TILES = 30
BACK = (3, 1, 2)


class Cfg:
    def __init__(self, n_dp, n_ctx, rows, width):
        self.n_dp = n_dp
        self.n_ctx = n_ctx
        self.rows = rows
        self.width = width
        self.blocks = rows // BR
        self.heads = n_ctx
        self.hd = self.heads * HEAD_DIM
        self.half = n_ctx // 2
        self.piece_z = rows // 2
        self.piece_c = n_ctx * BR // 2
        self.span = n_dp * BR
        self.side = math.isqrt(n_dp // 2)
        self.total = n_ctx * self.span
        self.tile = min(512, self.total // 3)
        self.tab_owner = n_dp
        self.tab_own = n_dp + self.blocks + 1


def permutation(contexts):
    size = contexts * GROUP * BR
    matrix = np.zeros((size, size), np.float32)
    for block in range(GROUP):
        for context in range(contexts):
            for row in range(BR):
                matrix[
                    (block * contexts + context) * BR + row, (context * GROUP + block) * BR + row
                ] = 1.0
    return matrix


def lane(shape):
    return lax.broadcasted_iota(jnp.int32, shape, len(shape) - 1)


def swap(tensor):
    return pltpu.roll(tensor, HEAD_DIM, 1)


def join(left, right):
    return jnp.where(lane(left.shape) < HEAD_DIM, left, right)


def mm(left, right):
    return jnp.dot(left, right, preferred_element_type=F32)


def mm_nt(left, right):
    return lax.dot_general(left, right, (((1,), (1,)), ((), ())), preferred_element_type=F32)


def layer_normalize(tensor):
    centre = jnp.mean(tensor, -1, keepdims=True)
    centred = tensor - centre
    inverse = lax.rsqrt(jnp.mean(centred * centred, -1, keepdims=True) + EPS)
    return centred * inverse, inverse


def layer_norm_backward(incoming, normal, inverse):
    first = jnp.mean(incoming, -1, keepdims=True)
    second = jnp.mean(incoming * normal, -1, keepdims=True)
    return (incoming - first - normal * second) * inverse


def silu(argument):
    return argument * jax.nn.sigmoid(argument)


def silu_grad(argument):
    sigmoid = jax.nn.sigmoid(argument)
    return sigmoid * (1.0 + argument * (1.0 - sigmoid))


def pack_rows(value):
    mid = value.shape[0] // 2
    top, low = value[:mid], value[mid:]
    return join(top, swap(low)), join(swap(top), low)


def unpack_rows(first, second):
    first, second = first.astype(F32), second.astype(F32)
    return jnp.concatenate([join(first, swap(second)), join(swap(first), second)], axis=0)


def greet(cfg, me, ctx):
    barrier = pltpu.get_barrier_semaphore()

    def along_dp(k, carry):
        pl.semaphore_signal(
            barrier, inc=1, device_id={"dp": lax.rem(me + k, cfg.n_dp)}, device_id_type=MESH
        )
        return carry

    def along_ctx(k, carry):
        pl.semaphore_signal(
            barrier, inc=1, device_id={"ctx": lax.rem(ctx + k, cfg.n_ctx)}, device_id_type=MESH
        )
        return carry

    lax.fori_loop(1, cfg.n_dp, along_dp, 0)
    lax.fori_loop(1, cfg.n_ctx, along_ctx, 0)
    return barrier, cfg.n_dp + cfg.n_ctx - 2


class Part:
    def __init__(self, ref, *prefix):
        self.ref, self.prefix = ref, prefix

    def whole(self, index):
        return (*self.prefix, *(index if isinstance(index, tuple) else (index,)))

    def at(self, index):
        return self.ref.at[self.whole(index)]

    def __getitem__(self, index):
        return self.ref[self.whole(index)]

    def __setitem__(self, index, value):
        self.ref[self.whole(index)] = value


class Exchange:
    def __init__(self, axis, count, mine, source, target, send_sem, recv_sem):
        self.axis, self.count, self.mine = axis, count, mine
        self.source, self.target = source, target
        self.send_sem, self.recv_sem = send_sem, recv_sem

    def copy(self, other, slot):
        return pltpu.make_async_remote_copy(
            src_ref=self.source.at(other),
            dst_ref=self.target.at(slot),
            send_sem=self.send_sem.at(other),
            recv_sem=self.recv_sem.at(slot),
            device_id={self.axis: other},
            device_id_type=MESH,
        )

    def each(self, act):
        def step(k, carry):
            act(lax.rem(self.mine + k, self.count))
            return carry

        lax.fori_loop(1, self.count, step, 0)

    def start(self, before=None):
        def act(other):
            if before is not None:
                before(other)
            self.copy(other, self.mine).start()

        self.each(act)

    def wait_recv(self):
        self.each(lambda other: self.copy(other, other).wait_recv())

    def wait_send(self):
        self.each(lambda other: self.copy(other, self.mine).wait_send())


def regroup_in(cfg, g, source, perm, chunks):
    half_blocks = cfg.blocks // 2
    yl, yr = (
        mm(perm[...], jnp.concatenate([source(i) for i in range(lo, lo + cfg.half)], axis=0))
        for lo in (0, cfg.half)
    )
    left = join(yl, swap(yr)).astype(BF)
    right = join(swap(yl), yr).astype(BF)
    for b in range(GROUP):
        rows = slice(b * cfg.piece_c, (b + 1) * cfg.piece_c)
        chunks[GROUP * g + b] = left[rows]
        chunks[half_blocks + GROUP * g + b] = right[rows]


def regroup_out(cfg, g, picked, perm_t, store):
    width = GROUP * BR
    yl, yr = (
        mm(
            perm_t[...],
            jnp.concatenate([picked(lo + GROUP * g + b) for b in range(GROUP)], axis=0),
        )
        for lo in (0, cfg.blocks // 2)
    )
    left = join(yl, swap(yr)).astype(BF)
    right = join(swap(yl), yr).astype(BF)
    for i in range(cfg.half):
        rows = slice(width * i, width * (i + 1))
        store(i, left[rows])
        store(cfg.half + i, right[rows])


def unstream(cfg, own, piece, perm_t, store):
    width = GROUP * BR
    for g in range(cfg.n_dp // GROUP):
        rows = [piece[lax.rem(own + GROUP * g + b, cfg.n_dp)] for b in range(GROUP)]
        straight = mm(perm_t[...], jnp.concatenate(rows, axis=0))
        turned = swap(straight)
        for i in range(cfg.half):
            cut = slice(width * i, width * (i + 1))
            for c, one, two in ((i, straight, turned), (cfg.half + i, turned, straight)):
                at = cfg.span * c + width * g
                store(slice(at, at + width), g, one[cut], two[cut])


def to_stream(cfg, source, perm, stream, in_right):
    width = GROUP * BR
    for g in range(cfg.n_dp // GROUP):
        xl, xr = (
            jnp.concatenate(
                [
                    source[cfg.span * i + width * g : cfg.span * i + width * (g + 1)]
                    for i in range(lo, lo + cfg.half)
                ],
                axis=0,
            )
            for lo in (0, cfg.half)
        )
        both = join(swap(xl), xr) if in_right else join(xl, swap(xr))
        y = mm(perm[...], both.astype(BF)).astype(BF)
        for b in range(GROUP):
            stream[GROUP * g + b] = y[b * cfg.piece_c : (b + 1) * cfg.piece_c]


def dma(*shape):
    return pltpu.SemaphoreType.DMA(shape)


def params(collective):
    return pltpu.CompilerParams(
        collective_id=collective, has_side_effects=True, vmem_limit_bytes=LIMIT
    )


def table(cfg, me, lengths, tab):
    n = cfg.n_dp
    wrap = n * cfg.blocks * n

    def owner(o, carry):
        start, own, own_first, own_total, owners = carry
        first = lengths[SEQ_DP * o]
        total = first + lengths[SEQ_DP * o + 1]
        block = start + lax.rem(me - start + wrap, n)
        tab[o] = jnp.clip((block - me) // n, 0, cfg.blocks - 1)
        mine = o == me
        own = jnp.where(mine, start, own)
        own_first = jnp.where(mine, first, own_first)
        own_total = jnp.where(mine, total, own_total)
        owners = tuple(
            count + jnp.where(start <= me + n * j, 1, 0) for j, count in enumerate(owners)
        )
        return start + total, own, own_first, own_total, owners

    zero = jnp.int32(0)
    _, own, first, total, owners = lax.fori_loop(
        0, n, owner, (zero, zero, zero, zero, (jnp.int32(-1),) * cfg.blocks)
    )
    for j, count in enumerate(owners):
        tab[cfg.tab_owner + j] = count
    tab[cfg.tab_own] = lax.rem(own, n)
    tab[cfg.tab_own + 1] = first * BR
    tab[cfg.tab_own + 2] = total * BR


def segments(cfg, tab):
    shape = (cfg.span, LANES)
    inside = lax.broadcasted_iota(jnp.int32, shape, 0)
    first, total = tab[cfg.tab_own + 1], tab[cfg.tab_own + 2]
    segment = jnp.where(inside < first, 0, jnp.where(inside < total, 1, 2))
    which = lane(shape)
    seg_q = jnp.where(which == segment, -BIG, 0.0)
    seg_k = jnp.where((which < 3) & (which != segment), 1.0, 0.0)
    return seg_q, seg_k


def pack_out_term(cfg, term, t_out):
    side = cfg.side
    for tile in range(cfg.width // LANES):
        straight = term[:, tile * LANES : (tile + 1) * LANES]
        turned = swap(straight)
        for c in range(cfg.n_ctx):
            at = c * HEAD_DIM
            mid, end = at + HEAD_DIM // 2, at + HEAD_DIM
            pieces = (
                join(straight[at:mid], turned[mid:end]),
                join(turned[at:mid], straight[mid:end]),
            )
            for odd, piece in enumerate(pieces):
                s, t = divmod(2 * tile + odd, side)
                place = (0, t, s) if c < cfg.half else (1, (s + t) % side, s)
                t_out[(*place, c % cfg.half)] = piece.astype(BF)


def triangle(cfg, axis):
    shape = (cfg.tile, cfg.tile)
    query = lax.broadcasted_iota(jnp.int32, shape, axis)
    return lax.broadcasted_iota(jnp.int32, shape, 1 - axis) > query


def span_of(cfg, index):
    return slice(index * cfg.tile, (index + 1) * cfg.tile)


def at_tile(cfg, index):
    return pl.ds(pl.multiple_of(index * cfg.tile, cfg.tile), cfg.tile)


def attend(cfg, vk, qs, keys, att):
    each = cfg.total // cfg.tile
    half = each // 2

    def pair(i, j, diagonal):
        it, jt = at_tile(cfg, i), at_tile(cfg, j)
        h = mm_nt(qs[it], keys[jt])
        if diagonal:
            h = jnp.where(triangle(cfg, 0), -BIG, h)
        step = mm((h + h * jnp.tanh(h)).astype(BF), vk[jt])
        att[it] = step if diagonal else att[it] + step

    def diagonal(k, carry):
        for p in range(half):
            pair(half * k + p, half * k + p, True)
        return carry

    def round_of(k, carry):
        for i, j in round_pairs(cfg, k):
            pair(i, j, False)
        return carry

    lax.fori_loop(0, 2, diagonal, 0)
    lax.fori_loop(0, each - 1, round_of, 0)


def weigh_back(cfg, qs, keys, i, j, diagonal):
    h = mm_nt(keys[at_tile(cfg, j)], qs[at_tile(cfg, i)])
    if diagonal:
        h = jnp.where(triangle(cfg, 1), -BIG, h)
    p = 1.0 + jnp.tanh(h)
    a = h * p
    return a.astype(BF), p * ((2.0 * h + 1.0) - a)


def round_pairs(cfg, k):
    last = cfg.total // cfg.tile - 1
    pairs = [(last, k)]
    for d in range(1, (last + 1) // 2):
        one, two = lax.rem(k + d, last), lax.rem(k - d + last, last)
        pairs.append((jnp.maximum(one, two), jnp.minimum(one, two)))
    return pairs


def prepare(cfg, qs, keys, tiles, rounds):
    each = cfg.total // cfg.tile

    def one(k, carry):
        for p, (i, j) in enumerate(round_pairs(cfg, k)):
            weights, slope = weigh_back(cfg, qs, keys, i, j, False)
            tiles[each * k + 2 * p] = weights
            tiles[each * k + 2 * p + 1] = slope.astype(BF)
        return carry

    lax.fori_loop(*rounds, one, 0)


def attend_back(cfg, vk, vkt, qs, keys, go, qz, dvk, dqt, tiles):
    each = cfg.total // cfg.tile
    half = each // 2

    def pair(i, j, weights, slope, first):
        it, jt = at_tile(cfg, i), at_tile(cfg, j)
        grad_s = (mm_nt(vk[jt], go[it]) * slope).astype(BF)
        query = mm(vkt[:, jt], grad_s)
        key = mm(
            jnp.concatenate([weights, grad_s], axis=1),
            jnp.concatenate([go[it], qz[it]], axis=0),
        )
        dqt[:, it] = query if first else dqt[:, it] + query
        dvk[jt] = key if first else dvk[jt] + key

    def diagonal(k, carry):
        for p in range(half):
            i = half * k + p
            pair(i, i, *weigh_back(cfg, qs, keys, i, i, True), True)
        return carry

    def round_of(k, carry):
        for p, (i, j) in enumerate(round_pairs(cfg, k)):
            if PREPARED:
                weights = tiles[each * k + 2 * p]
                slope = tiles[each * k + 2 * p + 1].astype(F32)
            else:
                weights, slope = weigh_back(cfg, qs, keys, i, j, False)
            pair(i, j, weights, slope, False)
        return carry

    lax.fori_loop(0, 2, diagonal, 0)
    lax.fori_loop(0, each - 1, round_of, 0)


def scratch(cfg):
    side, half, block, count = cfg.side, cfg.half, cfg.width // cfg.n_ctx, PIECES
    deep, line, tiles, groups = block + 32, 2 * cfg.side, cfg.hd // LANES, cfg.blocks // 2 // GROUP
    chunk = (cfg.piece_c, LANES)
    zpart = (cfg.piece_z, LANES)
    zhalf = (groups, cfg.n_ctx, cfg.piece_z // groups, LANES)
    stream = (cfg.total, LANES)
    buffers = {
        "xv": ((cfg.rows, cfg.width), BF),
        "upv": ((cfg.rows, cfg.width), BF),
        "wv": ((cfg.width, 4 * cfg.hd), BF),
        "wov": ((cfg.hd, cfg.width), BF),
        "pre": ((cfg.rows, 4 * cfg.hd), F32),
        "normed": ((2, cfg.rows, cfg.width // 2), BF),
        "zsend0": ((count, cfg.n_ctx, *zpart), BF),
        "zland0": ((count, cfg.n_ctx, *zpart), BF),
        "chunks": ((count, cfg.blocks, *chunk), BF),
        "send0": ((count, cfg.n_dp, *chunk), BF),
        "land00": ((cfg.n_dp, *chunk), BF),
        "land01": ((cfg.n_dp, *chunk), BF),
        "land02": ((cfg.n_dp, *chunk), BF),
        "vk": (stream, BF),
        "qs": (stream, BF),
        "keys": (stream, BF),
        "qz": (stream, BF),
        "go": (stream, BF),
        "rows32": (stream, F32),
        "dqt": ((LANES, cfg.total), F32),
        "stream": ((count, cfg.n_dp, *chunk), BF),
        "send1": ((cfg.n_dp, *chunk), BF),
        "land1": ((cfg.n_dp, *chunk), BF),
        "zsend1": (zhalf, BF),
        "zland1": (zhalf, BF),
        "zsend2": (zhalf, BF),
        "zland2": (zhalf, BF),
        "chunks2": ((cfg.blocks, *chunk), BF),
        "send2": ((cfg.n_dp, *chunk), BF),
        "land2": ((cfg.n_dp, *chunk), BF),
        "att_norm": ((cfg.rows, cfg.hd), F32),
        "gpu": ((tiles, cfg.rows, LANES), BF),
        "t_out": ((2, side, side, half, 32, LANES), BF),
        "send3": ((count, cfg.n_dp, *chunk), BF),
        "land30": ((cfg.n_dp, *chunk), BF),
        "land31": ((cfg.n_dp, *chunk), BF),
        "land32": ((cfg.n_dp, *chunk), BF),
        "zsend3": ((count, cfg.n_ctx, *zpart), BF),
        "zland3": ((count, cfg.n_ctx, *zpart), BF),
        "gp": ((cfg.rows, 4 * cfg.hd), BF),
        "gpt": ((count, tiles, cfg.rows, LANES), BF),
        "lrecv": ((line, cfg.rows, cfg.width // 2), BF),
        "grecv": ((side, line, cfg.rows, LANES), BF),
        "trecv": ((line, side, half, 32, LANES), BF),
        "normal_t": ((cfg.width // 2, line * cfg.rows), BF),
        "bsend": ((side, half, block, LANES), BF),
        "brecv": ((side, half, block, LANES), BF),
        "acc": ((half, deep, LANES), F32),
        "tiles": ((TILES, cfg.tile, cfg.tile), BF),
        "vkt": ((LANES, cfg.total), BF),
        "bsend_o": ((side, half, 32, LANES), BF),
        "brecv_o": ((side, half, 32, LANES), BF),
        "fsend": ((half, 2, deep // 2, LANES), BF),
        "frecv": ((cfg.n_ctx, deep // 2, LANES), BF),
    }
    sems = {
        "in": (7,),
        "ls": (6, line - 1),
        "lr": (6, line),
        "bs": (2, side),
        "br": (2, side),
        "fs": (half, 2),
        "fr": (cfg.n_ctx,),
    }
    for name, size, parts in (
        ("z0", cfg.n_ctx, count),
        ("x0", cfg.n_dp, count),
        ("x1", cfg.n_dp, 1),
        ("z1", cfg.n_ctx, groups),
        ("z2", cfg.n_ctx, groups),
        ("x2", cfg.n_dp, 1),
        ("x3", cfg.n_dp, count),
        ("z3", cfg.n_ctx, count),
    ):
        sems[name + "s"] = (parts, size)
        sems[name + "r"] = (parts, size)
    shapes = {name: pltpu.VMEM(*spec) for name, spec in buffers.items()}
    shapes["tab"] = pltpu.SMEM((cfg.tab_own + 3,), jnp.int32)
    shapes.update({name: dma(*size) for name, size in sems.items()})
    return shapes


def layer_kernel(cfg, names, *refs):
    r = dict(zip(names, refs))
    perm, perm_t, tab = r["perm"], r["perm_t"], r["tab"]
    hd, rows, side, half, n, n_ctx = cfg.hd, cfg.rows, cfg.side, cfg.half, cfg.n_dp, cfg.n_ctx
    count, width, groups = PIECES, GROUP * BR, cfg.blocks // 2 // GROUP
    me, ctx = lax.axis_index("dp"), lax.axis_index("ctx")
    core = lax.rem(me, 2)
    other = 1 - core
    chip_x, chip_y = me // (2 * side), lax.rem(me // 2, side)
    a_own = chip_x * other + chip_y * core
    b_own = chip_y * other + chip_x * core
    along_a = 2 * side - core * (2 * side - 2)
    along_b = 2 + core * (2 * side - 2)
    home = ctx // half
    m_own = 2 * a_own + core

    def device(a, b):
        return a * along_a + b * along_b + core

    adder = (chip_y * side + lax.rem(chip_x + chip_y, side)) * 2 + home
    s_own = lax.rem(chip_y - chip_x + side, side)
    owner = (s_own * side + chip_x) * 2

    def load(number, source, target):
        return pltpu.make_async_copy(source, target, r["in"].at[number])

    loads = [load(0, r["x"].at[0], r["xv"])]
    for i, s in enumerate((*OUT, 0)):
        cut = pl.ds(s * hd, hd)
        loads.append(load(1 + i, r["w"].at[:, cut], r["wv"].at[:, cut]))
    loads.append(load(5, r["up"].at[0], r["upv"]))
    loads.append(load(6, r["w_out"], r["wov"]))
    for item in loads:
        item.start()

    barrier, greetings = greet(cfg, me, ctx)
    for z in range(n_ctx):

        @pl.when(jnp.logical_or(z != ctx, adder != me))
        def _():
            pl.semaphore_signal(
                barrier, inc=1, device_id={"dp": adder, "ctx": z}, device_id_type=MESH
            )

    table(cfg, me, r["lengths"], tab)
    own = tab[cfg.tab_own]

    def moves(axis, source, target, sems, parts):
        size, mine = (n, me) if axis == "dp" else (n_ctx, ctx)
        return [
            Exchange(
                axis,
                size,
                mine,
                source(t),
                target(t),
                Part(r[sems + "s"], t),
                Part(r[sems + "r"], t),
            )
            for t in range(parts)
        ]

    def part(name):
        return lambda t: Part(r[name], t)

    z0 = moves("ctx", part("zsend0"), part("zland0"), "z0", count)
    x0 = moves("dp", part("send0"), lambda t: Part(r["land0" + str(t)]), "x0", count)
    x1 = moves("dp", lambda t: Part(r["send1"]), lambda t: Part(r["land1"]), "x1", 1)[0]
    z1 = moves("ctx", part("zsend1"), part("zland1"), "z1", groups)
    z2 = moves("ctx", part("zsend2"), part("zland2"), "z2", groups)
    x2 = moves("dp", lambda t: Part(r["send2"]), lambda t: Part(r["land2"]), "x2", 1)[0]
    x3 = moves("dp", part("send3"), lambda t: Part(r["land3" + str(t)]), "x3", count)
    z3 = moves("ctx", part("zsend3"), part("zland3"), "z3", count)

    xv, upv, wv, wov, pre = r["xv"], r["upv"], r["wv"], r["wov"], r["pre"]
    normed_ref = r["normed"]
    loads[0].wait()
    normal, inverse = layer_normalize(xv[...].astype(F32))
    normed = normal.astype(BF)
    normed_ref[0] = normed[:, : cfg.width // 2]
    normed_ref[1] = normed[:, cfg.width // 2 :]
    zsend0, zland0, chunks, send0 = r["zsend0"], r["zland0"], r["chunks"], r["send0"]
    step = min(256, hd)

    def section(number, t):
        for base in range(0, hd, step):
            at = number * hd + base
            value = mm(normed, wv[:, at : at + step])
            pre[:, at : at + step] = value
            if t is None:
                continue
            act = silu(value)
            for tile in range(step // LANES):
                head = (base + tile * LANES) // HEAD_DIM
                one, two = pack_rows(act[:, tile * LANES : (tile + 1) * LANES])
                zsend0[t, head] = one.astype(BF)
                zsend0[t, head + 1] = two.astype(BF)

    for t, number in enumerate(OUT):
        loads[1 + t].wait()
        section(number, t)
        if t == 0:
            pl.semaphore_wait(
                barrier, greetings + n_ctx - jnp.where(adder == me, 1, 0).astype(jnp.int32)
            )
        z0[t].start()
        zland0[t, ctx] = zsend0[t, ctx]
    loads[4].wait()
    section(0, None)
    loads[5].wait()
    loads[6].wait()
    back_gated = mm_nt(upv[...], wov[...])
    gate = silu(pre[:, :hd]).astype(BF).astype(F32)
    for t in range(count):
        z0[t].wait_recv()
        for g in range(groups):
            cut = slice(width * g, width * (g + 1))
            regroup_in(
                cfg, g, lambda i, t=t, cut=cut: zland0[t, i, cut], perm, Part(chunks, t)
            )

        def fill(device_at, t=t):
            send0[t, device_at] = chunks[t, tab[device_at]]

        x0[t].start(fill)
        r["land0" + str(t)][me] = chunks[t, tab[me]]

    vk, qs, keys, qz, go = r["vk"], r["qs"], r["keys"], r["qz"], r["go"]
    seg_q, seg_k = segments(cfg, tab)

    def store_k(cut, g, straight, turned):
        keys[cut] = join(seg_k[width * g : width * (g + 1)], turned).astype(BF)

    def store_v(cut, g, straight, turned):
        vk[cut] = join(straight.astype(BF), keys[cut])

    def store_q(cut, g, straight, turned):
        value = turned * (0.5 * HEAD_DIM**-0.5)
        qs[cut] = join(seg_q[width * g : width * (g + 1)], value).astype(BF)
        qz[cut] = join(jnp.zeros_like(value), value).astype(BF)

    tiles = r["tiles"]
    for t, store in enumerate((store_k, store_q, store_v)):
        x0[t].wait_recv()
        unstream(cfg, own, r["land0" + str(t)], perm_t, store)

    gpu, t_out, gpt = r["gpu"], r["t_out"], r["gpt"]
    lrecv, grecv, trecv = r["lrecv"], r["grecv"], r["trecv"]
    def tile_of(a, kind, s):
        return lax.rem(a - s * kind + side, side)

    def line_copy(what, j):
        if j < side - 1:
            kind, a = 0, lax.rem(chip_x + 1 + j, side)
            target, slot = (a * side + chip_y) * 2, 2 * chip_x + core
        elif j < 2 * (side - 1):
            kind, a = 1, lax.rem(chip_y + 1 + j - (side - 1), side)
            target, slot = (chip_x * side + a) * 2 + 1, 2 * chip_y + core
        else:
            kind, a = other, b_own
            target, slot = me + 1 - 2 * core, 2 * b_own + core
        if what == 4:
            source, target_ref = normed_ref.at[kind], lrecv.at[slot]
        elif what == 5:
            source, target_ref = t_out.at[kind, a], trecv.at[slot]
        elif what == 0:
            source, target_ref = gpu.at[tile_of(a, kind, 0)], grecv.at[0, slot]
        else:
            source, target_ref = gpt.at[what - 1, tile_of(a, kind, what)], grecv.at[what, slot]
        return pltpu.make_async_remote_copy(
            src_ref=source,
            dst_ref=target_ref,
            send_sem=r["ls"].at[what, j],
            recv_sem=r["lr"].at[what, slot],
            device_id={"dp": target},
            device_id_type=MESH,
        )

    def line_start(what):
        for j in range(2 * side - 1):
            line_copy(what, j).start()

    def line_wait(what):
        ref = {4: lrecv, 5: trecv}.get(what, None)
        for i in range(1, 2 * side):
            slot = lax.rem(m_own + i, 2 * side)
            place = grecv.at[what, slot] if ref is None else ref.at[slot]
            pltpu.make_async_remote_copy(
                src_ref=place,
                dst_ref=place,
                send_sem=r["ls"].at[what, 0],
                recv_sem=r["lr"].at[what, slot],
                device_id={"dp": me + 1 - 2 * core},
                device_id_type=MESH,
            ).wait_recv()


    line_start(4)
    rows32 = r["rows32"]
    attend(cfg, vk, qs, keys, rows32)

    stream, send1, land1 = r["stream"], r["send1"], r["land1"]
    to_stream(cfg, rows32, perm, Part(stream, 0), False)

    def place(t, device_at):
        return stream[t, lax.rem(device_at - own + n, n)]

    def fill1(device_at):
        send1[device_at] = place(0, device_at)

    x1.start(fill1)
    land1[me] = place(0, me)
    backward_gate = back_gated * gate
    lrecv[m_own] = normed_ref[core]
    line_wait(4)
    normal_t = r["normal_t"]
    for i in range(side):
        pair = jnp.concatenate([lrecv[2 * i], lrecv[2 * i + 1]], axis=0)
        normal_t[:, 2 * rows * i : 2 * rows * (i + 1)] = pair.T

    prepare(cfg, qs, keys, tiles, (0, 3))
    vkt = r["vkt"]
    for i in range(cfg.total // cfg.tile):
        vkt[:, span_of(cfg, i)] = vk[span_of(cfg, i)].T
    x1.wait_recv()
    zsend1, zland1, zsend2, zland2 = r["zsend1"], r["zland1"], r["zsend2"], r["zland2"]
    for g in range(groups):

        def store1(i, value, g=g):
            zsend1[g, i] = value

        regroup_out(cfg, g, lambda block: land1[tab[cfg.tab_owner + block]], perm_t, store1)
        z1[g].start()
        zland1[g, ctx] = zsend1[g, ctx]
    att_norm = r["att_norm"]
    mid = rows // 2
    for g in range(groups):
        z1[g].wait_recv()
        att_rows = jnp.concatenate(
            [
                unpack_rows(zland1[g, head], zland1[g, head + 1])
                for head in range(0, cfg.heads, 2)
            ],
            axis=1,
        )
        norm_part, att_inverse = layer_normalize(att_rows)
        top, low = slice(width * g, width * (g + 1)), slice(mid + width * g, mid + width * (g + 1))
        att_norm[top] = norm_part[:width]
        att_norm[low] = norm_part[width:]
        incoming = jnp.concatenate([backward_gate[top], backward_gate[low]], axis=0)
        grad_att = layer_norm_backward(incoming, norm_part, att_inverse)
        for tile in range(hd // LANES):
            one, two = pack_rows(grad_att[:, tile * LANES : (tile + 1) * LANES])
            zsend2[g, 2 * tile] = one.astype(BF)
            zsend2[g, 2 * tile + 1] = two.astype(BF)
        z2[g].start()
        zland2[g, ctx] = zsend2[g, ctx]

    gated = (att_norm[...] * gate).astype(BF)
    r["out"][0] = (xv[...].astype(F32) + mm(gated, wov[...])).astype(BF)
    chunks2, send2, land2 = r["chunks2"], r["send2"], r["land2"]
    for g in range(groups):
        z2[g].wait_recv()
        regroup_in(cfg, g, lambda i, g=g: zland2[g, i], perm, chunks2)

    def fill2(device_at):
        send2[device_at] = chunks2[tab[device_at]]

    x2.start(fill2)
    land2[me] = chunks2[tab[me]]
    gp = r["gp"]
    grad_u = (back_gated * att_norm[...] * silu_grad(pre[:, :hd])).astype(BF)
    gp[:, :hd] = grad_u
    for tile in range(hd // LANES):
        gpu[tile] = grad_u[:, tile * LANES : (tile + 1) * LANES]
    pack_out_term(
        cfg,
        lax.dot_general(gated, upv[...], (((0,), (0,)), ((), ())), preferred_element_type=F32),
        t_out,
    )
    prepare(cfg, qs, keys, tiles, (3, 5))
    x2.wait_recv()

    def store_go(cut, g, straight, turned):
        go[cut] = join(straight, jnp.zeros_like(straight)).astype(BF)

    line_start(0)
    line_start(5)
    unstream(cfg, own, land2, perm_t, store_go)
    dqt = r["dqt"]
    attend_back(cfg, vk, vkt, qs, keys, go, qz, rows32, dqt, tiles)

    send3, zsend3, zland3 = r["send3"], r["zsend3"], r["zland3"]
    for t in range(count):
        if t == 2:
            for i in range(cfg.total // cfg.tile):
                cut = slice(cfg.tile * i, cfg.tile * (i + 1))
                rows32[cut] = dqt[:, cut].T * (0.5 * HEAD_DIM**-0.5)
        to_stream(cfg, rows32, perm, Part(stream, t), t != 1)

        def fill3(device_at, t=t):
            send3[t, device_at] = place(t, device_at)

        x3[t].start(fill3)
        r["land3" + str(t)][me] = place(t, me)

    send_b, recv_b, acc = r["bsend"], r["brecv"], r["acc"]
    block = cfg.width // n_ctx
    grecv[0, m_own] = gpu[tile_of(a_own, core, 0)]
    trecv[m_own] = t_out[core, a_own]
    line_wait(0)
    line_wait(5)

    def add_copy(part, s):
        b = lax.rem(a_own + s * (1 - 2 * core) + side, side)
        slot = lax.rem(b_own - b + 2 * side - 1, side)
        source, target = ((send_b, recv_b), (r["bsend_o"], r["brecv_o"]))[part]
        return b == b_own, pltpu.make_async_remote_copy(
            src_ref=source.at[s],
            dst_ref=target.at[slot],
            send_sem=r["bs"].at[part, s],
            recv_sem=r["br"].at[part, slot],
            device_id={"dp": device(a_own, b)},
            device_id_type=MESH,
        )

    def add_part(part, s, value):
        mine, copy = add_copy(part, s)

        @pl.when(mine)
        def _():
            if part == 0:
                acc[:, :block] = value
            else:
                acc[:, block:] = value

        @pl.when(jnp.logical_not(mine))
        def _():
            if part == 0:
                send_b[s] = value.astype(BF)
            else:
                r["bsend_o"][s] = value.astype(BF)
            copy.start()

    def add_section(s):
        value = mm(normal_t[...], grecv[s].reshape(2 * side * rows, LANES))
        add_part(0, s, value.reshape(half, block, LANES))

    for s in range(side):
        low = trecv[0, s].astype(F32)
        for m in range(1, 2 * side):
            low = low + trecv[m, s].astype(F32)
        add_part(1, s, low)
    add_section(0)
    for t in range(count):
        x3[t].wait_recv()
        land = r["land3" + str(t)]
        for g in range(groups):

            def store3(i, value, t=t, g=g):
                zsend3[t, i, width * g : width * (g + 1)] = value

            regroup_out(
                cfg, g, lambda b, land=land: land[tab[cfg.tab_owner + b]], perm_t, store3
            )
        z3[t].start()
        zland3[t, ctx] = zsend3[t, ctx]

    def give_section(t):
        s = BACK[t]
        z3[t].wait_recv()
        for head in range(0, cfg.heads, 2):
            tile = head // 2
            at = s * hd + tile * LANES
            cut = slice(at, at + LANES)
            value = unpack_rows(zland3[t, head], zland3[t, head + 1])
            value = (value * silu_grad(pre[:, cut])).astype(BF)
            gp[:, cut] = value
            gpt[s - 1, tile] = value
        line_start(s)
        grecv[s, m_own] = gpt[s - 1, tile_of(a_own, core, s)]

    back = mm_nt(gp[:, :hd], wv[:, :hd])
    give_section(0)
    back = back + mm_nt(gp[:, 3 * hd :], wv[:, 3 * hd :])
    give_section(1)
    line_wait(BACK[0])
    add_section(BACK[0])
    give_section(2)
    line_wait(BACK[1])
    add_section(BACK[1])
    back = back + mm_nt(gp[:, hd : 2 * hd], wv[:, hd : 2 * hd])

    back = back + mm_nt(gp[:, 2 * hd : 3 * hd], wv[:, 2 * hd : 3 * hd])
    r["gradient"][0] = (
        upv[...].astype(F32) + layer_norm_backward(back, normal, inverse)
    ).astype(BF)
    line_wait(BACK[2])
    add_section(BACK[2])

    total = acc[...]
    for slot in range(side - 1):
        for part, target in enumerate((recv_b, r["brecv_o"])):
            pltpu.make_async_remote_copy(
                src_ref=target.at[slot],
                dst_ref=target.at[slot],
                send_sem=r["bs"].at[part, 0],
                recv_sem=r["br"].at[part, slot],
                device_id={"dp": me + 1 - 2 * core},
                device_id_type=MESH,
            ).wait_recv()
        arrived = jnp.concatenate([recv_b[slot], r["brecv_o"][slot]], axis=1)
        total = total + arrived.astype(F32)

    fsend, frecv = r["fsend"], r["frecv"]
    quarter = lax.rem(lane((16, LANES)), HEAD_DIM) < 32
    for h in range(half):
        top, low = total[h, : block // 2], total[h, block // 2 : block]
        u, v = total[h, block : block + 16], total[h, block + 16 :]
        fsend[h, 0, : block // 2] = join(top, swap(low)).astype(BF)
        fsend[h, 1, : block // 2] = join(swap(top), low).astype(BF)
        fsend[h, 0, block // 2 :] = jnp.where(quarter, u, pltpu.roll(v, 32, 1)).astype(BF)
        fsend[h, 1, block // 2 :] = jnp.where(quarter, pltpu.roll(u, 96, 1), v).astype(BF)

    def last_copy(h, kind):
        return pltpu.make_async_remote_copy(
            src_ref=fsend.at[h, kind],
            dst_ref=frecv.at[ctx],
            send_sem=r["fs"].at[h, kind],
            recv_sem=r["fr"].at[ctx],
            device_id={"dp": owner + kind, "ctx": half * core + h},
            device_id_type=MESH,
        )

    def stays(h, kind):
        return jnp.logical_and(half * core + h == ctx, owner + kind == me)

    for h in range(half):
        for kind in range(2):

            @pl.when(stays(h, kind))
            def _():
                frecv[ctx] = fsend[h, kind]

            @pl.when(jnp.logical_not(stays(h, kind)))
            def _():
                last_copy(h, kind).start()

    for z in range(n_ctx):

        @pl.when(jnp.logical_or(z != ctx, adder != me))
        def _():
            pltpu.make_async_remote_copy(
                src_ref=fsend.at[0, 0],
                dst_ref=frecv.at[z],
                send_sem=r["fs"].at[0, 0],
                recv_sem=r["fr"].at[z],
                device_id={"dp": me + 1 - 2 * core},
                device_id_type=MESH,
            ).wait_recv()

    total = frecv[0].astype(F32)
    for z in range(1, n_ctx):
        total = total + frecv[z].astype(F32)
    r["last"][...] = total * (rows * n * n_ctx) ** -0.5

    for move in (*z0, *x0, x1, *z1, *z2, x2, *x3, *z3):
        move.wait_send()
    for what in range(6):
        for j in range(2 * side - 1):
            line_copy(what, j).wait_send()
    for part in range(2):
        for s in range(side):
            mine, copy = add_copy(part, s)

            @pl.when(jnp.logical_not(mine))
            def _():
                copy.wait_send()

    for h in range(half):
        for kind in range(2):

            @pl.when(jnp.logical_not(stays(h, kind)))
            def _():
                last_copy(h, kind).wait_send()


def layer(cfg, lengths, x, up, w, w_out, perm, perm_t):
    block = cfg.width // cfg.n_ctx
    inputs = {
        "lengths": SMEM,
        "x": HBM,
        "up": HBM,
        "w": HBM,
        "w_out": HBM,
        "perm": VMEM,
        "perm_t": VMEM,
    }
    outputs = {
        "out": jax.ShapeDtypeStruct(x.shape, BF),
        "gradient": jax.ShapeDtypeStruct(x.shape, BF),
        "last": jax.ShapeDtypeStruct((block // 2 + 16, LANES), F32),
    }
    shapes = scratch(cfg)
    return pl.pallas_call(
        functools.partial(layer_kernel, cfg, [*inputs, *outputs, *shapes]),
        name="layer",
        out_shape=tuple(outputs.values()),
        in_specs=list(inputs.values()),
        out_specs=(VMEM,) * len(outputs),
        scratch_shapes=list(shapes.values()),
        compiler_params=params(0),
    )(lengths, x, up, w, w_out, perm, perm_t)


def finish_kernel(half_block, last, out, gradient, gw, go, out_copy, gradient_copy):
    front, low = last[:half_block].T, last[half_block:].T
    gw[...] = jnp.concatenate([front[:HEAD_DIM], front[HEAD_DIM:]], axis=1)
    go[...] = jnp.concatenate([low[32 * i : 32 * (i + 1)] for i in range(4)], axis=1)
    out_copy[...] = out[...]
    gradient_copy[...] = gradient[...]


def finish(cfg, last, out, gradient):
    block = cfg.width // cfg.n_ctx
    return pl.pallas_call(
        functools.partial(finish_kernel, block // 2),
        name="finish",
        out_shape=(
            jax.ShapeDtypeStruct((HEAD_DIM, block), F32),
            jax.ShapeDtypeStruct((32, HEAD_DIM), F32),
            jax.ShapeDtypeStruct(out.shape, BF),
            jax.ShapeDtypeStruct(out.shape, BF),
        ),
        in_specs=[VMEM] * 3,
        out_specs=(VMEM,) * 4,
        compiler_params=pltpu.CompilerParams(vmem_limit_bytes=LIMIT),
    )(last, out, gradient)


def shards(n_dp, n_ctx, embedded, upstream, w_uvqk, w_out, lengths):
    cfg = Cfg(n_dp, n_ctx, embedded.shape[1], embedded.shape[2])
    matrix = permutation(cfg.half)
    perm, perm_t = jnp.asarray(matrix, BF), jnp.asarray(matrix.T, BF)
    out, gradient, last = layer(cfg, lengths, embedded, upstream, w_uvqk, w_out, perm, perm_t)
    grad_w, grad_out, out, gradient = finish(cfg, last, out, gradient)
    return out, gradient, grad_w.T, grad_out.T


def solution(mesh):
    return jax.shard_map(
        functools.partial(shards, mesh.shape["dp"], mesh.shape["ctx"]),
        mesh=mesh,
        in_specs=(P("ctx", "dp", None), P("ctx", "dp", None), P(), P(), P()),
        out_specs=(P("ctx", "dp", None), P("ctx", "dp", None), P("ctx", "dp"), P("ctx", "dp")),
        check_vma=False,
    )
```

```python
import functools
import math

import jax
import jax.numpy as jnp
import numpy as np
from jax import lax
from jax.experimental import pallas as pl
from jax.experimental.pallas import tpu as pltpu
from jax.sharding import PartitionSpec as P

HEAD_DIM = 64
BR = 12
SEQ_DP = 2
GROUP = 4
LANES = 128
EPS = 1e-06
BIG = 1e30
MESH = pl.DeviceIdType.MESH
BF = jnp.bfloat16
F32 = jnp.float32
VMEM = pl.BlockSpec(memory_space=pltpu.VMEM)
SMEM = pl.BlockSpec(memory_space=pltpu.SMEM)
HBM = pl.BlockSpec(memory_space=pltpu.HBM)
LIMIT = 62 * 1024 * 1024
PIECES = 3
OUT = (3, 2, 1)
PREPARED = True
TILES = 30
BACK = (3, 1, 2)


class Cfg:
    def __init__(self, n_dp, n_ctx, rows, width):
        self.n_dp = n_dp
        self.n_ctx = n_ctx
        self.rows = rows
        self.width = width
        self.blocks = rows // BR
        self.heads = n_ctx
        self.hd = self.heads * HEAD_DIM
        self.half = n_ctx // 2
        self.piece_z = rows // 2
        self.piece_c = n_ctx * BR // 2
        self.span = n_dp * BR
        self.side = math.isqrt(n_dp // 2)
        self.total = n_ctx * self.span
        self.tile = min(512, self.total // 3)
        self.tab_owner = n_dp
        self.tab_own = n_dp + self.blocks + 1


def permutation(contexts):
    size = contexts * GROUP * BR
    matrix = np.zeros((size, size), np.float32)
    for block in range(GROUP):
        for context in range(contexts):
            for row in range(BR):
                matrix[
                    (block * contexts + context) * BR + row, (context * GROUP + block) * BR + row
                ] = 1.0
    return matrix


def lane(shape):
    return lax.broadcasted_iota(jnp.int32, shape, len(shape) - 1)


def swap(tensor):
    return pltpu.roll(tensor, HEAD_DIM, 1)


def join(left, right):
    return jnp.where(lane(left.shape) < HEAD_DIM, left, right)


def mm(left, right):
    return jnp.dot(left, right, preferred_element_type=F32)


def mm_nt(left, right):
    return lax.dot_general(left, right, (((1,), (1,)), ((), ())), preferred_element_type=F32)


def layer_normalize(tensor):
    centre = jnp.mean(tensor, -1, keepdims=True)
    centred = tensor - centre
    inverse = lax.rsqrt(jnp.mean(centred * centred, -1, keepdims=True) + EPS)
    return centred * inverse, inverse


def layer_norm_backward(incoming, normal, inverse):
    first = jnp.mean(incoming, -1, keepdims=True)
    second = jnp.mean(incoming * normal, -1, keepdims=True)
    return (incoming - first - normal * second) * inverse


def silu(argument):
    return argument * jax.nn.sigmoid(argument)


def silu_grad(argument):
    sigmoid = jax.nn.sigmoid(argument)
    return sigmoid * (1.0 + argument * (1.0 - sigmoid))


def pack_rows(value):
    mid = value.shape[0] // 2
    top, low = value[:mid], value[mid:]
    return join(top, swap(low)), join(swap(top), low)


def unpack_rows(first, second):
    first, second = first.astype(F32), second.astype(F32)
    return jnp.concatenate([join(first, swap(second)), join(swap(first), second)], axis=0)


def greet(cfg, me, ctx):
    barrier = pltpu.get_barrier_semaphore()

    def along_dp(k, carry):
        pl.semaphore_signal(
            barrier, inc=1, device_id={"dp": lax.rem(me + k, cfg.n_dp)}, device_id_type=MESH
        )
        return carry

    def along_ctx(k, carry):
        pl.semaphore_signal(
            barrier, inc=1, device_id={"ctx": lax.rem(ctx + k, cfg.n_ctx)}, device_id_type=MESH
        )
        return carry

    lax.fori_loop(1, cfg.n_dp, along_dp, 0)
    lax.fori_loop(1, cfg.n_ctx, along_ctx, 0)
    return barrier, cfg.n_dp + cfg.n_ctx - 2


class Part:
    def __init__(self, ref, *prefix):
        self.ref, self.prefix = ref, prefix

    def whole(self, index):
        return (*self.prefix, *(index if isinstance(index, tuple) else (index,)))

    def at(self, index):
        return self.ref.at[self.whole(index)]

    def __getitem__(self, index):
        return self.ref[self.whole(index)]

    def __setitem__(self, index, value):
        self.ref[self.whole(index)] = value


class Exchange:
    def __init__(self, axis, count, mine, source, target, send_sem, recv_sem):
        self.axis, self.count, self.mine = axis, count, mine
        self.source, self.target = source, target
        self.send_sem, self.recv_sem = send_sem, recv_sem

    def copy(self, other, slot):
        return pltpu.make_async_remote_copy(
            src_ref=self.source.at(other),
            dst_ref=self.target.at(slot),
            send_sem=self.send_sem.at(other),
            recv_sem=self.recv_sem.at(slot),
            device_id={self.axis: other},
            device_id_type=MESH,
        )

    def each(self, act):
        def step(k, carry):
            act(lax.rem(self.mine + k, self.count))
            return carry

        lax.fori_loop(1, self.count, step, 0)

    def start(self, before=None):
        def act(other):
            if before is not None:
                before(other)
            self.copy(other, self.mine).start()

        self.each(act)

    def wait_recv(self):
        self.each(lambda other: self.copy(other, other).wait_recv())

    def wait_send(self):
        self.each(lambda other: self.copy(other, self.mine).wait_send())


def regroup_in(cfg, g, source, perm, chunks):
    half_blocks = cfg.blocks // 2
    yl, yr = (
        mm(perm[...], jnp.concatenate([source(i) for i in range(lo, lo + cfg.half)], axis=0))
        for lo in (0, cfg.half)
    )
    left = join(yl, swap(yr)).astype(BF)
    right = join(swap(yl), yr).astype(BF)
    for b in range(GROUP):
        rows = slice(b * cfg.piece_c, (b + 1) * cfg.piece_c)
        chunks[GROUP * g + b] = left[rows]
        chunks[half_blocks + GROUP * g + b] = right[rows]


def regroup_out(cfg, g, picked, perm_t, store):
    width = GROUP * BR
    yl, yr = (
        mm(
            perm_t[...],
            jnp.concatenate([picked(lo + GROUP * g + b) for b in range(GROUP)], axis=0),
        )
        for lo in (0, cfg.blocks // 2)
    )
    left = join(yl, swap(yr)).astype(BF)
    right = join(swap(yl), yr).astype(BF)
    for i in range(cfg.half):
        rows = slice(width * i, width * (i + 1))
        store(i, left[rows])
        store(cfg.half + i, right[rows])


def in_pairs(count, act):
    def both(k, carry):
        act(2 * k)
        act(2 * k + 1)
        return carry

    lax.fori_loop(0, count // 2, both, 0)


def group_rows(cfg, context, g):
    return pl.ds(pl.multiple_of(cfg.span * context + GROUP * BR * g, GROUP * BR), GROUP * BR)


def unstream(cfg, own, piece, perm_t, store, extra):
    width = GROUP * BR

    def one(g):
        rows = [piece[lax.rem(own + GROUP * g + b, cfg.n_dp)] for b in range(GROUP)]
        straight = mm(perm_t[...], jnp.concatenate(rows, axis=0))
        turned = swap(straight)
        given = extra(g)
        for i in range(cfg.half):
            cut = slice(width * i, width * (i + 1))
            for c, first, second in ((i, straight, turned), (cfg.half + i, turned, straight)):
                store(group_rows(cfg, c, g), given, first[cut], second[cut])

    in_pairs(cfg.n_dp // GROUP, one)


def to_stream(cfg, source, perm, stream, in_right):
    def one(g):
        xl, xr = (
            jnp.concatenate(
                [source[group_rows(cfg, i, g)] for i in range(lo, lo + cfg.half)], axis=0
            )
            for lo in (0, cfg.half)
        )
        both = join(swap(xl), xr) if in_right else join(xl, swap(xr))
        y = mm(perm[...], both.astype(BF)).astype(BF)
        for b in range(GROUP):
            stream[GROUP * g + b] = y[b * cfg.piece_c : (b + 1) * cfg.piece_c]

    in_pairs(cfg.n_dp // GROUP, one)


def dma(*shape):
    return pltpu.SemaphoreType.DMA(shape)


def params(collective):
    return pltpu.CompilerParams(
        collective_id=collective, has_side_effects=True, vmem_limit_bytes=LIMIT
    )


def table(cfg, me, lengths, tab):
    n = cfg.n_dp
    wrap = n * cfg.blocks * n

    def owner(o, carry):
        start, own, own_first, own_total, owners = carry
        first = lengths[SEQ_DP * o]
        total = first + lengths[SEQ_DP * o + 1]
        block = start + lax.rem(me - start + wrap, n)
        tab[o] = jnp.clip((block - me) // n, 0, cfg.blocks - 1)
        mine = o == me
        own = jnp.where(mine, start, own)
        own_first = jnp.where(mine, first, own_first)
        own_total = jnp.where(mine, total, own_total)
        owners = tuple(
            count + jnp.where(start <= me + n * j, 1, 0) for j, count in enumerate(owners)
        )
        return start + total, own, own_first, own_total, owners

    zero = jnp.int32(0)
    _, own, first, total, owners = lax.fori_loop(
        0, n, owner, (zero, zero, zero, zero, (jnp.int32(-1),) * cfg.blocks)
    )
    for j, count in enumerate(owners):
        tab[cfg.tab_owner + j] = count
    tab[cfg.tab_own] = lax.rem(own, n)
    tab[cfg.tab_own + 1] = first * BR
    tab[cfg.tab_own + 2] = total * BR


def segments(cfg, tab, g):
    shape = (GROUP * BR, LANES)
    inside = lax.broadcasted_iota(jnp.int32, shape, 0) + GROUP * BR * g
    first, total = tab[cfg.tab_own + 1], tab[cfg.tab_own + 2]
    segment = jnp.where(inside < first, 0, jnp.where(inside < total, 1, 2))
    which = lane(shape)
    seg_q = jnp.where(which == segment, -BIG, 0.0)
    seg_k = jnp.where((which < 3) & (which != segment), 1.0, 0.0)
    return seg_q, seg_k


def pack_out_term(cfg, term, t_out):
    side = cfg.side
    for tile in range(cfg.width // LANES):
        straight = term[:, tile * LANES : (tile + 1) * LANES]
        turned = swap(straight)
        for c in range(cfg.n_ctx):
            at = c * HEAD_DIM
            mid, end = at + HEAD_DIM // 2, at + HEAD_DIM
            pieces = (
                join(straight[at:mid], turned[mid:end]),
                join(turned[at:mid], straight[mid:end]),
            )
            for odd, piece in enumerate(pieces):
                s, t = divmod(2 * tile + odd, side)
                place = (0, t, s) if c < cfg.half else (1, (s + t) % side, s)
                t_out[(*place, c % cfg.half)] = piece.astype(BF)


def triangle(cfg, axis):
    shape = (cfg.tile, cfg.tile)
    query = lax.broadcasted_iota(jnp.int32, shape, axis)
    return lax.broadcasted_iota(jnp.int32, shape, 1 - axis) > query


def span_of(cfg, index):
    return slice(index * cfg.tile, (index + 1) * cfg.tile)


def at_tile(cfg, index):
    return pl.ds(pl.multiple_of(index * cfg.tile, cfg.tile), cfg.tile)


def attend(cfg, vk, qs, keys, att):
    each = cfg.total // cfg.tile
    half = each // 2

    def pair(i, j, diagonal):
        it, jt = at_tile(cfg, i), at_tile(cfg, j)
        h = mm_nt(qs[it], keys[jt])
        if diagonal:
            h = jnp.where(triangle(cfg, 0), -BIG, h)
        step = mm((h + h * jnp.tanh(h)).astype(BF), vk[jt])
        att[it] = step if diagonal else att[it] + step

    def diagonal(k, carry):
        for p in range(half):
            pair(half * k + p, half * k + p, True)
        return carry

    def round_of(k, carry):
        for i, j in round_pairs(cfg, k):
            pair(i, j, False)
        return carry

    lax.fori_loop(0, 2, diagonal, 0)
    lax.fori_loop(0, each - 1, round_of, 0)


def weigh_back(cfg, qs, keys, i, j, diagonal):
    h = mm_nt(keys[at_tile(cfg, j)], qs[at_tile(cfg, i)])
    if diagonal:
        h = jnp.where(triangle(cfg, 1), -BIG, h)
    p = 1.0 + jnp.tanh(h)
    a = h * p
    return a.astype(BF), p * ((2.0 * h + 1.0) - a)


def round_pairs(cfg, k):
    last = cfg.total // cfg.tile - 1
    pairs = [(last, k)]
    for d in range(1, (last + 1) // 2):
        one, two = lax.rem(k + d, last), lax.rem(k - d + last, last)
        pairs.append((jnp.maximum(one, two), jnp.minimum(one, two)))
    return pairs


def prepare(cfg, qs, keys, tiles, rounds):
    each = cfg.total // cfg.tile

    def one(k, carry):
        for p, (i, j) in enumerate(round_pairs(cfg, k)):
            weights, slope = weigh_back(cfg, qs, keys, i, j, False)
            tiles[each * k + 2 * p] = weights
            tiles[each * k + 2 * p + 1] = slope.astype(BF)
        return carry

    lax.fori_loop(*rounds, one, 0)


def attend_back(cfg, vk, vkt, qs, keys, go, qz, dvk, dqt, tiles):
    each = cfg.total // cfg.tile
    half = each // 2

    def pair(i, j, weights, slope, first):
        it, jt = at_tile(cfg, i), at_tile(cfg, j)
        grad_s = (mm_nt(vk[jt], go[it]) * slope).astype(BF)
        query = mm(vkt[:, jt], grad_s)
        key = mm(
            jnp.concatenate([weights, grad_s], axis=1),
            jnp.concatenate([go[it], qz[it]], axis=0),
        )
        dqt[:, it] = query if first else dqt[:, it] + query
        dvk[jt] = key if first else dvk[jt] + key

    def diagonal(k, carry):
        for p in range(half):
            i = half * k + p
            pair(i, i, *weigh_back(cfg, qs, keys, i, i, True), True)
        return carry

    def round_of(k, carry):
        for p, (i, j) in enumerate(round_pairs(cfg, k)):
            if PREPARED:
                weights = tiles[each * k + 2 * p]
                slope = tiles[each * k + 2 * p + 1].astype(F32)
            else:
                weights, slope = weigh_back(cfg, qs, keys, i, j, False)
            pair(i, j, weights, slope, False)
        return carry

    lax.fori_loop(0, 2, diagonal, 0)
    lax.fori_loop(0, each - 1, round_of, 0)


def scratch(cfg):
    side, half, block, count = cfg.side, cfg.half, cfg.width // cfg.n_ctx, PIECES
    deep, line, tiles, groups = block + 32, 2 * cfg.side, cfg.hd // LANES, cfg.blocks // 2 // GROUP
    chunk = (cfg.piece_c, LANES)
    zpart = (cfg.piece_z, LANES)
    zhalf = (groups, cfg.n_ctx, cfg.piece_z // groups, LANES)
    stream = (cfg.total, LANES)
    buffers = {
        "xv": ((cfg.rows, cfg.width), BF),
        "upv": ((cfg.rows, cfg.width), BF),
        "wv": ((cfg.width, 4 * cfg.hd), BF),
        "wov": ((cfg.hd, cfg.width), BF),
        "pre": ((cfg.rows, 4 * cfg.hd), F32),
        "normed": ((2, cfg.rows, cfg.width // 2), BF),
        "zsend0": ((count, cfg.n_ctx, *zpart), BF),
        "zland0": ((count, cfg.n_ctx, *zpart), BF),
        "chunks": ((count, cfg.blocks, *chunk), BF),
        "send0": ((count, cfg.n_dp, *chunk), BF),
        "land00": ((cfg.n_dp, *chunk), BF),
        "land01": ((cfg.n_dp, *chunk), BF),
        "land02": ((cfg.n_dp, *chunk), BF),
        "vk": (stream, BF),
        "qs": (stream, BF),
        "keys": (stream, BF),
        "qz": (stream, BF),
        "go": (stream, BF),
        "rows32": (stream, F32),
        "dqt": ((LANES, cfg.total), F32),
        "stream": ((count, cfg.n_dp, *chunk), BF),
        "send1": ((cfg.n_dp, *chunk), BF),
        "land1": ((cfg.n_dp, *chunk), BF),
        "zsend1": (zhalf, BF),
        "zland1": (zhalf, BF),
        "zsend2": (zhalf, BF),
        "zland2": (zhalf, BF),
        "chunks2": ((cfg.blocks, *chunk), BF),
        "send2": ((cfg.n_dp, *chunk), BF),
        "land2": ((cfg.n_dp, *chunk), BF),
        "att_norm": ((cfg.rows, cfg.hd), F32),
        "gpu": ((tiles, cfg.rows, LANES), BF),
        "t_out": ((2, side, side, half, 32, LANES), BF),
        "send3": ((count, cfg.n_dp, *chunk), BF),
        "land30": ((cfg.n_dp, *chunk), BF),
        "land31": ((cfg.n_dp, *chunk), BF),
        "land32": ((cfg.n_dp, *chunk), BF),
        "zsend3": ((count, cfg.n_ctx, *zpart), BF),
        "zland3": ((count, cfg.n_ctx, *zpart), BF),
        "gp": ((cfg.rows, 4 * cfg.hd), BF),
        "gpt": ((count, tiles, cfg.rows, LANES), BF),
        "lrecv": ((line, cfg.rows, cfg.width // 2), BF),
        "grecv": ((side, line, cfg.rows, LANES), BF),
        "trecv": ((line, side, half, 32, LANES), BF),
        "normal_t": ((cfg.width // 2, line * cfg.rows), BF),
        "bsend": ((side, half, block, LANES), BF),
        "brecv": ((side, half, block, LANES), BF),
        "acc": ((half, deep, LANES), F32),
        "tiles": ((TILES, cfg.tile, cfg.tile), BF),
        "vkt": ((LANES, cfg.total), BF),
        "bsend_o": ((side, half, 32, LANES), BF),
        "brecv_o": ((side, half, 32, LANES), BF),
        "fsend": ((half, 2, deep // 2, LANES), BF),
        "frecv": ((cfg.n_ctx, deep // 2, LANES), BF),
    }
    sems = {
        "in": (7,),
        "ls": (6, line - 1),
        "lr": (6, line),
        "bs": (2, side),
        "br": (2, side),
        "fs": (half, 2),
        "fr": (cfg.n_ctx,),
    }
    for name, size, parts in (
        ("z0", cfg.n_ctx, count),
        ("x0", cfg.n_dp, count),
        ("x1", cfg.n_dp, 1),
        ("z1", cfg.n_ctx, groups),
        ("z2", cfg.n_ctx, groups),
        ("x2", cfg.n_dp, 1),
        ("x3", cfg.n_dp, count),
        ("z3", cfg.n_ctx, count),
    ):
        sems[name + "s"] = (parts, size)
        sems[name + "r"] = (parts, size)
    shapes = {name: pltpu.VMEM(*spec) for name, spec in buffers.items()}
    shapes["tab"] = pltpu.SMEM((cfg.tab_own + 3,), jnp.int32)
    shapes.update({name: dma(*size) for name, size in sems.items()})
    return shapes


def layer_kernel(cfg, names, *refs):
    r = dict(zip(names, refs))
    perm, perm_t, tab = r["perm"], r["perm_t"], r["tab"]
    hd, rows, side, half, n, n_ctx = cfg.hd, cfg.rows, cfg.side, cfg.half, cfg.n_dp, cfg.n_ctx
    count, width, groups = PIECES, GROUP * BR, cfg.blocks // 2 // GROUP
    me, ctx = lax.axis_index("dp"), lax.axis_index("ctx")
    core = lax.rem(me, 2)
    other = 1 - core
    chip_x, chip_y = me // (2 * side), lax.rem(me // 2, side)
    a_own = chip_x * other + chip_y * core
    b_own = chip_y * other + chip_x * core
    along_a = 2 * side - core * (2 * side - 2)
    along_b = 2 + core * (2 * side - 2)
    home = ctx // half
    m_own = 2 * a_own + core

    def device(a, b):
        return a * along_a + b * along_b + core

    adder = (chip_y * side + lax.rem(chip_x + chip_y, side)) * 2 + home
    s_own = lax.rem(chip_y - chip_x + side, side)
    owner = (s_own * side + chip_x) * 2

    def load(number, source, target):
        return pltpu.make_async_copy(source, target, r["in"].at[number])

    loads = [load(0, r["x"].at[0], r["xv"])]
    for i, s in enumerate((*OUT, 0)):
        cut = pl.ds(s * hd, hd)
        loads.append(load(1 + i, r["w"].at[:, cut], r["wv"].at[:, cut]))
    loads.append(load(5, r["up"].at[0], r["upv"]))
    loads.append(load(6, r["w_out"], r["wov"]))
    for item in loads:
        item.start()

    barrier, greetings = greet(cfg, me, ctx)
    for z in range(n_ctx):

        @pl.when(jnp.logical_or(z != ctx, adder != me))
        def _():
            pl.semaphore_signal(
                barrier, inc=1, device_id={"dp": adder, "ctx": z}, device_id_type=MESH
            )

    table(cfg, me, r["lengths"], tab)
    own = tab[cfg.tab_own]

    def moves(axis, source, target, sems, parts):
        size, mine = (n, me) if axis == "dp" else (n_ctx, ctx)
        return [
            Exchange(
                axis,
                size,
                mine,
                source(t),
                target(t),
                Part(r[sems + "s"], t),
                Part(r[sems + "r"], t),
            )
            for t in range(parts)
        ]

    def part(name):
        return lambda t: Part(r[name], t)

    z0 = moves("ctx", part("zsend0"), part("zland0"), "z0", count)
    x0 = moves("dp", part("send0"), lambda t: Part(r["land0" + str(t)]), "x0", count)
    x1 = moves("dp", lambda t: Part(r["send1"]), lambda t: Part(r["land1"]), "x1", 1)[0]
    z1 = moves("ctx", part("zsend1"), part("zland1"), "z1", groups)
    z2 = moves("ctx", part("zsend2"), part("zland2"), "z2", groups)
    x2 = moves("dp", lambda t: Part(r["send2"]), lambda t: Part(r["land2"]), "x2", 1)[0]
    x3 = moves("dp", part("send3"), lambda t: Part(r["land3" + str(t)]), "x3", count)
    z3 = moves("ctx", part("zsend3"), part("zland3"), "z3", count)

    xv, upv, wv, wov, pre = r["xv"], r["upv"], r["wv"], r["wov"], r["pre"]
    normed_ref = r["normed"]
    loads[0].wait()
    normal, inverse = layer_normalize(xv[...].astype(F32))
    normed = normal.astype(BF)
    normed_ref[0] = normed[:, : cfg.width // 2]
    normed_ref[1] = normed[:, cfg.width // 2 :]
    zsend0, zland0, chunks, send0 = r["zsend0"], r["zland0"], r["chunks"], r["send0"]
    step = min(256, hd)

    def section(number, t):
        for base in range(0, hd, step):
            at = number * hd + base
            value = mm(normed, wv[:, at : at + step])
            pre[:, at : at + step] = value
            if t is None:
                continue
            act = silu(value)
            for tile in range(step // LANES):
                head = (base + tile * LANES) // HEAD_DIM
                one, two = pack_rows(act[:, tile * LANES : (tile + 1) * LANES])
                zsend0[t, head] = one.astype(BF)
                zsend0[t, head + 1] = two.astype(BF)

    for t, number in enumerate(OUT):
        loads[1 + t].wait()
        section(number, t)
        if t == 0:
            pl.semaphore_wait(
                barrier, greetings + n_ctx - jnp.where(adder == me, 1, 0).astype(jnp.int32)
            )
        z0[t].start()
        zland0[t, ctx] = zsend0[t, ctx]
    loads[4].wait()
    section(0, None)
    loads[5].wait()
    loads[6].wait()
    back_gated = mm_nt(upv[...], wov[...])
    gate = silu(pre[:, :hd]).astype(BF).astype(F32)
    for t in range(count):
        z0[t].wait_recv()
        for g in range(groups):
            cut = slice(width * g, width * (g + 1))
            regroup_in(
                cfg, g, lambda i, t=t, cut=cut: zland0[t, i, cut], perm, Part(chunks, t)
            )

        def fill(device_at, t=t):
            send0[t, device_at] = chunks[t, tab[device_at]]

        x0[t].start(fill)
        r["land0" + str(t)][me] = chunks[t, tab[me]]

    vk, qs, keys, qz, go = r["vk"], r["qs"], r["keys"], r["qz"], r["go"]

    def store_k(cut, masks, straight, turned):
        keys[cut] = join(masks[1], turned).astype(BF)

    def store_v(cut, masks, straight, turned):
        vk[cut] = join(straight.astype(BF), keys[cut])

    def store_q(cut, masks, straight, turned):
        value = turned * (0.5 * HEAD_DIM**-0.5)
        qs[cut] = join(masks[0], value).astype(BF)
        qz[cut] = join(jnp.zeros_like(value), value).astype(BF)

    tiles = r["tiles"]
    for t, store in enumerate((store_k, store_q, store_v)):
        x0[t].wait_recv()
        unstream(
            cfg, own, r["land0" + str(t)], perm_t, store, lambda g: segments(cfg, tab, g)
        )

    gpu, t_out, gpt = r["gpu"], r["t_out"], r["gpt"]
    lrecv, grecv, trecv = r["lrecv"], r["grecv"], r["trecv"]
    def tile_of(a, kind, s):
        return lax.rem(a - s * kind + side, side)

    def line_copy(what, j):
        if j < side - 1:
            kind, a = 0, lax.rem(chip_x + 1 + j, side)
            target, slot = (a * side + chip_y) * 2, 2 * chip_x + core
        elif j < 2 * (side - 1):
            kind, a = 1, lax.rem(chip_y + 1 + j - (side - 1), side)
            target, slot = (chip_x * side + a) * 2 + 1, 2 * chip_y + core
        else:
            kind, a = other, b_own
            target, slot = me + 1 - 2 * core, 2 * b_own + core
        if what == 4:
            source, target_ref = normed_ref.at[kind], lrecv.at[slot]
        elif what == 5:
            source, target_ref = t_out.at[kind, a], trecv.at[slot]
        elif what == 0:
            source, target_ref = gpu.at[tile_of(a, kind, 0)], grecv.at[0, slot]
        else:
            source, target_ref = gpt.at[what - 1, tile_of(a, kind, what)], grecv.at[what, slot]
        return pltpu.make_async_remote_copy(
            src_ref=source,
            dst_ref=target_ref,
            send_sem=r["ls"].at[what, j],
            recv_sem=r["lr"].at[what, slot],
            device_id={"dp": target},
            device_id_type=MESH,
        )

    def line_start(what):
        for j in range(2 * side - 1):
            line_copy(what, j).start()

    def line_wait(what):
        ref = {4: lrecv, 5: trecv}.get(what, None)
        for i in range(1, 2 * side):
            slot = lax.rem(m_own + i, 2 * side)
            place = grecv.at[what, slot] if ref is None else ref.at[slot]
            pltpu.make_async_remote_copy(
                src_ref=place,
                dst_ref=place,
                send_sem=r["ls"].at[what, 0],
                recv_sem=r["lr"].at[what, slot],
                device_id={"dp": me + 1 - 2 * core},
                device_id_type=MESH,
            ).wait_recv()


    line_start(4)
    rows32 = r["rows32"]
    attend(cfg, vk, qs, keys, rows32)

    stream, send1, land1 = r["stream"], r["send1"], r["land1"]
    to_stream(cfg, rows32, perm, Part(stream, 0), False)

    def place(t, device_at):
        return stream[t, lax.rem(device_at - own + n, n)]

    def fill1(device_at):
        send1[device_at] = place(0, device_at)

    x1.start(fill1)
    land1[me] = place(0, me)
    backward_gate = back_gated * gate
    lrecv[m_own] = normed_ref[core]
    line_wait(4)
    normal_t = r["normal_t"]
    for i in range(side):
        pair = jnp.concatenate([lrecv[2 * i], lrecv[2 * i + 1]], axis=0)
        normal_t[:, 2 * rows * i : 2 * rows * (i + 1)] = pair.T

    prepare(cfg, qs, keys, tiles, (0, 3))
    vkt = r["vkt"]
    for i in range(cfg.total // cfg.tile):
        vkt[:, span_of(cfg, i)] = vk[span_of(cfg, i)].T
    x1.wait_recv()
    zsend1, zland1, zsend2, zland2 = r["zsend1"], r["zland1"], r["zsend2"], r["zland2"]
    for g in range(groups):

        def store1(i, value, g=g):
            zsend1[g, i] = value

        regroup_out(cfg, g, lambda block: land1[tab[cfg.tab_owner + block]], perm_t, store1)
        z1[g].start()
        zland1[g, ctx] = zsend1[g, ctx]
    att_norm = r["att_norm"]
    mid = rows // 2
    for g in range(groups):
        z1[g].wait_recv()
        att_rows = jnp.concatenate(
            [
                unpack_rows(zland1[g, head], zland1[g, head + 1])
                for head in range(0, cfg.heads, 2)
            ],
            axis=1,
        )
        norm_part, att_inverse = layer_normalize(att_rows)
        top, low = slice(width * g, width * (g + 1)), slice(mid + width * g, mid + width * (g + 1))
        att_norm[top] = norm_part[:width]
        att_norm[low] = norm_part[width:]
        incoming = jnp.concatenate([backward_gate[top], backward_gate[low]], axis=0)
        grad_att = layer_norm_backward(incoming, norm_part, att_inverse)
        for tile in range(hd // LANES):
            one, two = pack_rows(grad_att[:, tile * LANES : (tile + 1) * LANES])
            zsend2[g, 2 * tile] = one.astype(BF)
            zsend2[g, 2 * tile + 1] = two.astype(BF)
        z2[g].start()
        zland2[g, ctx] = zsend2[g, ctx]

    gated = (att_norm[...] * gate).astype(BF)
    r["out"][0] = (xv[...].astype(F32) + mm(gated, wov[...])).astype(BF)
    chunks2, send2, land2 = r["chunks2"], r["send2"], r["land2"]
    for g in range(groups):
        z2[g].wait_recv()
        regroup_in(cfg, g, lambda i, g=g: zland2[g, i], perm, chunks2)

    def fill2(device_at):
        send2[device_at] = chunks2[tab[device_at]]

    x2.start(fill2)
    land2[me] = chunks2[tab[me]]
    gp = r["gp"]
    grad_u = (back_gated * att_norm[...] * silu_grad(pre[:, :hd])).astype(BF)
    gp[:, :hd] = grad_u
    for tile in range(hd // LANES):
        gpu[tile] = grad_u[:, tile * LANES : (tile + 1) * LANES]
    pack_out_term(
        cfg,
        lax.dot_general(gated, upv[...], (((0,), (0,)), ((), ())), preferred_element_type=F32),
        t_out,
    )
    prepare(cfg, qs, keys, tiles, (3, 5))
    x2.wait_recv()

    def store_go(cut, masks, straight, turned):
        go[cut] = join(straight, jnp.zeros_like(straight)).astype(BF)

    line_start(0)
    line_start(5)
    unstream(cfg, own, land2, perm_t, store_go, lambda g: None)
    dqt = r["dqt"]
    attend_back(cfg, vk, vkt, qs, keys, go, qz, rows32, dqt, tiles)

    send3, zsend3, zland3 = r["send3"], r["zsend3"], r["zland3"]
    for t in range(count):
        if t == 2:
            for i in range(cfg.total // cfg.tile):
                cut = slice(cfg.tile * i, cfg.tile * (i + 1))
                rows32[cut] = dqt[:, cut].T * (0.5 * HEAD_DIM**-0.5)
        to_stream(cfg, rows32, perm, Part(stream, t), t != 1)

        def fill3(device_at, t=t):
            send3[t, device_at] = place(t, device_at)

        x3[t].start(fill3)
        r["land3" + str(t)][me] = place(t, me)

    send_b, recv_b, acc = r["bsend"], r["brecv"], r["acc"]
    block = cfg.width // n_ctx
    grecv[0, m_own] = gpu[tile_of(a_own, core, 0)]
    trecv[m_own] = t_out[core, a_own]
    line_wait(0)
    line_wait(5)

    def add_copy(part, s):
        b = lax.rem(a_own + s * (1 - 2 * core) + side, side)
        slot = lax.rem(b_own - b + 2 * side - 1, side)
        source, target = ((send_b, recv_b), (r["bsend_o"], r["brecv_o"]))[part]
        return b == b_own, pltpu.make_async_remote_copy(
            src_ref=source.at[s],
            dst_ref=target.at[slot],
            send_sem=r["bs"].at[part, s],
            recv_sem=r["br"].at[part, slot],
            device_id={"dp": device(a_own, b)},
            device_id_type=MESH,
        )

    def add_part(part, s, value):
        mine, copy = add_copy(part, s)

        @pl.when(mine)
        def _():
            if part == 0:
                acc[:, :block] = value
            else:
                acc[:, block:] = value

        @pl.when(jnp.logical_not(mine))
        def _():
            if part == 0:
                send_b[s] = value.astype(BF)
            else:
                r["bsend_o"][s] = value.astype(BF)
            copy.start()

    def add_section(s):
        value = mm(normal_t[...], grecv[s].reshape(2 * side * rows, LANES))
        add_part(0, s, value.reshape(half, block, LANES))

    for s in range(side):
        low = trecv[0, s].astype(F32)
        for m in range(1, 2 * side):
            low = low + trecv[m, s].astype(F32)
        add_part(1, s, low)
    add_section(0)
    for t in range(count):
        x3[t].wait_recv()
        land = r["land3" + str(t)]
        for g in range(groups):

            def store3(i, value, t=t, g=g):
                zsend3[t, i, width * g : width * (g + 1)] = value

            regroup_out(
                cfg, g, lambda b, land=land: land[tab[cfg.tab_owner + b]], perm_t, store3
            )
        z3[t].start()
        zland3[t, ctx] = zsend3[t, ctx]

    def give_section(t):
        s = BACK[t]
        z3[t].wait_recv()
        for head in range(0, cfg.heads, 2):
            tile = head // 2
            at = s * hd + tile * LANES
            cut = slice(at, at + LANES)
            value = unpack_rows(zland3[t, head], zland3[t, head + 1])
            value = (value * silu_grad(pre[:, cut])).astype(BF)
            gp[:, cut] = value
            gpt[s - 1, tile] = value
        line_start(s)
        grecv[s, m_own] = gpt[s - 1, tile_of(a_own, core, s)]

    back = mm_nt(gp[:, :hd], wv[:, :hd])
    give_section(0)
    back = back + mm_nt(gp[:, 3 * hd :], wv[:, 3 * hd :])
    give_section(1)
    line_wait(BACK[0])
    add_section(BACK[0])
    give_section(2)
    line_wait(BACK[1])
    add_section(BACK[1])
    back = back + mm_nt(gp[:, hd : 2 * hd], wv[:, hd : 2 * hd])

    back = back + mm_nt(gp[:, 2 * hd : 3 * hd], wv[:, 2 * hd : 3 * hd])
    r["gradient"][0] = (
        upv[...].astype(F32) + layer_norm_backward(back, normal, inverse)
    ).astype(BF)
    line_wait(BACK[2])
    add_section(BACK[2])

    total = acc[...]
    for slot in range(side - 1):
        for part, target in enumerate((recv_b, r["brecv_o"])):
            pltpu.make_async_remote_copy(
                src_ref=target.at[slot],
                dst_ref=target.at[slot],
                send_sem=r["bs"].at[part, 0],
                recv_sem=r["br"].at[part, slot],
                device_id={"dp": me + 1 - 2 * core},
                device_id_type=MESH,
            ).wait_recv()
        arrived = jnp.concatenate([recv_b[slot], r["brecv_o"][slot]], axis=1)
        total = total + arrived.astype(F32)

    fsend, frecv = r["fsend"], r["frecv"]
    quarter = lax.rem(lane((16, LANES)), HEAD_DIM) < 32
    for h in range(half):
        top, low = total[h, : block // 2], total[h, block // 2 : block]
        u, v = total[h, block : block + 16], total[h, block + 16 :]
        fsend[h, 0, : block // 2] = join(top, swap(low)).astype(BF)
        fsend[h, 1, : block // 2] = join(swap(top), low).astype(BF)
        fsend[h, 0, block // 2 :] = jnp.where(quarter, u, pltpu.roll(v, 32, 1)).astype(BF)
        fsend[h, 1, block // 2 :] = jnp.where(quarter, pltpu.roll(u, 96, 1), v).astype(BF)

    def last_copy(h, kind):
        return pltpu.make_async_remote_copy(
            src_ref=fsend.at[h, kind],
            dst_ref=frecv.at[ctx],
            send_sem=r["fs"].at[h, kind],
            recv_sem=r["fr"].at[ctx],
            device_id={"dp": owner + kind, "ctx": half * core + h},
            device_id_type=MESH,
        )

    def stays(h, kind):
        return jnp.logical_and(half * core + h == ctx, owner + kind == me)

    for h in range(half):
        for kind in range(2):

            @pl.when(stays(h, kind))
            def _():
                frecv[ctx] = fsend[h, kind]

            @pl.when(jnp.logical_not(stays(h, kind)))
            def _():
                last_copy(h, kind).start()

    for z in range(n_ctx):

        @pl.when(jnp.logical_or(z != ctx, adder != me))
        def _():
            pltpu.make_async_remote_copy(
                src_ref=fsend.at[0, 0],
                dst_ref=frecv.at[z],
                send_sem=r["fs"].at[0, 0],
                recv_sem=r["fr"].at[z],
                device_id={"dp": me + 1 - 2 * core},
                device_id_type=MESH,
            ).wait_recv()

    total = frecv[0].astype(F32)
    for z in range(1, n_ctx):
        total = total + frecv[z].astype(F32)
    r["last"][...] = total * (rows * n * n_ctx) ** -0.5

    for move in (*z0, *x0, x1, *z1, *z2, x2, *x3, *z3):
        move.wait_send()
    for what in range(6):
        for j in range(2 * side - 1):
            line_copy(what, j).wait_send()
    for part in range(2):
        for s in range(side):
            mine, copy = add_copy(part, s)

            @pl.when(jnp.logical_not(mine))
            def _():
                copy.wait_send()

    for h in range(half):
        for kind in range(2):

            @pl.when(jnp.logical_not(stays(h, kind)))
            def _():
                last_copy(h, kind).wait_send()


def layer(cfg, lengths, x, up, w, w_out, perm, perm_t):
    block = cfg.width // cfg.n_ctx
    inputs = {
        "lengths": SMEM,
        "x": HBM,
        "up": HBM,
        "w": HBM,
        "w_out": HBM,
        "perm": VMEM,
        "perm_t": VMEM,
    }
    outputs = {
        "out": jax.ShapeDtypeStruct(x.shape, BF),
        "gradient": jax.ShapeDtypeStruct(x.shape, BF),
        "last": jax.ShapeDtypeStruct((block // 2 + 16, LANES), F32),
    }
    shapes = scratch(cfg)
    return pl.pallas_call(
        functools.partial(layer_kernel, cfg, [*inputs, *outputs, *shapes]),
        name="layer",
        out_shape=tuple(outputs.values()),
        in_specs=list(inputs.values()),
        out_specs=(VMEM,) * len(outputs),
        scratch_shapes=list(shapes.values()),
        compiler_params=params(0),
    )(lengths, x, up, w, w_out, perm, perm_t)


def finish_kernel(half_block, last, out, gradient, gw, go, out_copy, gradient_copy):
    front, low = last[:half_block].T, last[half_block:].T
    gw[...] = jnp.concatenate([front[:HEAD_DIM], front[HEAD_DIM:]], axis=1)
    go[...] = jnp.concatenate([low[32 * i : 32 * (i + 1)] for i in range(4)], axis=1)
    out_copy[...] = out[...]
    gradient_copy[...] = gradient[...]


def finish(cfg, last, out, gradient):
    block = cfg.width // cfg.n_ctx
    return pl.pallas_call(
        functools.partial(finish_kernel, block // 2),
        name="finish",
        out_shape=(
            jax.ShapeDtypeStruct((HEAD_DIM, block), F32),
            jax.ShapeDtypeStruct((32, HEAD_DIM), F32),
            jax.ShapeDtypeStruct(out.shape, BF),
            jax.ShapeDtypeStruct(out.shape, BF),
        ),
        in_specs=[VMEM] * 3,
        out_specs=(VMEM,) * 4,
        compiler_params=pltpu.CompilerParams(vmem_limit_bytes=LIMIT),
    )(last, out, gradient)


def shards(n_dp, n_ctx, embedded, upstream, w_uvqk, w_out, lengths):
    cfg = Cfg(n_dp, n_ctx, embedded.shape[1], embedded.shape[2])
    matrix = permutation(cfg.half)
    perm, perm_t = jnp.asarray(matrix, BF), jnp.asarray(matrix.T, BF)
    out, gradient, last = layer(cfg, lengths, embedded, upstream, w_uvqk, w_out, perm, perm_t)
    grad_w, grad_out, out, gradient = finish(cfg, last, out, gradient)
    return out, gradient, grad_w.T, grad_out.T


def solution(mesh):
    return jax.shard_map(
        functools.partial(shards, mesh.shape["dp"], mesh.shape["ctx"]),
        mesh=mesh,
        in_specs=(P("ctx", "dp", None), P("ctx", "dp", None), P(), P(), P()),
        out_specs=(P("ctx", "dp", None), P("ctx", "dp", None), P("ctx", "dp"), P("ctx", "dp")),
        check_vma=False,
    )
```
